32 devices in a mesh: dp: 4 (over y, x), row: 2 (over core), col: 4 (over z).
Axes of the slice: x: 2, y: 2, z: 4, core: 2. Of those that a mesh axis runs over, the one named last changes fastest.
Arguments:
- inputs: bfloat16 [16384, 2048], P(('dp', 'col'), 'row'), may hold values from -6 to 6
- cotangent: bfloat16 [16384, 2048], P(('dp', 'col'), 'row'), may hold values from -6 to 6
- w_qkv: float32 [16, 128, 3, 16, 128], P('row', 'dp', None, 'col'), may hold values from -0.125 to 0.125
- w_out: float32 [16, 128, 2048], P('col', 'dp', 'row'), may hold values from -0.125 to 0.125
- w_gate_up: float32 [16, 128, 2, 8192], P('row', 'dp', None, 'col'), may hold values from -0.125 to 0.125
- w_down: float32 [64, 128, 2048], P('col', 'dp', 'row'), may hold values from -0.0625 to 0.0625
- gains: float32 [4, 2048], replicated, may hold values from 0.3 to 2.4, as said below
- gain_state: float32 [4, 2048], replicated, may hold values from 16384 to 98304, as said below
- row_state: float32 [14336], replicated, may hold values from 4915.2 to 98304, as said below
- col_state: float32 [26624], replicated, may hold values from 4915.2 to 98304, as said below
- positions: int32 [16, 1024], P(('dp', 'row')), may hold values from 0 to 1023, as said below
- block_map: int32 [16, 4], P(('dp', 'row')), may hold values from 0 to 3, as said below
Outputs:
- output: float32 [16384, 2048], P(('dp', 'col'), 'row')
- grad_inputs: float32 [16384, 2048], P(('dp', 'col'), 'row')
- grad_qkv: float32 [16, 128, 3, 16, 128], P('row', 'dp', None, 'col')
- grad_out: float32 [16, 128, 2048], P('col', 'dp', 'row')
- grad_gate_up: float32 [16, 128, 2, 8192], P('row', 'dp', None, 'col')
- grad_down: float32 [64, 128, 2048], P('col', 'dp', 'row')
- new_qkv: float32 [16, 128, 3, 16, 128], P('row', 'dp', None, 'col')
- new_out: float32 [16, 128, 2048], P('col', 'dp', 'row')
- new_gate_up: float32 [16, 128, 2, 8192], P('row', 'dp', None, 'col')
- new_down: float32 [64, 128, 2048], P('col', 'dp', 'row')
- copy_qkv: bfloat16 [16, 128, 3, 16, 128], P('row', 'dp', None, 'col')
- copy_out: bfloat16 [16, 128, 2048], P('col', 'dp', 'row')
- copy_gate_up: bfloat16 [16, 128, 2, 8192], P('row', 'dp', None, 'col')
- copy_down: bfloat16 [64, 128, 2048], P('col', 'dp', 'row')
- new_row_state: float32 [14336], replicated
- new_col_state: float32 [26624], replicated
- gain_grad: float32 [4, 2048], replicated
- new_gain_state: float32 [4, 2048], replicated
- new_gains: float32 [4, 2048], replicated
The draws below stay inside these ranges and needn't reach their ends.
Inputs may be any that keep to these rules, and one draw needn't show every extreme that they name: Within a sequence positions count up by one from 0 and restart at 0 where a new document begins; every sequence begins with 0. `block_map`: entry b of a sequence's row is at most b. `gains`: Positive. `gain_state`: Positive. `row_state`: Positive. `col_state`: Positive.
All inputs are finite; a program needn't handle non-finite values.
Results may differ from the reference program's by a relative error of at most 0.019.
The reference program's roundings to bfloat16 on the way count: a program that leaves them out, or rounds other values in their place, can miss the bound.
Values may be sent and summed in bfloat16 or wider, within the bound.
No kernel may reach another device: no remote copies, remote signals or barrier semaphores. Data moves between devices by JAX's collectives and lax.ppermute only.
A program may use at most 384 MiB of HBM per device.

```python
import math
import jax
import jax.numpy as jnp
from jax import lax

D = 2048
H = 16
HD = 128
FF = 8192
LEN = 1024
STEP = 3
SEQG = 4
NB = 4
SEQS = 16
TOKENS = 16384


def state_ratio():
    return STEP ** (-0.8) / (1.0 - STEP ** (-0.8))


def draw_gains(key, part):
    key = jax.random.fold_in(key, 3)
    places = jnp.arange(D, dtype=jnp.float32) / (D - 1)
    rising = 0.6 * jnp.exp(math.log(3.0) * places)
    spread = jax.random.uniform(key, (4, D), jnp.float32, 0.85, 1.15)
    return rising[None, :] * spread


def draw_gain_state(key, part):
    key = jax.random.fold_in(key, 5)
    factor = jnp.exp(jax.random.uniform(key, (4, D), jnp.float32, 0.0, math.log(4.0)))
    return TOKENS * 2.0 * state_ratio() * factor


def draw_row_state(key, part):
    key = jax.random.fold_in(key, 7)
    pieces = []
    for number, (row_count, weight) in enumerate(((D, 1.0), (D, 2.0), (D, 0.8), (FF, 1.2))):
        places = jnp.arange(row_count, dtype=jnp.float32)
        falloff = jnp.exp(-0.5 * math.log(3.0) * (places % HD / HD + places / row_count))
        factor = jnp.exp(jax.random.uniform(jax.random.fold_in(key, number), (row_count,), jnp.float32, 0.0, math.log(2.0)))
        pieces.append(TOKENS * weight * 2.0 * state_ratio() * falloff * factor)
    return jnp.concatenate(pieces)


def draw_col_state(key, part):
    key = jax.random.fold_in(key, 9)
    pieces = []
    for number, (col_count, period, weight) in enumerate(((3 * D, D, 1.0), (D, D, 2.0), (2 * FF, FF, 0.8), (D, D, 1.2))):
        places = jnp.arange(col_count, dtype=jnp.float32)
        falloff = jnp.exp(-math.log(3.0) * (places % period) / period)
        factor = jnp.exp(jax.random.uniform(jax.random.fold_in(key, number), (col_count,), jnp.float32, 0.0, math.log(2.0)))
        pieces.append(TOKENS * weight * 2.0 * state_ratio() * falloff * factor)
    return jnp.concatenate(pieces)


def draw_positions(key, part):
    key = jax.random.fold_in(key, 11)
    places = jnp.arange(LEN, dtype=jnp.int32)
    fresh = jax.random.randint(key, (SEQS, LEN), 0, max(LEN // 3, 2)) == 0
    fresh = fresh & (jnp.arange(SEQS, dtype=jnp.int32)[:, None] > 0)
    fresh = fresh | (places[None, :] == 0)
    latest = lax.cummax(jnp.where(fresh, places[None, :], 0), axis=1)
    return (places[None, :] - latest).astype(jnp.int32)


def draw_block_map(key, part):
    key = jax.random.fold_in(key, 13)
    limits = jnp.arange(NB, dtype=jnp.int32) + 1
    drawn = jax.random.randint(key, (SEQS, NB), 0, limits[None, :])
    corner = (jnp.arange(SEQS, dtype=jnp.int32)[:, None] == 0) & (jnp.arange(NB, dtype=jnp.int32)[None, :] == NB - 1)
    return jnp.where(corner, NB - 1, drawn).astype(jnp.int32)


def levels(key, shape, shards, low, top_value):
    def one(dim, parts):
        steps = jax.random.uniform(jax.random.fold_in(jax.random.fold_in(key, 6), dim), (parts,), jnp.float32, low / len(shards), top_value / len(shards))
        return jnp.repeat(jnp.exp(steps), shape[dim] // parts).reshape((-1,) + (1,) * (len(shape) - dim - 1))

    factor_of = one(*shards[0])
    for cut in shards[1:]:
        factor_of = factor_of * one(*cut)
    return factor_of


def centred(key, extent, scale, limit, shards=(), kind=jnp.bfloat16):
    factor_of = levels(key, extent, shards, -0.22, 0.18) if shards else 1.0
    array = jax.random.normal(key, extent, jnp.float32) * scale * factor_of
    return jnp.minimum(jnp.maximum(array, -limit), limit).astype(kind)


def setup_inputs(seed: int = 0) -> dict:
    streams_of = jax.random.split(jax.random.key(seed), 13)
    inputs = centred(streams_of[0], (TOKENS, D), 1.0, 6.0, ((0, 16), (1, 2)))
    cotangent = centred(streams_of[1], (TOKENS, D), 1.0, 6.0, ((0, 16), (1, 2)))
    w_qkv = centred(streams_of[2], (D // HD, HD, 3, H, HD), D ** -0.5, 0.125, ((0, 2), (1, 4), (3, 4)), jnp.float32)
    w_out = centred(streams_of[3], (H, HD, D), D ** -0.5, 0.125, ((0, 4), (1, 4), (2, 2)), jnp.float32)
    w_gate_up = centred(streams_of[4], (D // HD, HD, 2, FF), D ** -0.5, 0.125, ((0, 2), (1, 4), (3, 4)), jnp.float32)
    w_down = centred(streams_of[5], (FF // HD, HD, D), FF ** -0.5, 0.0625, ((0, 4), (1, 4), (2, 2)), jnp.float32)
    gains = draw_gains(jax.random.fold_in(streams_of[12], 71), 0)
    gain_state = draw_gain_state(jax.random.fold_in(streams_of[12], 71), 0)
    row_state = draw_row_state(jax.random.fold_in(streams_of[12], 71), 0)
    col_state = draw_col_state(jax.random.fold_in(streams_of[12], 71), 0)
    positions = draw_positions(jax.random.fold_in(streams_of[12], 71), 0)
    block_map = draw_block_map(jax.random.fold_in(streams_of[12], 71), 0)
    return {"inputs": inputs, "cotangent": cotangent, "w_qkv": w_qkv, "w_out": w_out, "w_gate_up": w_gate_up, "w_down": w_down, "gains": gains, "gain_state": gain_state, "row_state": row_state, "col_state": col_state, "positions": positions, "block_map": block_map}


EPSILON = 1e-06
TINY_SQUARE = 1e-30
ROPE_BASE = 500000.0
NEGATIVE = -1e+30
CLIP_LEVEL = 0.5
GAIN_RATE = 0.3

@jax.custom_vjp
def low(v):
    return lax.optimization_barrier(v.astype(jnp.bfloat16)).astype(jnp.float32)

@jax.custom_vjp
def low_back(v):
    return v

def low_keep(v):
    return (low(v), None)

def low_pass(kept, grad):
    return (grad,)

def back_keep(v):
    return (v, None)

def back_low(kept, grad):
    return (low(grad),)
low.defvjp(low_keep, low_pass)
low_back.defvjp(back_keep, back_low)

def matmul(left_side, right_side):
    return jnp.dot(left_side, right_side, precision=lax.Precision.HIGHEST, preferred_element_type=jnp.float32)

def rms_norm(values, gain_row):
    return values * lax.rsqrt(lax.optimization_barrier(jnp.mean(values * values, axis=-1, keepdims=True)) + EPSILON) * gain_row

def angles(places):
    halfway = HD // 2
    frequency = ROPE_BASE ** (-jnp.arange(halfway, dtype=jnp.float32) / halfway)
    turned = places.astype(jnp.float32)[:, None] * frequency[None, :]
    return (jnp.cos(turned)[:, None, :], jnp.sin(turned)[:, None, :])

def rotate(values, cosine, sine_term):
    halfway = values.shape[-1] // 2
    leading = values[..., :halfway]
    second = values[..., halfway:]
    return jnp.concatenate([leading * cosine - second * sine_term, second * cosine + leading * sine_term], axis=-1)

def allowed_pairs(position, starts):
    length = position.shape[0]
    nblock = starts.shape[0]
    places = jnp.arange(length, dtype=jnp.int32)
    blocks = places // (length // nblock)
    documents = jnp.cumsum((position == 0).astype(jnp.int32))
    earliest = lax.optimization_barrier(jnp.sum(jnp.where(blocks[:, None] == jnp.arange(nblock, dtype=jnp.int32)[None, :], starts[None, :], 0), axis=1))
    same_doc = documents[:, None] == documents[None, :]
    return same_doc & (blocks[None, :] >= earliest[:, None]) & (blocks[None, :] <= blocks[:, None])

def attend_one(pieces):
    queries, keys_in, values, position, starts = pieces
    allowed = allowed_pairs(position, starts)
    scaling = queries.shape[-1] ** (-0.5)
    scores = low_back(jnp.einsum('qhd,khd->hqk', queries, keys_in, precision=lax.Precision.HIGHEST) * scaling)
    scores = jnp.where(allowed[None], scores, NEGATIVE)
    highest = lax.optimization_barrier(jnp.max(scores, axis=-1, keepdims=True))
    exponent = jnp.exp(scores - highest)
    probability = low(exponent / lax.optimization_barrier(jnp.sum(exponent, axis=-1, keepdims=True)))
    return jnp.einsum('hqk,khd->qhd', probability, values, precision=lax.Precision.HIGHEST)

def block_layer(acts, matrix_qkv, matrix_out, matrix_gu, matrix_down, gain_rows, places, starts):
    count = acts.shape[0]
    nseq = places.shape[0]
    qkv = low_back(matmul(acts, low(matrix_qkv)))
    query_norm = rms_norm(qkv[:, :D], gain_rows[0])
    key_norm = rms_norm(qkv[:, D:2 * D], gain_rows[1])
    cosine, sine_term = angles(places.reshape(-1))
    query_rot = low(rotate(query_norm.reshape(count, H, HD), cosine, sine_term))
    key_rot = low(rotate(key_norm.reshape(count, H, HD), cosine, sine_term))
    value_low = low(qkv[:, 2 * D:].reshape(count, H, HD))
    mixed = lax.map(jax.checkpoint(attend_one), (query_rot.reshape(nseq, LEN, H, HD), key_rot.reshape(nseq, LEN, H, HD), value_low.reshape(nseq, LEN, H, HD), places, starts))
    mixed = low(low_back(mixed.reshape(count, D)))
    attn = low_back(matmul(mixed, low(matrix_out)))
    hidden_in = acts + rms_norm(attn, gain_rows[2])
    gate_up = low_back(matmul(low(hidden_in), low(matrix_gu)))
    hidden = low(jax.nn.silu(gate_up[:, :FF]) * gate_up[:, FF:])
    mlp = low_back(matmul(hidden, low(matrix_down)))
    return hidden_in + rms_norm(mlp, gain_rows[3])

def factored(grad_mat, weight_mat, row_old, col_old, rate, decay):
    square = grad_mat * grad_mat + TINY_SQUARE
    row_new = decay * row_old + (1.0 - decay) * lax.optimization_barrier(jnp.mean(square, axis=1))
    col_new = decay * col_old + (1.0 - decay) * lax.optimization_barrier(jnp.mean(square, axis=0))
    estimate = row_new[:, None] * col_new[None, :] / jnp.mean(row_new)
    update = grad_mat * lax.rsqrt(estimate)
    update = update / jnp.maximum(1.0, jnp.sqrt(jnp.mean(update * update)) / CLIP_LEVEL)
    return (weight_mat - rate * update, row_new, col_new)

def reference(inputs, cotangent, w_qkv, w_out, w_gate_up, w_down, gains, gain_state, row_state, col_state, positions, block_map):
    matrices = (w_qkv.reshape(D, 3 * D), w_out.reshape(D, D), w_gate_up.reshape(D, 2 * FF), w_down.reshape(FF, D))
    groups = SEQS // SEQG
    acts_all = inputs.astype(jnp.float32).reshape(groups, SEQG * LEN, D)
    back_all = cotangent.astype(jnp.float32).reshape(groups, SEQG * LEN, D)
    places_all = positions.reshape(groups, SEQG, LEN)
    starts_all = block_map.reshape(groups, SEQG, NB)

    def one_group(carry, pieces):
        group_in, group_back, group_places, group_starts = pieces

        def forward(acts, matrix_qkv, matrix_out, matrix_gu, matrix_down, gain_rows):
            return block_layer(acts, matrix_qkv, matrix_out, matrix_gu, matrix_down, gain_rows, group_places, group_starts)
        result, pullback = jax.vjp(forward, group_in, matrices[0], matrices[1], matrices[2], matrices[3], gains)
        grads = pullback(group_back)
        carry = tuple((total + piece for total, piece in zip(carry, grads[1:])))
        return (carry, (result, grads[0]))
    initial = tuple((jnp.zeros_like(item) for item in matrices)) + (jnp.zeros_like(gains),)
    sums, (outputs, grad_acts) = lax.scan(one_group, initial, (acts_all, back_all, places_all, starts_all))
    grad_qkv, grad_out, grad_gu, grad_down, gain_grad = sums
    decay = 1.0 - STEP ** (-0.8)
    rows_at = [0, D, 2 * D, 3 * D, 3 * D + FF]
    cols_at = [0, 3 * D, 4 * D, 4 * D + 2 * FF, 5 * D + 2 * FF]
    rates = [3.0 * D ** (-0.5), 3.0 * D ** (-0.5), 3.0 * D ** (-0.5), 3.0 * FF ** (-0.5)]
    grads = [grad_qkv, grad_out, grad_gu, grad_down]
    fresh = []
    row_parts = []
    col_parts = []
    for number in range(4):
        weight_new, row_new, col_new = factored(grads[number], matrices[number], row_state[rows_at[number]:rows_at[number + 1]], col_state[cols_at[number]:cols_at[number + 1]], rates[number], decay)
        fresh.append(weight_new)
        row_parts.append(row_new)
        col_parts.append(col_new)
    gain_new_state = decay * gain_state + (1.0 - decay) * (gain_grad * gain_grad + TINY_SQUARE)
    gain_update = gain_grad * lax.rsqrt(gain_new_state)
    gain_update = gain_update / jnp.maximum(1.0, jnp.sqrt(lax.optimization_barrier(jnp.mean(gain_update * gain_update, axis=1, keepdims=True))) / CLIP_LEVEL)
    new_gains = gains - GAIN_RATE * gain_update
    new_qkv = fresh[0].reshape(w_qkv.shape)
    new_out = fresh[1].reshape(w_out.shape)
    new_gu = fresh[2].reshape(w_gate_up.shape)
    new_down = fresh[3].reshape(w_down.shape)
    return (outputs.reshape(TOKENS, D), grad_acts.reshape(TOKENS, D), grad_qkv.reshape(w_qkv.shape), grad_out.reshape(w_out.shape), grad_gu.reshape(w_gate_up.shape), grad_down.reshape(w_down.shape), new_qkv, new_out, new_gu, new_down, new_qkv.astype(jnp.bfloat16), new_out.astype(jnp.bfloat16), new_gu.astype(jnp.bfloat16), new_down.astype(jnp.bfloat16), jnp.concatenate(row_parts), jnp.concatenate(col_parts), gain_grad, gain_new_state, new_gains)
```

```python
import functools

import jax
import jax.numpy as jnp
from jax import lax
from jax.experimental import pallas as pl
from jax.experimental.pallas import tpu as pltpu
from jax.sharding import PartitionSpec as P

D = 2048
H = 16
HD = 128
FF = 8192
STEP = 3


EPSILON = 1e-06
TINY_SQUARE = 1e-30
ROPE_BASE = 500000.0
NEGATIVE = -1e30
CLIP_LEVEL = 0.5
GAIN_RATE = 0.3

LOW = jnp.bfloat16
FULL = jnp.float32


def product(operand, weight):
    return jnp.dot(operand, weight, preferred_element_type=FULL)


def product_back(operand, weight):
    return lax.dot_general(operand, weight, (((1,), (1,)), ((), ())), preferred_element_type=FULL)


def weight_grad(operand, upstream):
    return lax.dot_general(
        operand, upstream, (((0,), (0,)), ((), ())), preferred_element_type=FULL
    )


def swap(values, axis, step):
    count = lax.axis_size(axis)
    return lax.ppermute(values, axis, [(i, i ^ step) for i in range(count)])


def is_relative():
    return lax.axis_size("dp") == 4


def place_of(entry):
    if is_relative():
        return lax.axis_index("dp") ^ entry
    return entry


def gather_dp(values):
    if not is_relative():
        whole = lax.all_gather(values, "dp", axis=0)
        return [whole[k] for k in range(whole.shape[0])]
    half = values.shape[0] // 2
    first = swap(values, "dp", 1)
    second = swap(values, "dp", 2)
    third = jnp.concatenate([swap(second[:half], "dp", 1), swap(first[half:], "dp", 2)], axis=0)
    return [values, first, second, third]


def scatter_dp(parts):
    if not is_relative():
        stacked = jnp.stack(parts).astype(LOW)
        return lax.psum_scatter(stacked, "dp", scatter_dimension=0).astype(FULL)
    half = parts[0].shape[0] // 2
    own, first, second, third = [part.astype(LOW) for part in parts]
    low_third = swap(third[:half], "dp", 1)
    high_third = swap(third[half:], "dp", 2)
    first_low = swap(first[:half], "dp", 1)
    second_high = swap(second[half:], "dp", 2)
    first_high = swap(
        (first[half:].astype(FULL) + high_third.astype(FULL)).astype(LOW), "dp", 1
    )
    second_low = swap(
        (second[:half].astype(FULL) + low_third.astype(FULL)).astype(LOW), "dp", 2
    )
    own_full = parts[0].astype(FULL)
    return jnp.concatenate(
        [
            own_full[:half] + first_low.astype(FULL) + second_low.astype(FULL),
            own_full[half:] + first_high.astype(FULL) + second_high.astype(FULL),
        ],
        axis=0,
    )


def trade_dp(parts):
    if not is_relative():
        traded = lax.all_to_all(jnp.stack(parts), "dp", 0, 0, tiled=True)
        return [traded[k] for k in range(traded.shape[0])]
    return [parts[0]] + [swap(parts[k], "dp", k) for k in range(1, 4)]


def exchange_dp(blocks):
    if not is_relative():
        return lax.all_to_all(blocks, "dp", 0, 0, tiled=True)
    me = lax.axis_index("dp")
    result = blocks
    for k in range(1, 4):
        sent = lax.dynamic_index_in_dim(blocks, me ^ k, 0, keepdims=True)
        result = lax.dynamic_update_slice_in_dim(result, swap(sent, "dp", k), me ^ k, 0)
    return result


def sum_dp(values):
    if not is_relative():
        return lax.psum(values, "dp")
    one = swap(values, "dp", 1)
    values = values + jnp.stack([one[1], one[0], one[3], one[2]])
    two = swap(values, "dp", 2)
    return values + jnp.stack([two[2], two[3], two[0], two[1]])


def sum_all(values):
    for axis in ("row", "dp", "col"):
        step = 1
        while step < lax.axis_size(axis):
            values = values + swap(values, axis, step)
            step *= 2
    return values


def join_row(values, axis):
    return jnp.concatenate([values, swap(values, "row", 1)], axis=axis)


def halve_row(values, axis):
    half = values.shape[axis] // 2
    kept = lax.slice_in_dim(values, 0, half, axis=axis)
    sent = lax.slice_in_dim(values, half, 2 * half, axis=axis)
    return kept + swap(sent.astype(LOW), "row", 1).astype(FULL)


def attend_kernel(starts, query, key, value, doc_key, doc_query, mixed, log_total):
    sequence = pl.program_id(0)
    parts, _, part, _ = query.shape
    length = parts * part
    nblock = starts.shape[1]
    block = length // nblock
    keys_in = key[...].reshape(length, HD)
    queries = query[...].reshape(length, HD)
    values_turned = value[...].reshape(length, HD).T
    scaling = HD ** (-0.5)
    for b in range(nblock):
        lo = b * block
        hi = lo + block
        scores = (
            lax.dot_general(
                keys_in[:hi],
                queries[lo:hi],
                (((1,), (1,)), ((), ())),
                preferred_element_type=FULL,
            )
            * scaling
        )
        place = lax.broadcasted_iota(jnp.int32, (hi, 1), 0)
        group = jnp.where(place >= starts[sequence, b] * block, doc_key[0, :hi, :], -1)
        scores = jnp.where(group == doc_query[0, :, lo:hi], scores, NEGATIVE)
        highest = jnp.max(scores, axis=0, keepdims=True)
        exponent = jnp.exp(scores - highest)
        total = jnp.sum(exponent, axis=0, keepdims=True)
        probability = (exponent * (1.0 / total)).astype(LOW)
        turned = jnp.dot(values_turned[:, :hi], probability, preferred_element_type=FULL)
        at = lo // part
        mixed[at, 0, lo - at * part : hi - at * part, :] = turned.T.astype(LOW)
        log_total[0, 0, :, lo:hi] = highest + jnp.log(total)


def attend_back_kernel(
    starts, query, key, value, grad_mixed, doc_key, doc_query, log_total, grads, grad_key, grad_value
):
    sequence = pl.program_id(0)
    head = pl.program_id(1)
    heads = pl.num_programs(1)
    parts, _, part, _ = query.shape
    length = parts * part
    nblock = starts.shape[1]
    block = length // nblock
    keys_in = key[...].reshape(length, HD)
    queries = query[...].reshape(length, HD)
    values = value[...].reshape(length, HD)
    upstream = grad_mixed[...].reshape(length, HD)
    keys_turned = keys_in.T
    scaling = HD ** (-0.5)
    query_at = pl.ds(pl.multiple_of(head * HD, HD), HD)
    for b in range(nblock - 1, -1, -1):
        lo = b * block
        hi = lo + block
        scores = (
            lax.dot_general(
                keys_in[:hi],
                queries[lo:hi],
                (((1,), (1,)), ((), ())),
                preferred_element_type=FULL,
            )
            * scaling
        )
        place = lax.broadcasted_iota(jnp.int32, (hi, 1), 0)
        group = jnp.where(place >= starts[sequence, b] * block, doc_key[0, :hi, :], -1)
        scores = jnp.where(group == doc_query[0, :, lo:hi], scores, NEGATIVE)
        probability = jnp.exp(scores - log_total[0, 0, :, lo:hi])
        term_value = jnp.dot(
            probability.astype(LOW), upstream[lo:hi], preferred_element_type=FULL
        )
        grad_prob = lax.dot_general(
            values[:hi], upstream[lo:hi], (((1,), (1,)), ((), ())), preferred_element_type=FULL
        )
        weighted = probability * grad_prob
        center = jnp.sum(weighted, axis=0, keepdims=True)
        grad_scores = (weighted - probability * center).astype(LOW)
        term_key = jnp.dot(grad_scores, queries[lo:hi], preferred_element_type=FULL)
        if b == nblock - 1:
            grad_value[...] = term_value
            grad_key[...] = term_key
        else:
            grad_value[:hi] += term_value
            grad_key[:hi] += term_key
        turned = jnp.dot(keys_turned[:, :hi], grad_scores, preferred_element_type=FULL) * scaling
        at = lo // part
        grads[at, 0, lo - at * part : hi - at * part, query_at] = turned.T.astype(LOW)
    width = heads * HD
    key_at = pl.ds(pl.multiple_of(width + head * HD, HD), HD)
    value_at = pl.ds(pl.multiple_of(2 * width + head * HD, HD), HD)
    grads[:, 0, :, key_at] = (grad_key[...] * scaling).astype(LOW).reshape(parts, part, HD)
    grads[:, 0, :, value_at] = grad_value[...].astype(LOW).reshape(parts, part, HD)


def attention_cost(packed, heads, products):
    parts, nseq, part, _ = packed.shape
    pairs = nseq * heads * (parts * part) ** 2 * 5 // 8
    return pl.CostEstimate(
        flops=2 * pairs * HD * products, bytes_accessed=2 * packed.size * 2, transcendentals=pairs
    )


def piece_spec(packed, offset):
    parts, _, part, _ = packed.shape
    return pl.BlockSpec((parts, 1, part, HD), lambda s, h, *_: (0, s, 0, offset + h))


def attend_forward(packed, starts, documents):
    parts, nseq, part, width = packed.shape
    heads = width // (3 * HD)
    length = parts * part
    return pl.pallas_call(
        attend_kernel,
        grid_spec=pltpu.PrefetchScalarGridSpec(
            num_scalar_prefetch=1,
            grid=(nseq, heads),
            in_specs=[
                piece_spec(packed, 0),
                piece_spec(packed, heads),
                piece_spec(packed, 2 * heads),
                pl.BlockSpec((1, length, 1), lambda s, h, *_: (s, 0, 0)),
                pl.BlockSpec((1, 1, length), lambda s, h, *_: (s, 0, 0)),
            ],
            out_specs=[
                piece_spec(packed, 0),
                pl.BlockSpec((1, 1, 1, length), lambda s, h, *_: (s, h, 0, 0)),
            ],
        ),
        out_shape=[
            jax.ShapeDtypeStruct((parts, nseq, part, heads * HD), LOW),
            jax.ShapeDtypeStruct((nseq, heads, 1, length), FULL),
        ],
        cost_estimate=attention_cost(packed, heads, 2),
        compiler_params=pltpu.CompilerParams(vmem_limit_bytes=48 * 1024 * 1024),
        name="attend",
    )(starts, packed, packed, packed, documents[:, :, None], documents[:, None, :])


def attend_backward(packed, starts, documents, log_total, grad_mixed):
    parts, nseq, part, width = packed.shape
    heads = width // (3 * HD)
    length = parts * part
    return pl.pallas_call(
        attend_back_kernel,
        grid_spec=pltpu.PrefetchScalarGridSpec(
            num_scalar_prefetch=1,
            grid=(nseq, heads),
            in_specs=[
                piece_spec(packed, 0),
                piece_spec(packed, heads),
                piece_spec(packed, 2 * heads),
                piece_spec(packed, 0),
                pl.BlockSpec((1, length, 1), lambda s, h, *_: (s, 0, 0)),
                pl.BlockSpec((1, 1, length), lambda s, h, *_: (s, 0, 0)),
                pl.BlockSpec((1, 1, 1, length), lambda s, h, *_: (s, h, 0, 0)),
            ],
            out_specs=pl.BlockSpec((parts, 1, part, width), lambda s, h, *_: (0, s, 0, 0)),
            scratch_shapes=[pltpu.VMEM((length, HD), FULL), pltpu.VMEM((length, HD), FULL)],
        ),
        out_shape=jax.ShapeDtypeStruct(packed.shape, LOW),
        cost_estimate=attention_cost(packed, heads, 5),
        compiler_params=pltpu.CompilerParams(vmem_limit_bytes=48 * 1024 * 1024),
        name="attend_back",
    )(
        starts,
        packed,
        packed,
        packed,
        grad_mixed,
        documents[:, :, None],
        documents[:, None, :],
        log_total,
    )


def angles(places):
    halfway = HD // 2
    frequency = ROPE_BASE ** (-jnp.arange(halfway, dtype=FULL) / halfway)
    turned = places.astype(FULL)[..., None] * frequency
    return (jnp.cos(turned)[..., None, :], jnp.sin(turned)[..., None, :])


def rotate(values, cosine, sine_term):
    halfway = values.shape[-1] // 2
    leading = values[..., :halfway]
    second = values[..., halfway:]
    return jnp.concatenate(
        [leading * cosine - second * sine_term, second * cosine + leading * sine_term], axis=-1
    )


def norm_back(upstream, normed, scaling, gain):
    scaled = upstream * gain
    inner = jnp.mean(normed * scaled, axis=1, keepdims=True)
    return (scaling * (scaled - normed * inner), jnp.sum(upstream * normed, axis=0))


def placed(shape, piece, starts):
    return lax.dynamic_update_slice(jnp.zeros(shape, FULL), piece, starts).reshape(-1)


def sequence_span(length, tokens):
    return max(1, length // tokens)


def regroup(values, span):
    if span == 1:
        return values
    n_dp, n_col = lax.axis_size("dp"), lax.axis_size("col")
    moves = []
    for i in range(n_dp):
        for j in range(n_col):
            to_i = i - i % span + j % span
            to_j = j - j % span + i % span
            moves.append((i * n_col + j, to_i * n_col + to_j))
    return lax.ppermute(values, ("dp", "col"), moves)


def heads_line_up():
    return H // lax.axis_size("col") == lax.axis_size("dp")


def fetch_qkv(low):
    nb, inner, three, heads, _ = low.shape
    n_dp, n_col = lax.axis_size("dp"), lax.axis_size("col")
    if not heads_line_up():
        whole = lax.all_gather(low, "dp", axis=1, tiled=True)
        whole = lax.all_gather(whole, "col", axis=3, tiled=True)
        mine = H // n_dp
        whole = lax.dynamic_slice_in_dim(whole, lax.axis_index("dp") * mine, mine, 3)
        return join_row(whole.reshape(nb * HD, three * mine * HD), 0)
    sent = low.transpose(3, 0, 1, 2, 4)
    got = exchange_dp(sent).transpose(1, 0, 2, 3, 4).reshape(nb * HD, three * HD)
    whole = join_row(lax.all_gather(got, "col", axis=0), 1)
    whole = whole.reshape(n_col, 2 * nb * HD, three, HD).transpose(1, 2, 0, 3)
    return whole.reshape(2 * nb * HD, three * n_col * HD)


def fetch_out(low):
    heads, inner, cols = low.shape
    n_dp, n_col = lax.axis_size("dp"), lax.axis_size("col")
    if not heads_line_up():
        whole = lax.all_gather(low, "dp", axis=1, tiled=True)
        whole = lax.all_gather(whole, "col", axis=0, tiled=True)
        return join_row(whole.reshape(D, cols), 1)
    got = exchange_dp(low).reshape(HD, cols)
    whole = lax.all_gather(got, "col", axis=0).reshape(n_col * HD, cols)
    return join_row(jnp.concatenate(gather_dp(whole), axis=0), 1)


def fetch_gate_up(low):
    nb, inner, two, cols = low.shape
    n_dp, n_col = lax.axis_size("dp"), lax.axis_size("col")
    mine = cols // n_dp
    sent = low.reshape(nb, inner, two, n_dp, mine).transpose(3, 2, 0, 1, 4)
    got = exchange_dp(sent).transpose(1, 2, 0, 3, 4).reshape(two, nb * HD, mine)
    whole = join_row(lax.all_gather(got, "col", axis=0), 2)
    return whole.transpose(2, 1, 0, 3).reshape(2 * nb * HD, two * n_col * mine)


def fetch_down(low):
    blocks, inner, cols = low.shape
    n_dp, n_col = lax.axis_size("dp"), lax.axis_size("col")
    mine = blocks // n_dp
    got = exchange_dp(low.reshape(n_dp, mine, inner, cols)).transpose(1, 0, 2, 3)
    whole = lax.all_gather(got.reshape(mine * HD, cols), "col", axis=0)
    return join_row(whole.reshape(n_col * mine * HD, cols), 1)


def reduce_col(values):
    return lax.psum_scatter(values.astype(LOW), "col", scatter_dimension=0)


def settle_qkv(grad, shape):
    nb, inner, three, heads, _ = shape
    n_dp, n_col = lax.axis_size("dp"), lax.axis_size("col")
    mine = H // n_dp
    half = halve_row(grad, 0).astype(LOW)
    if not heads_line_up():
        whole = lax.dynamic_update_slice_in_dim(
            jnp.zeros((nb, HD, three, H, HD), LOW),
            half.reshape(nb, HD, three, mine, HD),
            lax.axis_index("dp") * mine,
            3,
        )
        whole = lax.psum_scatter(whole, "dp", scatter_dimension=1, tiled=True)
        return lax.psum_scatter(whole, "col", scatter_dimension=3, tiled=True).astype(FULL)
    half = half.reshape(nb * HD, three, n_col, HD).transpose(2, 0, 1, 3)
    summed = reduce_col(half.reshape(n_col, nb * HD, three * HD))
    sent = summed.reshape(nb, n_dp, inner, three, HD).transpose(1, 0, 2, 3, 4)
    return exchange_dp(sent).transpose(1, 2, 3, 0, 4).astype(FULL)


def settle_out(grad, shape):
    heads, inner, cols = shape
    n_dp, n_col = lax.axis_size("dp"), lax.axis_size("col")
    half = halve_row(grad, 1)
    if not heads_line_up():
        whole = half.astype(LOW).reshape(H, HD, cols)
        whole = lax.psum_scatter(whole, "dp", scatter_dimension=1, tiled=True)
        return lax.psum_scatter(whole, "col", scatter_dimension=0, tiled=True).astype(FULL)
    rows = half.shape[0] // n_dp
    mine = scatter_dp([half[k * rows : (k + 1) * rows] for k in range(n_dp)])
    summed = reduce_col(mine.reshape(n_col, HD, cols))
    return exchange_dp(summed.reshape(n_dp, inner, cols)).astype(FULL)


def settle_gate_up(grad, shape):
    nb, inner, two, cols = shape
    n_dp, n_col = lax.axis_size("dp"), lax.axis_size("col")
    mine = cols // n_dp
    half = halve_row(grad, 0).astype(LOW)
    half = half.reshape(nb * HD, two, n_col, mine).transpose(2, 1, 0, 3)
    summed = reduce_col(half)
    sent = summed.reshape(two, nb, n_dp, inner, mine).transpose(2, 0, 1, 3, 4)
    got = exchange_dp(sent).transpose(2, 3, 1, 0, 4)
    return got.reshape(nb, inner, two, cols).astype(FULL)


def settle_down(grad, shape):
    blocks, inner, cols = shape
    n_dp, n_col = lax.axis_size("dp"), lax.axis_size("col")
    mine = blocks // n_dp
    half = halve_row(grad, 1).reshape(n_col, mine * HD, cols)
    summed = reduce_col(half)
    sent = summed.reshape(mine, n_dp, inner, cols).transpose(1, 0, 2, 3)
    return exchange_dp(sent).reshape(blocks, inner, cols).astype(FULL)


DECAY = 1.0 - STEP ** (-0.8)


def second_moments(squares, old_row, old_col, row_count, col_count, row_shape, col_shape, row_at, col_at):
    column_axes = tuple(range(2, squares.ndim))
    row_part = placed(row_shape, jnp.sum(squares, axis=column_axes), row_at)
    col_part = placed(col_shape, jnp.sum(squares, axis=(0, 1)), col_at)
    sums = sum_all(jnp.concatenate([row_part, col_part]))
    row_means = sums[:row_count] / col_count + TINY_SQUARE
    col_means = sums[row_count:] / row_count + TINY_SQUARE
    return (
        DECAY * old_row + (1.0 - DECAY) * row_means,
        DECAY * old_col + (1.0 - DECAY) * col_means,
    )


def step_matrix(grad, weight, old_row, old_col, row_shape, col_shape, row_at, col_at, rate):
    row_count = old_row.shape[0]
    col_count = old_col.shape[0]
    new_row, new_col = second_moments(
        grad * grad, old_row, old_col, row_count, col_count, row_shape, col_shape, row_at, col_at
    )
    row_here = lax.dynamic_slice(new_row.reshape(row_shape), row_at, grad.shape[:2])
    col_here = lax.dynamic_slice(new_col.reshape(col_shape), col_at, grad.shape[2:])
    row_here = row_here.reshape(grad.shape[:2] + (1,) * (grad.ndim - 2))
    update = grad * lax.rsqrt(row_here * col_here[None, None] / jnp.mean(new_row))
    size = sum_all(jnp.sum(update * update).reshape(1, 1))[0, 0]
    count = row_count * col_count
    renewed = weight - rate * update / jnp.maximum(1.0, jnp.sqrt(size / count) / CLIP_LEVEL)
    return (renewed, new_row, new_col)


def shards(
    inputs,
    cotangent,
    w_qkv,
    w_out,
    w_gate_up,
    w_down,
    gains,
    gain_state,
    row_state,
    col_state,
    positions,
    block_map,
):
    row_pos = lax.axis_index("row")
    col_pos = lax.axis_index("col")
    data_pos = lax.axis_index("dp")
    n_dp, n_col = lax.axis_size("dp"), lax.axis_size("col")
    length = positions.shape[1]
    chip_tokens = inputs.shape[0]
    tokens = chip_tokens // 2
    width = inputs.shape[1]
    span = sequence_span(length, chip_tokens)
    heads_here = H // n_dp
    local = heads_here * HD

    def enter(values):
        values = regroup(values, span)
        kept = lax.dynamic_slice_in_dim(values, row_pos * tokens, tokens, 0)
        sent = lax.dynamic_slice_in_dim(values, (1 - row_pos) * tokens, tokens, 0)
        return jnp.concatenate([kept, swap(sent, "row", 1)], axis=1)

    def leave(values):
        got = swap(values[:, width:], "row", 1)
        result = jnp.zeros((chip_tokens, width), values.dtype)
        result = lax.dynamic_update_slice_in_dim(result, values[:, :width], row_pos * tokens, 0)
        result = lax.dynamic_update_slice_in_dim(result, got, (1 - row_pos) * tokens, 0)
        return regroup(result, span)

    def own_first(vector):
        parts = vector.reshape(2, width)
        return jnp.concatenate(
            [
                lax.dynamic_index_in_dim(parts, row_pos, 0, keepdims=False),
                lax.dynamic_index_in_dim(parts, 1 - row_pos, 0, keepdims=False),
            ]
        )

    x_own = enter(inputs)
    grad_result = enter(cotangent).astype(FULL)
    x_parts = gather_dp(x_own)
    matrix_qkv = fetch_qkv(w_qkv.astype(LOW))
    matrix_out = fetch_out(w_out.astype(LOW))
    matrix_gu = fetch_gate_up(w_gate_up.astype(LOW))
    matrix_down = fetch_down(w_down.astype(LOW))

    every_place = lax.all_gather(
        jnp.concatenate([positions, block_map], axis=1), ("dp", "row"), axis=0, tiled=True
    )
    sequences = n_dp // span
    numbers = []
    for k in range(sequences):
        first = place_of(k) if span == 1 else k * span + col_pos % span
        numbers.append(first * (n_col // span) + col_pos // span)
    here = jnp.concatenate(
        [lax.dynamic_slice_in_dim(every_place, number, 1, 0) for number in numbers], axis=0
    )
    places = here[:, :length]
    starts = here[:, length:]
    documents = jnp.cumsum((places == 0).astype(jnp.int32), axis=1)
    token_places = lax.dynamic_index_in_dim(
        places.reshape(n_dp, 2, tokens), row_pos, 1, keepdims=False
    )
    cosine, sine_term = angles(token_places)

    qkv = jnp.stack([product(part, matrix_qkv) for part in x_parts])
    query_raw = qkv[:, :, :local]
    key_raw = qkv[:, :, local : 2 * local]
    value_raw = qkv[:, :, 2 * local :]
    squares = sum_dp(
        jnp.stack(
            [jnp.sum(query_raw * query_raw, axis=2), jnp.sum(key_raw * key_raw, axis=2)], axis=1
        )
    )
    scales = lax.rsqrt(squares / D + EPSILON)
    query_scale = scales[:, 0, :, None]
    key_scale = scales[:, 1, :, None]
    if heads_line_up():
        gain_here = lax.dynamic_index_in_dim(
            gains[:2].reshape(2, n_col, n_dp, HD), data_pos, 2, keepdims=False
        ).reshape(2, local)
    else:
        gain_here = lax.dynamic_slice_in_dim(gains[:2], data_pos * local, local, 1)
    query_hat = query_raw * query_scale
    key_hat = key_raw * key_scale
    by_head = (n_dp, tokens, heads_here, HD)
    query_rot = rotate((query_hat * gain_here[0]).reshape(by_head), cosine, sine_term)
    key_rot = rotate((key_hat * gain_here[1]).reshape(by_head), cosine, sine_term)

    def to_heads(pieces):
        pieces = [piece.astype(LOW).reshape(n_dp, tokens, 2, local // 2) for piece in pieces]
        sent = jnp.stack(
            [
                jnp.concatenate([piece[:, :, core] for piece in pieces], axis=2)
                for core in range(2)
            ]
        )
        return lax.all_to_all(sent, "row", 0, 0, tiled=True)

    def from_heads(values):
        return lax.all_to_all(values, "row", 0, 0, tiled=True)

    def by_sequence(values):
        if span == 1:
            return values
        last = values.shape[-1]
        values = values.reshape(2, sequences, span, tokens, last).transpose(1, 2, 0, 3, 4)
        return values.reshape(1, sequences, length, last)

    def by_shard(values):
        if span == 1:
            return values
        last = values.shape[-1]
        values = values.reshape(sequences, span, 2, tokens, last).transpose(2, 0, 1, 3, 4)
        return values.reshape(2, n_dp, tokens, last)

    packed = by_sequence(
        to_heads([query_rot.reshape(qkv.shape[:2] + (local,)), key_rot.reshape(qkv.shape[:2] + (local,)), value_raw])
    )
    mixed, log_total = attend_forward(packed, starts, documents)
    mixed = from_heads(by_shard(mixed))
    mixed = trade_dp([mixed[:, k] for k in range(n_dp)])
    attended = jnp.stack(mixed).transpose(2, 0, 1, 3).reshape(tokens, D)

    attn = product(attended, matrix_out)
    gain_attn = own_first(gains[2])[None, :]
    gain_mlp = own_first(gains[3])[None, :]
    attn_scale = lax.rsqrt(jnp.mean(attn * attn, axis=1, keepdims=True) + EPSILON)
    attn_hat = attn * attn_scale
    hidden_in = x_own.astype(FULL) + attn_hat * gain_attn
    h_parts = gather_dp(hidden_in.astype(LOW))

    ff_here = matrix_gu.shape[1] // 2
    gates, ups, hiddens, terms = [], [], [], []
    for part in h_parts:
        gate_up = product(part, matrix_gu)
        gate = gate_up[:, :ff_here]
        up_part = gate_up[:, ff_here:]
        hidden = (jax.nn.silu(gate) * up_part).astype(LOW)
        gates.append(gate)
        ups.append(up_part)
        hiddens.append(hidden)
        terms.append(product(hidden, matrix_down))
    mlp = scatter_dp(terms)
    mlp_scale = lax.rsqrt(jnp.mean(mlp * mlp, axis=1, keepdims=True) + EPSILON)
    mlp_hat = mlp * mlp_scale
    result = leave(hidden_in + mlp_hat * gain_mlp)

    grad_mlp, gain_mlp_grad = norm_back(grad_result, mlp_hat, mlp_scale, gain_mlp)
    m_parts = gather_dp(grad_mlp.astype(LOW))
    gu_parts, terms = [], []
    for k, part in enumerate(m_parts):
        grad_hidden = product_back(part, matrix_down)
        gate, up_part = gates[k], ups[k]
        sigmoid_gate = jax.nn.sigmoid(gate)
        grad_gate = grad_hidden * up_part * sigmoid_gate * (1.0 + gate * (1.0 - sigmoid_gate))
        grad_up = grad_hidden * gate * sigmoid_gate
        gu_parts.append(jnp.concatenate([grad_gate, grad_up], axis=1).astype(LOW))
        terms.append(product_back(gu_parts[k], matrix_gu))
    grad_hidden_in = grad_result + scatter_dp(terms)
    down_grad = weight_grad(jnp.concatenate(hiddens), jnp.concatenate(m_parts))
    gu_grad = weight_grad(jnp.concatenate(h_parts), jnp.concatenate(gu_parts))
    grad_down = settle_down(down_grad, w_down.shape)
    grad_gu = settle_gate_up(gu_grad, w_gate_up.shape)

    grad_attn, gain_attn_grad = norm_back(grad_hidden_in, attn_hat, attn_scale, gain_attn)
    grad_attn_low = grad_attn.astype(LOW)
    grad_attended = product_back(grad_attn_low, matrix_out).astype(LOW)
    grad_out = settle_out(weight_grad(attended, grad_attn_low), w_out.shape)
    sent = grad_attended.reshape(tokens, n_dp, 2, local // 2).transpose(1, 2, 0, 3)
    got = jnp.stack(trade_dp([sent[k] for k in range(n_dp)]), axis=1)
    grad_mixed = by_sequence(from_heads(got))
    grads = attend_backward(packed, starts, documents, log_total, grad_mixed)
    grads = from_heads(by_shard(grads))
    grads = grads.reshape(2, n_dp, tokens, 3, local // 2).transpose(3, 1, 2, 0, 4)
    grads = grads.reshape(3, n_dp, tokens, local)

    grad_qn = rotate(grads[0].astype(FULL).reshape(by_head), cosine, -sine_term)
    grad_kn = rotate(grads[1].astype(FULL).reshape(by_head), cosine, -sine_term)
    grad_qn = grad_qn.reshape(n_dp, tokens, local)
    grad_kn = grad_kn.reshape(n_dp, tokens, local)
    scaled_query = grad_qn * gain_here[0]
    scaled_key = grad_kn * gain_here[1]
    inner = sum_dp(
        jnp.stack(
            [jnp.sum(query_hat * scaled_query, axis=2), jnp.sum(key_hat * scaled_key, axis=2)],
            axis=1,
        )
    )
    inner = inner / D
    grad_query = query_scale * (scaled_query - query_hat * inner[:, 0, :, None])
    grad_key = key_scale * (scaled_key - key_hat * inner[:, 1, :, None])
    gain_query_grad = jnp.sum(grad_qn * query_hat, axis=(0, 1))
    gain_key_grad = jnp.sum(grad_kn * key_hat, axis=(0, 1))
    qkv_low = jnp.concatenate(
        [grad_query.astype(LOW), grad_key.astype(LOW), grads[2]], axis=2
    )
    x_term = scatter_dp([product_back(qkv_low[k], matrix_qkv) for k in range(n_dp)])
    grad_inputs = leave(grad_hidden_in + x_term)
    qkv_grad = weight_grad(
        jnp.concatenate(x_parts), qkv_low.reshape(n_dp * tokens, 3 * local)
    )
    grad_qkv = settle_qkv(qkv_grad, w_qkv.shape)

    pair = jnp.stack([gain_query_grad, gain_key_grad])
    if heads_line_up():
        pair = placed(
            (2, n_col, n_dp, HD), pair.reshape(2, n_col, 1, HD), (0, 0, data_pos, 0)
        )
    else:
        pair = placed((2, D), pair, (0, data_pos * local))
    gain_partial = jnp.concatenate(
        [
            pair.reshape(2, D),
            own_first(gain_attn_grad)[None, :],
            own_first(gain_mlp_grad)[None, :],
        ]
    )
    gain_grad = sum_all(gain_partial)

    nb_rows, inner_rows, _, heads_col, _ = grad_qkv.shape
    ff_blocks = grad_down.shape[0]
    ff_cols = grad_gu.shape[3]
    row_at = (row_pos * nb_rows, data_pos * inner_rows)
    new_down, row_down, col_down = step_matrix(
        grad_down,
        w_down,
        row_state[3 * D :],
        col_state[4 * D + 2 * FF :],
        (FF // HD, HD),
        (D,),
        (col_pos * ff_blocks, data_pos * inner_rows),
        (row_pos * width,),
        3.0 * FF ** (-0.5),
    )
    new_gu, row_gu, col_gu = step_matrix(
        grad_gu,
        w_gate_up,
        row_state[2 * D : 3 * D],
        col_state[4 * D : 4 * D + 2 * FF],
        (D // HD, HD),
        (2, FF),
        row_at,
        (0, col_pos * ff_cols),
        3.0 * D ** (-0.5),
    )
    new_out, row_out, col_out = step_matrix(
        grad_out,
        w_out,
        row_state[D : 2 * D],
        col_state[3 * D : 4 * D],
        (H, HD),
        (D,),
        (col_pos * heads_col, data_pos * inner_rows),
        (row_pos * width,),
        3.0 * D ** (-0.5),
    )
    new_qkv, row_qkv, col_qkv = step_matrix(
        grad_qkv,
        w_qkv,
        row_state[:D],
        col_state[: 3 * D],
        (D // HD, HD),
        (3, H, HD),
        row_at,
        (0, col_pos * heads_col, 0),
        3.0 * D ** (-0.5),
    )
    gain_new_state = DECAY * gain_state + (1.0 - DECAY) * (gain_grad * gain_grad + TINY_SQUARE)
    gain_update = gain_grad * lax.rsqrt(gain_new_state)
    gain_update = gain_update / jnp.maximum(
        1.0, jnp.sqrt(jnp.mean(gain_update * gain_update, axis=1, keepdims=True)) / CLIP_LEVEL
    )
    new_gains = gains - GAIN_RATE * gain_update
    return (
        result,
        grad_inputs,
        grad_qkv,
        grad_out,
        grad_gu,
        grad_down,
        new_qkv,
        new_out,
        new_gu,
        new_down,
        new_qkv.astype(LOW),
        new_out.astype(LOW),
        new_gu.astype(LOW),
        new_down.astype(LOW),
        jnp.concatenate([row_qkv, row_out, row_gu, row_down]),
        jnp.concatenate([col_qkv, col_out, col_gu, col_down]),
        gain_grad,
        gain_new_state,
        new_gains,
    )


def solution(mesh):
    return jax.shard_map(
        shards,
        mesh=mesh,
        in_specs=(
            P(("dp", "col"), "row"),
            P(("dp", "col"), "row"),
            P("row", "dp", None, "col", None),
            P("col", "dp", "row"),
            P("row", "dp", None, "col"),
            P("col", "dp", "row"),
            P(),
            P(),
            P(),
            P(),
            P(("dp", "row"), None),
            P(("dp", "row"), None),
        ),
        out_specs=(
            P(("dp", "col"), "row"),
            P(("dp", "col"), "row"),
            P("row", "dp", None, "col", None),
            P("col", "dp", "row"),
            P("row", "dp", None, "col"),
            P("col", "dp", "row"),
            P("row", "dp", None, "col", None),
            P("col", "dp", "row"),
            P("row", "dp", None, "col"),
            P("col", "dp", "row"),
            P("row", "dp", None, "col", None),
            P("col", "dp", "row"),
            P("row", "dp", None, "col"),
            P("col", "dp", "row"),
            P(),
            P(),
            P(),
            P(),
            P(),
        ),
        check_vma=False,
    )
```

```python
import functools

import jax
import jax.numpy as jnp
from jax import lax
from jax.experimental import pallas as pl
from jax.experimental.pallas import tpu as pltpu
from jax.sharding import PartitionSpec as P

D = 2048
H = 16
HD = 128
FF = 8192
STEP = 3


EPSILON = 1e-06
TINY_SQUARE = 1e-30
ROPE_BASE = 500000.0
NEGATIVE = -1e30
CLIP_LEVEL = 0.5
GAIN_RATE = 0.3

LOW = jnp.bfloat16
FULL = jnp.float32


VMEM_LIMIT = 56 * 1024 * 1024


def dot(left, right):
    return jnp.dot(left, right, preferred_element_type=FULL)


def dot_back(left, right):
    return lax.dot_general(left, right, (((1,), (1,)), ((), ())), preferred_element_type=FULL)


def scaled_cost(flops, bytes_accessed, transcendentals, factor=2):
    return pl.CostEstimate(
        flops=factor * flops,
        bytes_accessed=factor * bytes_accessed,
        transcendentals=factor * transcendentals,
    )


def with_deps(kernel, count, deps):
    def body(*refs):
        return kernel(*refs[:count], *refs[count + len(deps) :])

    return body


def dep_specs(deps):
    return [pl.BlockSpec(memory_space=pl.ANY)] * len(deps)


def after(value, *others):
    if not others:
        return value

    def body(*refs):
        pass

    return pl.pallas_call(
        body,
        in_specs=dep_specs((value,) + others),
        out_specs=pl.BlockSpec(memory_space=pl.ANY),
        out_shape=jax.ShapeDtypeStruct(value.shape, value.dtype),
        input_output_aliases={0: 0},
        name="after",
    )(value, *others)


def kernel_params():
    return pltpu.CompilerParams(vmem_limit_bytes=VMEM_LIMIT)


def gate_kernel(h, gu_own, gu_other, hidden, by_gate, by_up):
    half = gu_own.shape[2]
    left = h[:, :half]
    right = h[:, half:]
    gate = dot(left, gu_own[0, 0]) + dot(right, gu_other[0, 0])
    up = dot(left, gu_own[0, 1]) + dot(right, gu_other[0, 1])
    sigmoid_gate = 1.0 / (1.0 + jnp.exp(-gate))
    silu = gate * sigmoid_gate
    hidden[...] = (silu * up).astype(LOW)
    by_gate[...] = (up * sigmoid_gate * (1.0 + gate * (1.0 - sigmoid_gate))).astype(LOW)
    by_up[...] = silu.astype(LOW)


def gate_forward(h, gu_own, gu_other, deps=()):
    tokens, width = h.shape
    n_col, _, half, mine = gu_own.shape
    weight = pl.BlockSpec((1, 2, half, mine), lambda j: (j, 0, 0, 0))
    piece = pl.BlockSpec((tokens, mine), lambda j: (0, j))
    shape = jax.ShapeDtypeStruct((tokens, n_col * mine), LOW)
    return pl.pallas_call(
        with_deps(gate_kernel, 3, deps),
        grid=(n_col,),
        in_specs=[pl.BlockSpec((tokens, width), lambda j: (0, 0)), weight, weight]
        + dep_specs(deps),
        out_specs=[piece, piece, piece],
        out_shape=[shape, shape, shape],
        cost_estimate=scaled_cost(
            flops=4 * tokens * width * n_col * mine,
            bytes_accessed=4 * gu_own.size + 2 * h.size + 6 * tokens * n_col * mine,
            transcendentals=tokens * n_col * mine,
        ),
        compiler_params=kernel_params(),
        name="gate_up",
    )(h, gu_own, gu_other, *deps)


def down_kernel(hidden, down_own, down_other, term):
    half = down_own.shape[1]
    term[:, :half] = dot(hidden[...], down_own[...]).astype(term.dtype)
    term[:, half:] = dot(hidden[...], down_other[...]).astype(term.dtype)


def down_forward(hidden, down_own, down_other, kind=LOW, deps=()):
    tokens, units = hidden.shape
    half = down_own.shape[1]
    rows = min(tokens, 256)
    weight = pl.BlockSpec((units, half), lambda i: (0, 0))
    return pl.pallas_call(
        with_deps(down_kernel, 3, deps),
        grid=(tokens // rows,),
        in_specs=[pl.BlockSpec((rows, units), lambda i: (i, 0)), weight, weight]
        + dep_specs(deps),
        out_specs=pl.BlockSpec((rows, 2 * half), lambda i: (i, 0)),
        out_shape=jax.ShapeDtypeStruct((tokens, 2 * half), kind),
        cost_estimate=scaled_cost(
            flops=4 * tokens * units * half,
            bytes_accessed=4 * down_own.size + 2 * hidden.size + 4 * tokens * half,
            transcendentals=0,
        ),
        compiler_params=kernel_params(),
        name="down",
    )(hidden, down_own, down_other, *deps)


def attended_back_kernel(grad, out_own, out_other, *results):
    half = out_own.shape[1]
    value = dot_back(grad[:, :half], out_own[...]) + dot_back(grad[:, half:], out_other[...])
    for k in range(len(results)):

        @pl.when(pl.program_id(0) == k)
        def _(k=k):
            results[k][0] = value.astype(LOW)


def attended_backward(grad, out_own, out_other, n_dp, deps):
    tokens, width = grad.shape
    rows, half = out_own.shape
    columns = rows // n_dp // 2
    weight = pl.BlockSpec((columns, half), lambda k, c: (2 * k + c, 0))

    def result_spec(i):
        return pl.BlockSpec(
            (1, tokens, columns), lambda k, c: (jnp.clip(2 * (k - i) + c, 0, 1), 0, 0)
        )

    return pl.pallas_call(
        with_deps(attended_back_kernel, 3, deps),
        grid=(n_dp, 2),
        in_specs=[pl.BlockSpec((tokens, width), lambda k, c: (0, 0)), weight, weight]
        + dep_specs(deps),
        out_specs=[result_spec(i) for i in range(n_dp)],
        out_shape=[jax.ShapeDtypeStruct((2, tokens, columns), LOW)] * n_dp,
        cost_estimate=scaled_cost(
            factor=3,
            flops=2 * grad.size * rows,
            bytes_accessed=4 * out_own.size + 2 * grad.size + 2 * tokens * rows,
            transcendentals=0,
        ),
        compiler_params=kernel_params(),
        name="attended_back",
    )(grad, out_own, out_other, *deps)


def mlp_back_kernel(
    m, by_gate, by_up, gu_own, gu_other, down_own, down_other, grad_gate, grad_up, term, total
):
    j = pl.program_id(0)
    half = gu_own.shape[2]
    grad_hidden = dot_back(m[:, :half], down_own[0]) + dot_back(m[:, half:], down_other[0])
    low_gate = (grad_hidden * by_gate[...].astype(FULL)).astype(LOW)
    low_up = (grad_hidden * by_up[...].astype(FULL)).astype(LOW)
    grad_gate[...] = low_gate
    grad_up[...] = low_up
    own = dot_back(low_gate, gu_own[0, 0]) + dot_back(low_up, gu_own[0, 1])
    other = dot_back(low_gate, gu_other[0, 0]) + dot_back(low_up, gu_other[0, 1])

    @pl.when(j == 0)
    def _():
        total[:, :half] = own
        total[:, half:] = other

    @pl.when(j > 0)
    def _():
        total[:, :half] += own
        total[:, half:] += other

    @pl.when(j == pl.num_programs(0) - 1)
    def _():
        term[...] = total[...].astype(LOW)


def mlp_backward(m, by_gate, by_up, gu_own, gu_other, down_own, down_other, deps=()):
    tokens, width = m.shape
    n_col, _, half, mine = gu_own.shape
    weight = pl.BlockSpec((1, 2, half, mine), lambda j: (j, 0, 0, 0))
    weight_down = pl.BlockSpec((1, mine, half), lambda j: (j, 0, 0))
    piece = pl.BlockSpec((tokens, mine), lambda j: (0, j))
    whole = pl.BlockSpec((tokens, width), lambda j: (0, 0))
    shape = jax.ShapeDtypeStruct((tokens, n_col * mine), LOW)
    return pl.pallas_call(
        with_deps(mlp_back_kernel, 7, deps),
        grid=(n_col,),
        in_specs=[whole, piece, piece, weight, weight, weight_down, weight_down]
        + dep_specs(deps),
        out_specs=[piece, piece, whole],
        out_shape=[shape, shape, jax.ShapeDtypeStruct((tokens, width), LOW)],
        scratch_shapes=[pltpu.VMEM((tokens, width), FULL)],
        cost_estimate=scaled_cost(
            flops=6 * tokens * width * n_col * mine,
            bytes_accessed=6 * gu_own.size + 4 * m.size + 8 * tokens * n_col * mine,
            transcendentals=0,
        ),
        compiler_params=kernel_params(),
        name="mlp_back",
    )(
        m,
        by_gate,
        by_up,
        gu_own,
        gu_other,
        down_own.reshape(n_col, mine, half),
        down_other.reshape(n_col, mine, half),
        *deps,
    )


def grad_kernel(count, groups, received, *refs):
    left = refs[:count]
    right = refs[count : count + count * groups]
    result, turned = refs[-2], refs[-1]
    part = left[0].shape[0]

    @pl.when(pl.program_id(1) == 0)
    def _():
        for k in range(count):
            turned[:, k * part : (k + 1) * part] = left[k][...].T

    for g in range(groups):
        total = None
        for k in range(count):
            term = dot(turned[:, k * part : (k + 1) * part], right[g * count + k][...])
            total = term if total is None else total + term
        if received:
            total = total + refs[-3][0, g].astype(FULL)
        result[0, g] = total.astype(LOW)


def grad_block(
    left, left_at, rows, right, right_at, columns, steps, received, deps=(), factor=2
):
    count, groups = len(left), len(right)
    part = left[0].shape[0]
    tile = min(rows, 512)
    tiles = rows // tile
    left_spec = pl.BlockSpec((part, tile), lambda a, j: (0, left_at * tiles + a))
    right_spec = pl.BlockSpec((part, columns), lambda a, j: (0, right_at + j))
    result_spec = pl.BlockSpec((1, groups, tile, columns), lambda a, j: (j, 0, a, 0))
    operands = list(left) + [piece for group in right for piece in group]
    specs = [left_spec] * count + [right_spec] * (count * groups)
    if received is not None:
        operands.append(received)
        specs.append(result_spec)
    reads = len(operands)
    size = steps * groups * rows * columns
    return pl.pallas_call(
        with_deps(
            functools.partial(grad_kernel, count, groups, received is not None), reads, deps
        ),
        grid=(tiles, steps),
        in_specs=specs + dep_specs(deps),
        out_specs=result_spec,
        out_shape=jax.ShapeDtypeStruct((steps, groups, rows, columns), LOW),
        scratch_shapes=[pltpu.VMEM((tile, count * part), LOW)],
        cost_estimate=scaled_cost(
            factor=factor,
            flops=2 * size * count * part,
            bytes_accessed=4 * size + 2 * count * part * (rows + steps * groups * columns * tiles),
            transcendentals=0,
        ),
        compiler_params=kernel_params(),
        name="weight_grad",
    )(*operands, *deps)


def qkv_kernel(x, w_own, w_other, raw, squares, query_sum, key_sum):
    j = pl.program_id(1)
    half = w_own.shape[1]
    got = dot(x[0, :, :half], w_own[0]) + dot(x[0, :, half:], w_other[0])
    raw[0] = got
    query = got[:, :HD]
    key = got[:, HD : 2 * HD]

    @pl.when(j == 0)
    def _():
        query_sum[...] = query * query
        key_sum[...] = key * key

    @pl.when(j > 0)
    def _():
        query_sum[...] += query * query
        key_sum[...] += key * key

    @pl.when(j == pl.num_programs(1) - 1)
    def _():
        squares[0, 0:1] = jnp.sum(query_sum[...].T, axis=0, keepdims=True)
        squares[0, 1:2] = jnp.sum(key_sum[...].T, axis=0, keepdims=True)


def qkv_forward(x, w_own, w_other):
    shards_of, tokens, width = x.shape
    heads, half, columns = w_own.shape
    weight = pl.BlockSpec((1, half, columns), lambda k, j: (j, 0, 0))
    return pl.pallas_call(
        qkv_kernel,
        grid=(shards_of, heads),
        in_specs=[pl.BlockSpec((1, tokens, width), lambda k, j: (k, 0, 0)), weight, weight],
        out_specs=[
            pl.BlockSpec((1, tokens, columns), lambda k, j: (k, 0, j)),
            pl.BlockSpec((1, 2, tokens), lambda k, j: (k, 0, 0)),
        ],
        out_shape=[
            jax.ShapeDtypeStruct((shards_of, tokens, heads * columns), FULL),
            jax.ShapeDtypeStruct((shards_of, 2, tokens), FULL),
        ],
        scratch_shapes=[pltpu.VMEM((tokens, HD), FULL), pltpu.VMEM((tokens, HD), FULL)],
        cost_estimate=scaled_cost(
            flops=2 * x.size * heads * columns,
            bytes_accessed=2 * x.size + 4 * shards_of * w_own.size + 4 * shards_of * tokens * heads * columns,
            transcendentals=0,
        ),
        compiler_params=kernel_params(),
        name="qkv",
    )(x, w_own, w_other)


def token_scales(squares):
    return lax.rsqrt(squares[0] / D + EPSILON).T


def rope_kernel(raw, squares, cosine, sine_term, gain, packed):
    heads = gain.shape[1] // HD
    scales = token_scales(squares)
    for h in range(heads):
        core, at = h // (heads // 2), h % (heads // 2) * 3 * HD
        for n in range(2):
            value = raw[0, :, (3 * h + n) * HD : (3 * h + n + 1) * HD] * scales[:, n : n + 1]
            value = value * gain[n : n + 1, h * HD : (h + 1) * HD]
            turned = value * cosine[0] + pltpu.roll(value, HD // 2, 1) * sine_term[0]
            packed[core, 0, :, at + n * HD : at + (n + 1) * HD] = turned.astype(LOW)
        packed[core, 0, :, at + 2 * HD : at + 3 * HD] = raw[
            0, :, (3 * h + 2) * HD : (3 * h + 3) * HD
        ].astype(LOW)


def rope_specs(raw, gain):
    shards_of, tokens, columns = raw.shape
    return [
        pl.BlockSpec((1, tokens, columns), lambda k: (k, 0, 0)),
        pl.BlockSpec((1, 2, tokens), lambda k: (k, 0, 0)),
        pl.BlockSpec((1, tokens, HD), lambda k: (k, 0, 0)),
        pl.BlockSpec((1, tokens, HD), lambda k: (k, 0, 0)),
        pl.BlockSpec(gain.shape, lambda k: (0, 0)),
    ]


def rope_forward(raw, squares, cosine, sine_term, gain, deps=()):
    shards_of, tokens, columns = raw.shape
    return pl.pallas_call(
        with_deps(rope_kernel, 5, deps),
        grid=(shards_of,),
        in_specs=rope_specs(raw, gain) + dep_specs(deps),
        out_specs=pl.BlockSpec((2, 1, tokens, columns // 2), lambda k: (0, k, 0, 0)),
        out_shape=jax.ShapeDtypeStruct((2, shards_of, tokens, columns // 2), LOW),
        cost_estimate=scaled_cost(
            flops=8 * raw.size, bytes_accessed=6 * raw.size, transcendentals=0
        ),
        compiler_params=kernel_params(),
        name="rope",
    )(raw, squares, cosine, sine_term, gain, *deps)


def turned_back(grads, raw, cosine, sine_term, gain, scales, h, n):
    heads = gain.shape[1] // HD
    core, at = h // (heads // 2), (h % (heads // 2) * 3 + n) * HD
    value = grads[core, 0, :, at : at + HD].astype(FULL)
    value = value * cosine[0] - pltpu.roll(value, HD // 2, 1) * sine_term[0]
    normed = raw[0, :, (3 * h + n) * HD : (3 * h + n + 1) * HD] * scales[:, n : n + 1]
    return (value, normed, value * gain[n : n + 1, h * HD : (h + 1) * HD])


def rope_inner_kernel(raw, squares, cosine, sine_term, gain, grads, inner, gain_grad):
    heads = gain.shape[1] // HD
    scales = token_scales(squares)

    @pl.when(pl.program_id(0) == 0)
    def _():
        gain_grad[...] = jnp.zeros(gain_grad.shape, FULL)

    for n in range(2):
        total = None
        for h in range(heads):
            value, normed, scaled = turned_back(
                grads, raw, cosine, sine_term, gain, scales, h, n
            )
            term = normed * scaled
            total = term if total is None else total + term
            gain_grad[n : n + 1, h * HD : (h + 1) * HD] += jnp.sum(
                value * normed, axis=0, keepdims=True
            )
        inner[0, n : n + 1] = jnp.sum(total.T, axis=0, keepdims=True)


def rope_inner(raw, squares, cosine, sine_term, gain, grads, deps=()):
    shards_of, tokens, columns = raw.shape
    return pl.pallas_call(
        with_deps(rope_inner_kernel, 6, deps),
        grid=(shards_of,),
        in_specs=rope_specs(raw, gain)
        + [pl.BlockSpec((2, 1, tokens, columns // 2), lambda k: (0, k, 0, 0))]
        + dep_specs(deps),
        out_specs=[
            pl.BlockSpec((1, 2, tokens), lambda k: (k, 0, 0)),
            pl.BlockSpec(gain.shape, lambda k: (0, 0)),
        ],
        out_shape=[
            jax.ShapeDtypeStruct((shards_of, 2, tokens), FULL),
            jax.ShapeDtypeStruct(gain.shape, FULL),
        ],
        cost_estimate=scaled_cost(
            factor=4,
            flops=12 * raw.size, bytes_accessed=6 * raw.size, transcendentals=0
        ),
        compiler_params=kernel_params(),
        name="rope_inner",
    )(raw, squares, cosine, sine_term, gain, grads, *deps)


def rope_back_kernel(raw, squares, cosine, sine_term, gain, grads, inner, result):
    heads = gain.shape[1] // HD
    scales = token_scales(squares)
    means = (inner[0] / D).T
    for h in range(heads):
        for n in range(2):
            _, normed, scaled = turned_back(grads, raw, cosine, sine_term, gain, scales, h, n)
            value = scales[:, n : n + 1] * (scaled - normed * means[:, n : n + 1])
            result[0, :, (3 * h + n) * HD : (3 * h + n + 1) * HD] = value.astype(LOW)
        core, at = h // (heads // 2), (h % (heads // 2) * 3 + 2) * HD
        result[0, :, (3 * h + 2) * HD : (3 * h + 3) * HD] = grads[core, 0, :, at : at + HD]


def rope_backward(raw, squares, cosine, sine_term, gain, grads, inner, deps=()):
    shards_of, tokens, columns = raw.shape
    return pl.pallas_call(
        with_deps(rope_back_kernel, 7, deps),
        grid=(shards_of,),
        in_specs=rope_specs(raw, gain)
        + [
            pl.BlockSpec((2, 1, tokens, columns // 2), lambda k: (0, k, 0, 0)),
            pl.BlockSpec((1, 2, tokens), lambda k: (k, 0, 0)),
        ]
        + dep_specs(deps),
        out_specs=pl.BlockSpec((1, tokens, columns), lambda k: (k, 0, 0)),
        out_shape=jax.ShapeDtypeStruct((shards_of, tokens, columns), LOW),
        cost_estimate=scaled_cost(
            factor=4,
            flops=12 * raw.size, bytes_accessed=8 * raw.size, transcendentals=0
        ),
        compiler_params=kernel_params(),
        name="rope_back",
    )(raw, squares, cosine, sine_term, gain, grads, inner, *deps)


def qkv_back_kernel(grad, w_own, w_other, term):
    heads, half, columns = w_own.shape
    for part, weight in enumerate((w_own, w_other)):
        total = None
        for j in range(heads):
            value = dot_back(grad[:, j * columns : (j + 1) * columns], weight[j])
            total = value if total is None else total + value
        term[:, part * half : (part + 1) * half] = total.astype(LOW)


def qkv_backward(grad, w_own, w_other, deps=()):
    tokens, columns = grad.shape
    heads, half, _ = w_own.shape
    rows = min(tokens, 256)
    weight = pl.BlockSpec(w_own.shape, lambda i: (0, 0, 0))
    return pl.pallas_call(
        with_deps(qkv_back_kernel, 3, deps),
        grid=(tokens // rows,),
        in_specs=[pl.BlockSpec((rows, columns), lambda i: (i, 0)), weight, weight]
        + dep_specs(deps),
        out_specs=pl.BlockSpec((rows, 2 * half), lambda i: (i, 0)),
        out_shape=jax.ShapeDtypeStruct((tokens, 2 * half), LOW),
        cost_estimate=scaled_cost(
            factor=4,
            flops=4 * grad.size * half,
            bytes_accessed=4 * w_own.size + 2 * grad.size + 4 * tokens * half,
            transcendentals=0,
        ),
        compiler_params=kernel_params(),
        name="qkv_back",
    )(grad, w_own, w_other, *deps)


def swap(values, axis, step):
    count = lax.axis_size(axis)
    return lax.ppermute(values, axis, [(i, i ^ step) for i in range(count)])


def is_relative():
    return lax.axis_size("dp") == 4


def place_of(entry):
    if is_relative():
        return lax.axis_index("dp") ^ entry
    return entry


def gather_begin(values):
    if not is_relative():
        return ()
    return (swap(values, "dp", 1), swap(values, "dp", 2))


def gather_end(values, begun):
    if not is_relative():
        whole = lax.all_gather(values, "dp", axis=0)
        return [whole[k] for k in range(whole.shape[0])]
    first, second = begun
    half = first.shape[0] // 2
    third = jnp.concatenate([swap(second[:half], "dp", 1), swap(first[half:], "dp", 2)], axis=0)
    return [values, first, second, third]


def scatter_begin(parts):
    if not is_relative():
        return ()
    half = parts[0].shape[0] // 2
    _, first, second, third = parts
    return (
        swap(third[:half], "dp", 1),
        swap(third[half:], "dp", 2),
        swap(first[:half], "dp", 1),
        swap(second[half:], "dp", 2),
    )


def scatter_middle(parts, begun):
    if not is_relative():
        return ()
    half = parts[0].shape[0] // 2
    _, first, second, _ = parts
    low_third, high_third = begun[:2]
    return (
        swap((first[half:].astype(FULL) + high_third.astype(FULL)).astype(LOW), "dp", 1),
        swap((second[:half].astype(FULL) + low_third.astype(FULL)).astype(LOW), "dp", 2),
    )


def scatter_end(parts, begun, middle):
    if not is_relative():
        return lax.psum_scatter(jnp.stack(parts), "dp", scatter_dimension=0).astype(FULL)
    half = parts[0].shape[0] // 2
    own = parts[0].astype(FULL)
    first_low, second_high = begun[2:]
    first_high, second_low = middle
    return jnp.concatenate(
        [
            own[:half] + first_low.astype(FULL) + second_low.astype(FULL),
            own[half:] + first_high.astype(FULL) + second_high.astype(FULL),
        ],
        axis=0,
    )


def scatter_dp(parts):
    begun = scatter_begin(parts)
    return scatter_end(parts, begun, scatter_middle(parts, begun))


def trade_dp(parts):
    if not is_relative():
        traded = lax.all_to_all(jnp.stack(parts), "dp", 0, 0, tiled=True)
        return [traded[k] for k in range(traded.shape[0])]
    return [parts[0]] + [swap(parts[k], "dp", k) for k in range(1, 4)]


def exchange_dp(blocks):
    if not is_relative():
        return lax.all_to_all(blocks, "dp", 0, 0, tiled=True)
    me = lax.axis_index("dp")
    got = []
    for k in range(4):
        sent = lax.dynamic_index_in_dim(blocks, me ^ k, 0, keepdims=False)
        got.append(swap(sent, "dp", k) if k else sent)
    odd, far = me % 2 == 1, me >= 2
    first, second = jnp.where(odd, got[1], got[0]), jnp.where(odd, got[0], got[1])
    third, fourth = jnp.where(odd, got[3], got[2]), jnp.where(odd, got[2], got[3])
    return jnp.stack(
        [
            jnp.where(far, third, first),
            jnp.where(far, fourth, second),
            jnp.where(far, first, third),
            jnp.where(far, second, fourth),
        ]
    )


def exchange_row(blocks):
    other = 1 - lax.axis_index("row")
    sent = lax.dynamic_index_in_dim(blocks, other, 0, keepdims=True)
    return lax.dynamic_update_slice_in_dim(blocks, swap(sent, "row", 1), other, 0)


def sum_dp(values):
    if not is_relative():
        return lax.psum(values, "dp")
    one = swap(values, "dp", 1)
    values = values + jnp.stack([one[1], one[0], one[3], one[2]])
    two = swap(values, "dp", 2)
    return values + jnp.stack([two[2], two[3], two[0], two[1]])


def sum_all(values):
    for axis in ("row", "dp", "col"):
        step = 1
        while step < lax.axis_size(axis):
            values = values + swap(values, axis, step)
            step *= 2
    return values


def other_row(values):
    return swap(values, "row", 1)


def attend_kernel(starts, query, key, value, doc_key, doc_query, mixed, log_total):
    sequence = pl.program_id(0)
    parts, _, part, _ = query.shape
    length = parts * part
    nblock = starts.shape[1]
    block = length // nblock
    keys_in = key[...].reshape(length, HD)
    queries = query[...].reshape(length, HD)
    values_turned = value[...].reshape(length, HD).T
    scaling = HD ** (-0.5)
    for b in range(nblock):
        lo = b * block
        hi = lo + block
        scores = (
            lax.dot_general(
                keys_in[:hi],
                queries[lo:hi],
                (((1,), (1,)), ((), ())),
                preferred_element_type=FULL,
            )
            * scaling
        )
        place = lax.broadcasted_iota(jnp.int32, (hi, 1), 0)
        group = jnp.where(place >= starts[sequence, b] * block, doc_key[0, :hi, :], -1)
        scores = jnp.where(group == doc_query[0, :, lo:hi], scores, NEGATIVE)
        highest = jnp.max(scores, axis=0, keepdims=True)
        exponent = jnp.exp(scores - highest)
        total = jnp.sum(exponent, axis=0, keepdims=True)
        probability = (exponent * (1.0 / total)).astype(LOW)
        turned = jnp.dot(values_turned[:, :hi], probability, preferred_element_type=FULL)
        at = lo // part
        mixed[at, 0, lo - at * part : hi - at * part, :] = turned.T.astype(LOW)
        log_total[0, 0, :, lo:hi] = highest + jnp.log(total)


def attend_back_kernel(
    starts, query, key, value, grad_mixed, doc_key, doc_query, log_total, grads, grad_key, grad_value
):
    sequence = pl.program_id(0)
    head = pl.program_id(1)
    parts, _, part, _ = query.shape
    length = parts * part
    nblock = starts.shape[1]
    block = length // nblock
    keys_in = key[...].reshape(length, HD)
    queries = query[...].reshape(length, HD)
    values = value[...].reshape(length, HD)
    upstream = grad_mixed[...].reshape(length, HD)
    keys_turned = keys_in.T
    scaling = HD ** (-0.5)
    query_at = pl.ds(pl.multiple_of(3 * head * HD, HD), HD)
    for b in range(nblock - 1, -1, -1):
        lo = b * block
        hi = lo + block
        scores = (
            lax.dot_general(
                keys_in[:hi],
                queries[lo:hi],
                (((1,), (1,)), ((), ())),
                preferred_element_type=FULL,
            )
            * scaling
        )
        place = lax.broadcasted_iota(jnp.int32, (hi, 1), 0)
        group = jnp.where(place >= starts[sequence, b] * block, doc_key[0, :hi, :], -1)
        scores = jnp.where(group == doc_query[0, :, lo:hi], scores, NEGATIVE)
        probability = jnp.exp(scores - log_total[0, 0, :, lo:hi])
        term_value = jnp.dot(
            probability.astype(LOW), upstream[lo:hi], preferred_element_type=FULL
        )
        grad_prob = lax.dot_general(
            values[:hi], upstream[lo:hi], (((1,), (1,)), ((), ())), preferred_element_type=FULL
        )
        weighted = probability * grad_prob
        center = jnp.sum(weighted, axis=0, keepdims=True)
        grad_scores = (weighted - probability * center).astype(LOW)
        term_key = jnp.dot(grad_scores, queries[lo:hi], preferred_element_type=FULL)
        if b == nblock - 1:
            grad_value[...] = term_value
            grad_key[...] = term_key
        else:
            grad_value[:hi] += term_value
            grad_key[:hi] += term_key
        turned = jnp.dot(keys_turned[:, :hi], grad_scores, preferred_element_type=FULL) * scaling
        at = lo // part
        grads[at, 0, lo - at * part : hi - at * part, query_at] = turned.T.astype(LOW)
    key_at = pl.ds(pl.multiple_of((3 * head + 1) * HD, HD), HD)
    value_at = pl.ds(pl.multiple_of((3 * head + 2) * HD, HD), HD)
    grads[:, 0, :, key_at] = (grad_key[...] * scaling).astype(LOW).reshape(parts, part, HD)
    grads[:, 0, :, value_at] = grad_value[...].astype(LOW).reshape(parts, part, HD)


def attention_cost(packed, heads, products):
    parts, nseq, part, _ = packed.shape
    pairs = nseq * heads * (parts * part) ** 2 * 5 // 8
    return scaled_cost(
        factor=5, flops=2 * pairs * HD * products, bytes_accessed=2 * packed.size * 2, transcendentals=pairs
    )


def piece_spec(packed, stride, offset):
    parts, _, part, _ = packed.shape
    return pl.BlockSpec((parts, 1, part, HD), lambda s, h, *_: (0, s, 0, stride * h + offset))


def attend_forward(packed, starts, documents):
    parts, nseq, part, width = packed.shape
    heads = width // (3 * HD)
    length = parts * part
    return pl.pallas_call(
        attend_kernel,
        grid_spec=pltpu.PrefetchScalarGridSpec(
            num_scalar_prefetch=1,
            grid=(nseq, heads),
            in_specs=[
                piece_spec(packed, 3, 0),
                piece_spec(packed, 3, 1),
                piece_spec(packed, 3, 2),
                pl.BlockSpec((1, length, 1), lambda s, h, *_: (s, 0, 0)),
                pl.BlockSpec((1, 1, length), lambda s, h, *_: (s, 0, 0)),
            ],
            out_specs=[
                piece_spec(packed, 1, 0),
                pl.BlockSpec((1, 1, 1, length), lambda s, h, *_: (s, h, 0, 0)),
            ],
        ),
        out_shape=[
            jax.ShapeDtypeStruct((parts, nseq, part, heads * HD), LOW),
            jax.ShapeDtypeStruct((nseq, heads, 1, length), FULL),
        ],
        cost_estimate=attention_cost(packed, heads, 2),
        compiler_params=pltpu.CompilerParams(vmem_limit_bytes=48 * 1024 * 1024),
        name="attend",
    )(starts, packed, packed, packed, documents[:, :, None], documents[:, None, :])


def attend_backward(packed, starts, documents, log_total, grad_mixed, deps=()):
    parts, nseq, part, width = packed.shape
    heads = width // (3 * HD)
    length = parts * part
    return pl.pallas_call(
        with_deps(attend_back_kernel, 8, deps),
        grid_spec=pltpu.PrefetchScalarGridSpec(
            num_scalar_prefetch=1,
            grid=(nseq, heads),
            in_specs=[
                piece_spec(packed, 3, 0),
                piece_spec(packed, 3, 1),
                piece_spec(packed, 3, 2),
                piece_spec(packed, 1, 0),
                pl.BlockSpec((1, length, 1), lambda s, h, *_: (s, 0, 0)),
                pl.BlockSpec((1, 1, length), lambda s, h, *_: (s, 0, 0)),
                pl.BlockSpec((1, 1, 1, length), lambda s, h, *_: (s, h, 0, 0)),
            ]
            + dep_specs(deps),
            out_specs=pl.BlockSpec((parts, 1, part, width), lambda s, h, *_: (0, s, 0, 0)),
            scratch_shapes=[pltpu.VMEM((length, HD), FULL), pltpu.VMEM((length, HD), FULL)],
        ),
        out_shape=jax.ShapeDtypeStruct(packed.shape, LOW),
        cost_estimate=attention_cost(packed, heads, 5),
        compiler_params=pltpu.CompilerParams(vmem_limit_bytes=48 * 1024 * 1024),
        name="attend_back",
    )(
        starts,
        packed,
        packed,
        packed,
        grad_mixed,
        documents[:, :, None],
        documents[:, None, :],
        log_total,
        *deps,
    )


def angles(places):
    halfway = HD // 2
    frequency = ROPE_BASE ** (-jnp.arange(halfway, dtype=FULL) / halfway)
    turned = places.astype(FULL)[..., None] * jnp.concatenate([frequency, frequency])
    sign = jnp.where(jnp.arange(HD) < halfway, -1.0, 1.0)
    return (jnp.cos(turned), jnp.sin(turned) * sign)


def norm_back(upstream, normed, scaling, gain):
    scaled = upstream * gain
    inner = jnp.mean(normed * scaled, axis=1, keepdims=True)
    return (scaling * (scaled - normed * inner), jnp.sum(upstream * normed, axis=0))


def placed(shape, piece, starts):
    return lax.dynamic_update_slice(jnp.zeros(shape, FULL), piece, starts).reshape(-1)


def sequence_span(length, tokens):
    return max(1, length // tokens)


def regroup(values, span):
    if span == 1:
        return values
    n_dp, n_col = lax.axis_size("dp"), lax.axis_size("col")
    moves = []
    for i in range(n_dp):
        for j in range(n_col):
            to_i = i - i % span + j % span
            to_j = j - j % span + i % span
            moves.append((i * n_col + j, to_i * n_col + to_j))
    return lax.ppermute(values, ("dp", "col"), moves)


def heads_line_up():
    return H // lax.axis_size("col") == lax.axis_size("dp")


def fetch_qkv(low, deps):
    nb, inner, three, heads, _ = low.shape
    n_dp = lax.axis_size("dp")
    if not heads_line_up():
        whole = lax.all_gather(low, "dp", axis=1, tiled=True)
        whole = lax.all_gather(whole, "col", axis=3, tiled=True)
        mine = H // n_dp
        whole = lax.dynamic_slice_in_dim(whole, lax.axis_index("dp") * mine, mine, 3)
        return whole.transpose(3, 0, 1, 2, 4).reshape(mine, nb * HD, three * HD)
    sent = low.transpose(3, 0, 1, 2, 4).reshape(heads, nb * inner, three * HD)
    got = exchange_dp(after(sent, *deps)).reshape(n_dp, nb, inner, three * HD).transpose(1, 0, 2, 3)
    got = got.reshape(nb * HD, three * HD)
    return lax.all_gather(got, "col", axis=0)


def fetch_out(low):
    heads, inner, cols = low.shape
    if not heads_line_up():
        whole = lax.all_gather(low, "dp", axis=1, tiled=True)
        return lax.all_gather(whole, "col", axis=0, tiled=True).reshape(D, cols)
    got = exchange_dp(low).reshape(HD, cols)
    return lax.all_gather(got, "col", axis=0).reshape(heads * HD, cols)


def send_gate_up(weight):
    nb, inner, two, cols = weight.shape
    n_dp = lax.axis_size("dp")
    mine = cols // n_dp
    sent = weight.astype(LOW).reshape(nb, inner, two, n_dp, mine).transpose(3, 2, 0, 1, 4)
    return sent.reshape(n_dp, two * nb * inner, mine)


def fetch_gate_up(sent, shape):
    nb, inner, two, cols = shape
    n_dp = lax.axis_size("dp")
    mine = cols // n_dp
    got = exchange_dp(sent)
    got = got.reshape(n_dp, two, nb, inner, mine).transpose(1, 2, 0, 3, 4)
    got = got.reshape(two, nb * HD, mine)
    return (lax.all_gather(got, "col", axis=0), got)


def send_down(weight):
    blocks, inner, cols = weight.shape
    n_dp = lax.axis_size("dp")
    return weight.astype(LOW).reshape(n_dp, blocks // n_dp * inner, cols)


def fetch_down(sent, shape):
    blocks, inner, cols = shape
    n_dp, n_col = lax.axis_size("dp"), lax.axis_size("col")
    mine = blocks // n_dp
    got = exchange_dp(sent)
    got = got.reshape(n_dp, mine, inner, cols).transpose(1, 0, 2, 3).reshape(mine * HD, cols)
    return (lax.all_gather(got, "col", axis=0).reshape(n_col * mine * HD, cols), got)


def reduce_col(values):
    return lax.psum_scatter(values, "col", scatter_dimension=0)


def grad_for_other(left, rows, right, columns, steps, by_rows, deps=(), factor=2):
    places = (1, 0) if by_rows else (0, 1)
    return grad_block(left, places[0], rows, right, places[1], columns, steps, None, deps, factor)


def grad_for_own(left, rows, right, columns, steps, received, deps=(), factor=2):
    return grad_block(left, 0, rows, right, 0, columns, steps, received, deps, factor)


def in_turn(order, call, results, deps=()):
    for k in order:
        results[k] = call(k, deps)
        last = results[k]
        deps = (last[0] if isinstance(last, (list, tuple)) else last,)
    return deps


def settle_qkv(half, shape):
    nb, inner, three, heads, _ = shape
    n_dp = lax.axis_size("dp")
    mine = H // n_dp
    if not heads_line_up():
        half = half.reshape(mine, nb, HD, three, HD).transpose(1, 2, 3, 0, 4)
        whole = lax.dynamic_update_slice_in_dim(
            jnp.zeros((nb, HD, three, H, HD), LOW), half, lax.axis_index("dp") * mine, 3
        )
        whole = lax.psum_scatter(whole, "dp", scatter_dimension=1, tiled=True)
        return lax.psum_scatter(whole, "col", scatter_dimension=3, tiled=True).astype(FULL)
    summed = half
    sent = summed.reshape(nb, n_dp, inner, three * HD).transpose(1, 0, 2, 3)
    got = exchange_dp(sent.reshape(n_dp, nb * inner, three * HD))
    return got.reshape(n_dp, nb, inner, three, HD).transpose(1, 2, 3, 0, 4).astype(FULL)


def settle_out(half, shape):
    heads, inner, cols = shape
    if not heads_line_up():
        whole = half.reshape(H, HD, cols)
        whole = lax.psum_scatter(whole, "dp", scatter_dimension=1, tiled=True)
        return lax.psum_scatter(whole, "col", scatter_dimension=0, tiled=True).astype(FULL)
    return exchange_dp(half.reshape(lax.axis_size("dp"), inner, cols)).astype(FULL)


def send_gate_up_grad(summed, shape):
    nb, inner, two, cols = shape
    n_dp = lax.axis_size("dp")
    mine = cols // n_dp
    sent = summed.reshape(two, nb, n_dp, inner, mine).transpose(2, 0, 1, 3, 4)
    return sent.reshape(n_dp, two * nb * inner, mine)


def gate_up_grad(got, shape):
    nb, inner, two, cols = shape
    n_dp = lax.axis_size("dp")
    got = got.reshape(n_dp, two, nb, inner, cols // n_dp).transpose(2, 3, 1, 0, 4)
    return got.reshape(shape).astype(FULL)


def send_down_grad(summed, shape):
    blocks, inner, cols = shape
    n_dp = lax.axis_size("dp")
    mine = blocks // n_dp
    sent = summed.reshape(mine, n_dp, inner, cols).transpose(1, 0, 2, 3)
    return sent.reshape(n_dp, mine * inner, cols)


DECAY = 1.0 - STEP ** (-0.8)


def square_sums(matrices, also=None):
    partials = []
    for grad, _, _, _, row_shape, col_shape, row_at, col_at, _ in matrices:
        squares = grad * grad
        partials.append(
            placed(row_shape, jnp.sum(squares, axis=tuple(range(2, grad.ndim))), row_at)
        )
        partials.append(placed(col_shape, jnp.sum(squares, axis=(0, 1)), col_at))
    if also is not None:
        partials.append(also.reshape(-1))
    return jnp.concatenate(partials)


def scaled_updates(matrices, sums):
    updates, rows, cols, sizes = [], [], [], []
    at = 0
    for grad, _, old_row, old_col, row_shape, col_shape, row_at, col_at, _ in matrices:
        row_count, col_count = old_row.shape[0], old_col.shape[0]
        row_means = sums[at : at + row_count] / col_count + TINY_SQUARE
        at += row_count
        col_means = sums[at : at + col_count] / row_count + TINY_SQUARE
        at += col_count
        new_row = DECAY * old_row + (1.0 - DECAY) * row_means
        new_col = DECAY * old_col + (1.0 - DECAY) * col_means
        row_here = lax.dynamic_slice(new_row.reshape(row_shape), row_at, grad.shape[:2])
        col_here = lax.dynamic_slice(new_col.reshape(col_shape), col_at, grad.shape[2:])
        row_here = row_here.reshape(grad.shape[:2] + (1,) * (grad.ndim - 2))
        update = grad * lax.rsqrt(row_here * col_here[None, None] / jnp.mean(new_row))
        updates.append(update)
        rows.append(new_row)
        cols.append(new_col)
        sizes.append(jnp.sum(update * update))
    return (updates, rows, cols, jnp.stack(sizes))


def renew(matrices, updates, rows, cols, sizes):
    renewed = []
    for n, matrix in enumerate(matrices):
        mean_size = sizes[n] / (rows[n].shape[0] * cols[n].shape[0])
        clip = jnp.maximum(1.0, jnp.sqrt(mean_size) / CLIP_LEVEL)
        renewed.append(matrix[1] - matrix[-1] * updates[n] / clip)
    return renewed


def shards(
    inputs,
    cotangent,
    w_qkv,
    w_out,
    w_gate_up,
    w_down,
    gains,
    gain_state,
    row_state,
    col_state,
    positions,
    block_map,
):
    row_pos = lax.axis_index("row")
    col_pos = lax.axis_index("col")
    data_pos = lax.axis_index("dp")
    n_dp, n_col = lax.axis_size("dp"), lax.axis_size("col")
    length = positions.shape[1]
    chip_tokens = inputs.shape[0]
    tokens = chip_tokens // 2
    width = inputs.shape[1]
    span = sequence_span(length, chip_tokens)
    heads_here = H // n_dp
    local = heads_here * HD

    def enter(values):
        values = regroup(values, span)
        kept = lax.dynamic_slice_in_dim(values, row_pos * tokens, tokens, 0)
        sent = lax.dynamic_slice_in_dim(values, (1 - row_pos) * tokens, tokens, 0)
        return jnp.concatenate([kept, swap(sent, "row", 1)], axis=1)

    def leave(values):
        got = swap(values[:, width:], "row", 1)
        result = jnp.zeros((chip_tokens, width), values.dtype)
        result = lax.dynamic_update_slice_in_dim(result, values[:, :width], row_pos * tokens, 0)
        result = lax.dynamic_update_slice_in_dim(result, got, (1 - row_pos) * tokens, 0)
        return regroup(result, span)

    def own_first(vector):
        parts = vector.reshape(2, width)
        return jnp.concatenate(
            [
                lax.dynamic_index_in_dim(parts, row_pos, 0, keepdims=False),
                lax.dynamic_index_in_dim(parts, 1 - row_pos, 0, keepdims=False),
            ]
        )

    x_own = enter(inputs)
    qkv_own = fetch_qkv(w_qkv.astype(LOW), (x_own,))
    out_rows = fetch_out(w_out.astype(LOW))
    gu_sent = send_gate_up(w_gate_up)
    down_sent = send_down(w_down)
    begun = gather_begin(x_own)
    begun = tuple(after(share, gu_sent, down_sent) for share in begun)
    every_place = after(jnp.concatenate([positions, block_map], axis=1), *begun)
    if is_relative() and span == 1:
        twin = other_row(every_place)
        first = row_pos == 0
        every_place = jnp.concatenate(
            [jnp.where(first, every_place, twin), jnp.where(first, twin, every_place)]
        )
        every_place = lax.dynamic_slice_in_dim(every_place, col_pos, 1, 0)
        here = jnp.concatenate(trade_dp([every_place] * n_dp))
        sequences = n_dp
    else:
        every_place = lax.all_gather(every_place, ("dp", "row"), axis=0, tiled=True)
        sequences = n_dp // span
        numbers = []
        for k in range(sequences):
            first = place_of(k) if span == 1 else k * span + col_pos % span
            numbers.append(first * (n_col // span) + col_pos // span)
        here = jnp.concatenate(
            [lax.dynamic_slice_in_dim(every_place, number, 1, 0) for number in numbers]
        )
    places = here[:, :length]
    starts = here[:, length:]
    documents = jnp.cumsum((places == 0).astype(jnp.int32), axis=1)
    x_parts = gather_end(x_own, begun)
    qkv_own = after(qkv_own, *begun)
    qkv_other = other_row(qkv_own)
    x_all = jnp.stack(x_parts)
    gu_own, gu_got = fetch_gate_up(after(gu_sent, x_all), w_gate_up.shape)
    down_own, down_got = fetch_down(after(down_sent, x_all), w_down.shape)
    grad_result = enter(cotangent).astype(FULL)

    token_places = lax.dynamic_index_in_dim(
        places.reshape(n_dp, 2, tokens), row_pos, 1, keepdims=False
    )
    cosine, sine_term = angles(token_places)

    if heads_line_up():
        gain_here = lax.dynamic_index_in_dim(
            gains[:2].reshape(2, n_col, n_dp, HD), data_pos, 2, keepdims=False
        ).reshape(2, local)
    else:
        gain_here = lax.dynamic_slice_in_dim(gains[:2], data_pos * local, local, 1)

    raw, squares = qkv_forward(x_all, qkv_own, qkv_other)
    squares = sum_dp(squares)
    turn = (raw, squares, cosine, sine_term, gain_here)
    out_begun = ()
    if heads_line_up():
        out_begun = gather_begin(after(out_rows, gu_got, down_got))
    packed = rope_forward(*turn, (gu_got, down_got))

    def by_sequence(values):
        if span == 1:
            return values
        last = values.shape[-1]
        values = values.reshape(2, sequences, span, tokens, last).transpose(1, 2, 0, 3, 4)
        return values.reshape(1, sequences, length, last)

    def by_shard(values):
        if span == 1:
            return values
        last = values.shape[-1]
        values = values.reshape(sequences, span, 2, tokens, last).transpose(2, 0, 1, 3, 4)
        return values.reshape(2, n_dp, tokens, last)

    packed = by_sequence(exchange_row(packed))
    out_own = out_rows
    mixed, log_total = attend_forward(packed, starts, documents)
    if heads_line_up():
        out_begun = tuple(after(share, log_total) for share in out_begun)
        out_own = jnp.concatenate(gather_end(out_rows, out_begun), axis=0)
    out_other = other_row(out_own)
    mixed = exchange_row(by_shard(mixed))
    mixed = trade_dp([mixed[:, k] for k in range(n_dp)])
    attended = jnp.concatenate([piece[core] for piece in mixed for core in range(2)], axis=1)

    attn = down_forward(attended, out_own, out_other, FULL)
    gain_attn = own_first(gains[2])[None, :]
    gain_mlp = own_first(gains[3])[None, :]
    attn_scale = lax.rsqrt(jnp.mean(attn * attn, axis=1, keepdims=True) + EPSILON)
    attn_hat = attn * attn_scale
    hidden_in = x_own.astype(FULL) + attn_hat * gain_attn
    h_own = hidden_in.astype(LOW)
    begun = gather_begin(h_own)
    h_parts = gather_end(h_own, begun)
    gu_own = after(gu_own, *begun)
    gu_other = other_row(gu_own)
    by_arrival = list(range(n_dp))
    by_distance = [3, 1, 2, 0] if is_relative() else by_arrival
    gated = [None] * n_dp
    in_turn(
        by_arrival,
        lambda k, deps: gate_forward(
            h_parts[k], gu_own, gu_other, deps + ((h_parts[3],) if k == 2 else ())
        ),
        gated,
    )
    hiddens = [entry[0] for entry in gated]
    down_own = after(down_own, hiddens[2])
    down_other = other_row(down_own)
    terms = [None] * n_dp
    in_turn(
        by_distance,
        lambda k, deps: down_forward(hiddens[k], down_own, down_other, LOW, deps),
        terms,
    )
    mlp = scatter_dp(terms)
    mlp_scale = lax.rsqrt(jnp.mean(mlp * mlp, axis=1, keepdims=True) + EPSILON)
    mlp_hat = mlp * mlp_scale
    result = leave(hidden_in + mlp_hat * gain_mlp)

    grad_mlp, gain_mlp_grad = norm_back(grad_result, mlp_hat, mlp_scale, gain_mlp)
    m_own = grad_mlp.astype(LOW)
    weights = (gu_own, gu_other, down_own, down_other)
    backs = [None] * n_dp
    begun = gather_begin(m_own)
    if is_relative():
        m_parts = [m_own]
        last = in_turn(
            [0], lambda k, deps: mlp_backward(m_own, *gated[k][1:], *weights, deps), backs
        )
        begun = tuple(after(share, *last) for share in begun)
        rest = [1, 3, 2]
    else:
        last, rest = (), by_arrival
    m_parts = gather_end(m_own, begun)
    last = in_turn(
        rest,
        lambda k, deps: mlp_backward(m_parts[k], *gated[k][1:], *weights, deps),
        backs,
        last,
    )
    units = hiddens[0].shape[1]
    down_block = (hiddens, units, [m_parts], width, 1)
    gu_block = (
        h_parts,
        width,
        [[entry[0] for entry in backs], [entry[1] for entry in backs]],
        gu_own.shape[3],
        n_col,
    )
    terms = [entry[2] for entry in backs]
    begun = scatter_begin(terms)
    gu_rest = grad_for_other(*gu_block, True, last + begun[2:3])
    down_rest = grad_for_other(*down_block, False, (gu_rest,) + begun[:2])
    middle = scatter_middle(terms, begun)
    gu_half = grad_for_own(*gu_block, other_row(gu_rest), (down_rest,) + begun[3:])
    gu_sum = reduce_col(gu_half)
    terms[0] = after(terms[0], gu_half)
    grad_hidden_in = grad_result + scatter_end(terms, begun, middle)

    grad_attn, gain_attn_grad = norm_back(grad_hidden_in, attn_hat, attn_scale, gain_attn)
    grad_attn_low = grad_attn.astype(LOW)
    sent = attended_backward(grad_attn_low, out_own, out_other, n_dp, (gu_half,))
    down_half = grad_for_own(*down_block, other_row(down_rest), (sent[0],))
    down_sum = reduce_col(down_half.reshape(n_col, -1, width))
    out_block = ([attended], D, [[grad_attn_low]], width, 1)
    out_rest = grad_for_other(*out_block, False, (down_half,), 4)
    grad_mixed = by_sequence(exchange_row(jnp.stack(trade_dp(sent), axis=1)))
    grads = attend_backward(packed, starts, documents, log_total, grad_mixed, (out_rest,))
    out_half = grad_for_own(*out_block, other_row(out_rest), (grads,), 4)
    grads = exchange_row(by_shard(grads))
    inner, gain_pair = rope_inner(*turn, grads, (gu_sum,))
    gu_got = exchange_dp(send_gate_up_grad(gu_sum, w_gate_up.shape))
    out_begun = ()
    if heads_line_up():
        out_parts = out_half.reshape(n_dp, local, width)
        out_parts = [out_parts[k] for k in range(n_dp)]
        out_begun = scatter_begin(out_parts)
    qkv_low = rope_backward(*turn, grads, sum_dp(inner), out_begun)
    qkv_block = (
        [x_all.reshape(n_dp * tokens, D)],
        width,
        [[qkv_low.reshape(n_dp * tokens, 3 * local)]],
        3 * HD,
        heads_here,
    )
    out_middle = ()
    if heads_line_up():
        out_middle = scatter_middle(out_parts, out_begun)
    qkv_rest = grad_for_other(*qkv_block, True, (gu_got,) + out_middle, 4)
    if heads_line_up():
        out_half = scatter_end(out_parts, out_begun, out_middle).astype(LOW)
        out_half = reduce_col(out_half.reshape(n_col, HD, width))
    down_got = exchange_dp(send_down_grad(down_sum, w_down.shape))
    grad_gu = gate_up_grad(gu_got, w_gate_up.shape)
    grad_down = down_got.reshape(w_down.shape).astype(FULL)
    grad_out = settle_out(out_half, w_out.shape)
    terms = [None] * n_dp

    def back_term(k, deps):
        return qkv_backward(qkv_low[k], qkv_own, qkv_other, deps)

    last = in_turn(by_distance, back_term, terms, (qkv_rest,))
    begun = scatter_begin(terms)
    qkv_half = grad_for_own(
        *qkv_block, other_row(qkv_rest), last + begun, 4
    )
    middle = scatter_middle(terms, begun)
    if heads_line_up():
        qkv_sum = reduce_col(qkv_half[:, 0])
    else:
        qkv_sum = qkv_half
    grad_qkv = settle_qkv(qkv_sum, w_qkv.shape)
    grad_inputs = leave(grad_hidden_in + scatter_end(terms, begun, middle))

    if heads_line_up():
        gain_pair = placed(
            (2, n_col, n_dp, HD), gain_pair.reshape(2, n_col, 1, HD), (0, 0, data_pos, 0)
        )
    else:
        gain_pair = placed((2, D), gain_pair, (0, data_pos * local))
    gain_partial = jnp.concatenate(
        [
            gain_pair.reshape(2, D),
            own_first(gain_attn_grad)[None, :],
            own_first(gain_mlp_grad)[None, :],
        ]
    )

    nb_rows, inner_rows, _, heads_col, _ = grad_qkv.shape
    ff_blocks = grad_down.shape[0]
    ff_cols = grad_gu.shape[3]
    row_at = (row_pos * nb_rows, data_pos * inner_rows)
    early = [
        (
            grad_down,
            w_down,
            row_state[3 * D :],
            col_state[4 * D + 2 * FF :],
            (FF // HD, HD),
            (D,),
            (col_pos * ff_blocks, data_pos * inner_rows),
            (row_pos * width,),
            3.0 * FF ** (-0.5),
        ),
        (
            grad_gu,
            w_gate_up,
            row_state[2 * D : 3 * D],
            col_state[4 * D : 4 * D + 2 * FF],
            (D // HD, HD),
            (2, FF),
            row_at,
            (0, col_pos * ff_cols),
            3.0 * D ** (-0.5),
        ),
        (
            grad_out,
            w_out,
            row_state[D : 2 * D],
            col_state[3 * D : 4 * D],
            (H, HD),
            (D,),
            (col_pos * heads_col, data_pos * inner_rows),
            (row_pos * width,),
            3.0 * D ** (-0.5),
        ),
    ]
    early_updates, early_rows, early_cols, early_sizes = scaled_updates(
        early, sum_all(after(square_sums(early), qkv_half))
    )
    row_down, row_gu, row_out = early_rows
    col_down, col_gu, col_out = early_cols
    late = [
        (
            grad_qkv,
            w_qkv,
            row_state[:D],
            col_state[: 3 * D],
            (D // HD, HD),
            (3, H, HD),
            row_at,
            (0, col_pos * heads_col, 0),
            3.0 * D ** (-0.5),
        )
    ]
    sums = sum_all(square_sums(late, gain_partial))
    gain_grad = sums[-gain_partial.size :].reshape(gain_partial.shape)
    late_updates, late_rows, late_cols, late_sizes = scaled_updates(late, sums)
    new_down, new_gu, new_out, new_qkv = renew(
        early + late,
        early_updates + late_updates,
        early_rows + late_rows,
        early_cols + late_cols,
        sum_all(jnp.concatenate([early_sizes, late_sizes])),
    )
    (row_qkv,), (col_qkv,) = late_rows, late_cols
    gain_new_state = DECAY * gain_state + (1.0 - DECAY) * (gain_grad * gain_grad + TINY_SQUARE)
    gain_update = gain_grad * lax.rsqrt(gain_new_state)
    gain_update = gain_update / jnp.maximum(
        1.0, jnp.sqrt(jnp.mean(gain_update * gain_update, axis=1, keepdims=True)) / CLIP_LEVEL
    )
    new_gains = gains - GAIN_RATE * gain_update
    return (
        result,
        grad_inputs,
        grad_qkv,
        grad_out,
        grad_gu,
        grad_down,
        new_qkv,
        new_out,
        new_gu,
        new_down,
        new_qkv.astype(LOW),
        new_out.astype(LOW),
        new_gu.astype(LOW),
        new_down.astype(LOW),
        jnp.concatenate([row_qkv, row_out, row_gu, row_down]),
        jnp.concatenate([col_qkv, col_out, col_gu, col_down]),
        gain_grad,
        gain_new_state,
        new_gains,
    )


def solution(mesh):
    return jax.shard_map(
        shards,
        mesh=mesh,
        in_specs=(
            P(("dp", "col"), "row"),
            P(("dp", "col"), "row"),
            P("row", "dp", None, "col", None),
            P("col", "dp", "row"),
            P("row", "dp", None, "col"),
            P("col", "dp", "row"),
            P(),
            P(),
            P(),
            P(),
            P(("dp", "row"), None),
            P(("dp", "row"), None),
        ),
        out_specs=(
            P(("dp", "col"), "row"),
            P(("dp", "col"), "row"),
            P("row", "dp", None, "col", None),
            P("col", "dp", "row"),
            P("row", "dp", None, "col"),
            P("col", "dp", "row"),
            P("row", "dp", None, "col", None),
            P("col", "dp", "row"),
            P("row", "dp", None, "col"),
            P("col", "dp", "row"),
            P("row", "dp", None, "col", None),
            P("col", "dp", "row"),
            P("row", "dp", None, "col"),
            P("col", "dp", "row"),
            P(),
            P(),
            P(),
            P(),
            P(),
        ),
        check_vma=False,
    )
```

```python
import functools

import jax
import jax.numpy as jnp
from jax import lax
from jax.experimental import pallas as pl
from jax.experimental.pallas import tpu as pltpu
from jax.sharding import PartitionSpec as P

D = 2048
H = 16
HD = 128
FF = 8192
STEP = 3


EPSILON = 1e-06
TINY_SQUARE = 1e-30
ROPE_BASE = 500000.0
NEGATIVE = -1e30
CLIP_LEVEL = 0.5
GAIN_RATE = 0.3

LOW = jnp.bfloat16
FULL = jnp.float32


VMEM_LIMIT = 56 * 1024 * 1024


def dot(left, right):
    return jnp.dot(left, right, preferred_element_type=FULL)


def dot_back(left, right):
    return lax.dot_general(left, right, (((1,), (1,)), ((), ())), preferred_element_type=FULL)


def scaled_cost(flops, bytes_accessed, transcendentals, factor=2):
    return pl.CostEstimate(
        flops=factor * flops,
        bytes_accessed=factor * bytes_accessed,
        transcendentals=factor * transcendentals,
    )


def with_deps(kernel, count, deps):
    def body(*refs):
        return kernel(*refs[:count], *refs[count + len(deps) :])

    return body


def dep_specs(deps):
    return [pl.BlockSpec(memory_space=pl.ANY)] * len(deps)


def after(value, *others):
    if not others:
        return value

    def body(*refs):
        pass

    return pl.pallas_call(
        body,
        in_specs=dep_specs((value,) + others),
        out_specs=pl.BlockSpec(memory_space=pl.ANY),
        out_shape=jax.ShapeDtypeStruct(value.shape, value.dtype),
        input_output_aliases={0: 0},
        name="after",
    )(value, *others)


def kernel_params():
    return pltpu.CompilerParams(vmem_limit_bytes=VMEM_LIMIT)


def gate_kernel(h, gu_own, gu_other, hidden, by_gate, by_up):
    half = gu_own.shape[2]
    left = h[:, :half]
    right = h[:, half:]
    gate = dot(left, gu_own[0, 0]) + dot(right, gu_other[0, 0])
    up = dot(left, gu_own[0, 1]) + dot(right, gu_other[0, 1])
    sigmoid_gate = 1.0 / (1.0 + jnp.exp(-gate))
    silu = gate * sigmoid_gate
    hidden[...] = (silu * up).astype(LOW)
    by_gate[...] = (up * sigmoid_gate * (1.0 + gate * (1.0 - sigmoid_gate))).astype(LOW)
    by_up[...] = silu.astype(LOW)


def gate_forward(h, gu_own, gu_other, deps=()):
    tokens, width = h.shape
    n_col, _, half, mine = gu_own.shape
    weight = pl.BlockSpec((1, 2, half, mine), lambda j: (j, 0, 0, 0))
    piece = pl.BlockSpec((tokens, mine), lambda j: (0, j))
    shape = jax.ShapeDtypeStruct((tokens, n_col * mine), LOW)
    return pl.pallas_call(
        with_deps(gate_kernel, 3, deps),
        grid=(n_col,),
        in_specs=[pl.BlockSpec((tokens, width), lambda j: (0, 0)), weight, weight]
        + dep_specs(deps),
        out_specs=[piece, piece, piece],
        out_shape=[shape, shape, shape],
        cost_estimate=scaled_cost(
            flops=4 * tokens * width * n_col * mine,
            bytes_accessed=4 * gu_own.size + 2 * h.size + 6 * tokens * n_col * mine,
            transcendentals=tokens * n_col * mine,
        ),
        compiler_params=kernel_params(),
        name="gate_up",
    )(h, gu_own, gu_other, *deps)


def down_kernel(hidden, down_own, down_other, term):
    half = down_own.shape[1]
    term[:, :half] = dot(hidden[...], down_own[...]).astype(term.dtype)
    term[:, half:] = dot(hidden[...], down_other[...]).astype(term.dtype)


def down_forward(hidden, down_own, down_other, kind=LOW, deps=()):
    tokens, units = hidden.shape
    half = down_own.shape[1]
    rows = min(tokens, 256)
    weight = pl.BlockSpec((units, half), lambda i: (0, 0))
    return pl.pallas_call(
        with_deps(down_kernel, 3, deps),
        grid=(tokens // rows,),
        in_specs=[pl.BlockSpec((rows, units), lambda i: (i, 0)), weight, weight]
        + dep_specs(deps),
        out_specs=pl.BlockSpec((rows, 2 * half), lambda i: (i, 0)),
        out_shape=jax.ShapeDtypeStruct((tokens, 2 * half), kind),
        cost_estimate=scaled_cost(
            flops=4 * tokens * units * half,
            bytes_accessed=4 * down_own.size + 2 * hidden.size + 4 * tokens * half,
            transcendentals=0,
        ),
        compiler_params=kernel_params(),
        name="down",
    )(hidden, down_own, down_other, *deps)


def attended_back_kernel(grad, out_own, out_other, *results):
    half = out_own.shape[1]
    value = dot_back(grad[:, :half], out_own[...]) + dot_back(grad[:, half:], out_other[...])
    for k in range(len(results)):

        @pl.when(pl.program_id(0) == k)
        def _(k=k):
            results[k][0] = value.astype(LOW)


def attended_backward(grad, out_own, out_other, n_dp, deps):
    tokens, width = grad.shape
    rows, half = out_own.shape
    columns = rows // n_dp // 2
    weight = pl.BlockSpec((columns, half), lambda k, c: (2 * k + c, 0))

    def result_spec(i):
        return pl.BlockSpec(
            (1, tokens, columns), lambda k, c: (jnp.clip(2 * (k - i) + c, 0, 1), 0, 0)
        )

    return pl.pallas_call(
        with_deps(attended_back_kernel, 3, deps),
        grid=(n_dp, 2),
        in_specs=[pl.BlockSpec((tokens, width), lambda k, c: (0, 0)), weight, weight]
        + dep_specs(deps),
        out_specs=[result_spec(i) for i in range(n_dp)],
        out_shape=[jax.ShapeDtypeStruct((2, tokens, columns), LOW)] * n_dp,
        cost_estimate=scaled_cost(
            factor=3,
            flops=2 * grad.size * rows,
            bytes_accessed=4 * out_own.size + 2 * grad.size + 2 * tokens * rows,
            transcendentals=0,
        ),
        compiler_params=kernel_params(),
        name="attended_back",
    )(grad, out_own, out_other, *deps)


def mlp_back_kernel(
    m, by_gate, by_up, gu_own, gu_other, down_own, down_other, grad_gate, grad_up, term, total
):
    j = pl.program_id(0)
    half = gu_own.shape[2]
    grad_hidden = dot_back(m[:, :half], down_own[0]) + dot_back(m[:, half:], down_other[0])
    low_gate = (grad_hidden * by_gate[...].astype(FULL)).astype(LOW)
    low_up = (grad_hidden * by_up[...].astype(FULL)).astype(LOW)
    grad_gate[...] = low_gate
    grad_up[...] = low_up
    own = dot_back(low_gate, gu_own[0, 0]) + dot_back(low_up, gu_own[0, 1])
    other = dot_back(low_gate, gu_other[0, 0]) + dot_back(low_up, gu_other[0, 1])

    @pl.when(j == 0)
    def _():
        total[:, :half] = own
        total[:, half:] = other

    @pl.when(j > 0)
    def _():
        total[:, :half] += own
        total[:, half:] += other

    @pl.when(j == pl.num_programs(0) - 1)
    def _():
        term[...] = total[...].astype(LOW)


def mlp_backward(m, by_gate, by_up, gu_own, gu_other, down_own, down_other, deps=()):
    tokens, width = m.shape
    n_col, _, half, mine = gu_own.shape
    weight = pl.BlockSpec((1, 2, half, mine), lambda j: (j, 0, 0, 0))
    weight_down = pl.BlockSpec((1, mine, half), lambda j: (j, 0, 0))
    piece = pl.BlockSpec((tokens, mine), lambda j: (0, j))
    whole = pl.BlockSpec((tokens, width), lambda j: (0, 0))
    shape = jax.ShapeDtypeStruct((tokens, n_col * mine), LOW)
    return pl.pallas_call(
        with_deps(mlp_back_kernel, 7, deps),
        grid=(n_col,),
        in_specs=[whole, piece, piece, weight, weight, weight_down, weight_down]
        + dep_specs(deps),
        out_specs=[piece, piece, whole],
        out_shape=[shape, shape, jax.ShapeDtypeStruct((tokens, width), LOW)],
        scratch_shapes=[pltpu.VMEM((tokens, width), FULL)],
        cost_estimate=scaled_cost(
            flops=6 * tokens * width * n_col * mine,
            bytes_accessed=6 * gu_own.size + 4 * m.size + 8 * tokens * n_col * mine,
            transcendentals=0,
        ),
        compiler_params=kernel_params(),
        name="mlp_back",
    )(
        m,
        by_gate,
        by_up,
        gu_own,
        gu_other,
        down_own.reshape(n_col, mine, half),
        down_other.reshape(n_col, mine, half),
        *deps,
    )


def grad_kernel(count, groups, received, pieces, *refs):
    left = refs[:count]
    right = refs[count : count + count * groups]
    others = refs[count + count * groups : count + count * groups + received]
    results, turned = refs[-1 - pieces : -1], refs[-1]
    part = left[0].shape[0]
    step = pl.program_id(1)

    @pl.when(step == 0)
    def _():
        for k in range(count):
            turned[:, k * part : (k + 1) * part] = left[k][...].T

    for g in range(groups):
        total = None
        for k in range(count):
            term = dot(turned[:, k * part : (k + 1) * part], right[g * count + k][...])
            total = term if total is None else total + term
        if not received and pieces == 1:
            results[0][0, g] = total.astype(LOW)
        for n in range(max(received, pieces) if received or pieces > 1 else 0):

            @pl.when(step == n)
            def _(n=n):
                value = total + others[n][0, g].astype(FULL) if received else total
                results[n if pieces > 1 else 0][0, g] = value.astype(LOW)


def grad_block(
    left, left_at, rows, right, right_at, columns, steps, received, deps=(), factor=2, split=False
):
    count, groups = len(left), len(right)
    part = left[0].shape[0]
    tile = min(rows, 512)
    tiles = rows // tile
    left_spec = pl.BlockSpec((part, tile), lambda a, j: (0, left_at * tiles + a))
    right_spec = pl.BlockSpec((part, columns), lambda a, j: (0, right_at + j))
    share_spec = pl.BlockSpec((1, groups, tile, columns), lambda a, j: (0, 0, a, 0))
    result_spec = pl.BlockSpec((1, groups, tile, columns), lambda a, j: (j, 0, a, 0))
    operands = list(left) + [piece for group in right for piece in group] + list(received)
    specs = [left_spec] * count + [right_spec] * (count * groups) + [share_spec] * len(received)
    reads = len(operands)
    size = steps * groups * rows * columns
    pieces = steps if split else 1
    results = pl.pallas_call(
        with_deps(
            functools.partial(grad_kernel, count, groups, len(received), pieces), reads, deps
        ),
        grid=(tiles, steps),
        in_specs=specs + dep_specs(deps),
        out_specs=[share_spec if split else result_spec] * pieces,
        out_shape=[jax.ShapeDtypeStruct((steps // pieces, groups, rows, columns), LOW)] * pieces,
        scratch_shapes=[pltpu.VMEM((tile, count * part), LOW)],
        cost_estimate=scaled_cost(
            factor=factor,
            flops=2 * size * count * part,
            bytes_accessed=4 * size + 2 * count * part * (rows + steps * groups * columns * tiles),
            transcendentals=0,
        ),
        compiler_params=kernel_params(),
        name="weight_grad",
    )(*operands, *deps)
    return results if split else results[0]


def qkv_kernel(x, w_own, w_other, raw, squares, query_sum, key_sum):
    j = pl.program_id(1)
    half = w_own.shape[1]
    got = dot(x[0, :, :half], w_own[0]) + dot(x[0, :, half:], w_other[0])
    raw[0] = got
    query = got[:, :HD]
    key = got[:, HD : 2 * HD]

    @pl.when(j == 0)
    def _():
        query_sum[...] = query * query
        key_sum[...] = key * key

    @pl.when(j > 0)
    def _():
        query_sum[...] += query * query
        key_sum[...] += key * key

    @pl.when(j == pl.num_programs(1) - 1)
    def _():
        squares[0, 0:1] = jnp.sum(query_sum[...].T, axis=0, keepdims=True)
        squares[0, 1:2] = jnp.sum(key_sum[...].T, axis=0, keepdims=True)


def qkv_forward(x, w_own, w_other):
    shards_of, tokens, width = x.shape
    heads, half, columns = w_own.shape
    weight = pl.BlockSpec((1, half, columns), lambda k, j: (j, 0, 0))
    return pl.pallas_call(
        qkv_kernel,
        grid=(shards_of, heads),
        in_specs=[pl.BlockSpec((1, tokens, width), lambda k, j: (k, 0, 0)), weight, weight],
        out_specs=[
            pl.BlockSpec((1, tokens, columns), lambda k, j: (k, 0, j)),
            pl.BlockSpec((1, 2, tokens), lambda k, j: (k, 0, 0)),
        ],
        out_shape=[
            jax.ShapeDtypeStruct((shards_of, tokens, heads * columns), FULL),
            jax.ShapeDtypeStruct((shards_of, 2, tokens), FULL),
        ],
        scratch_shapes=[pltpu.VMEM((tokens, HD), FULL), pltpu.VMEM((tokens, HD), FULL)],
        cost_estimate=scaled_cost(
            flops=2 * x.size * heads * columns,
            bytes_accessed=2 * x.size + 4 * shards_of * w_own.size + 4 * shards_of * tokens * heads * columns,
            transcendentals=0,
        ),
        compiler_params=kernel_params(),
        name="qkv",
    )(x, w_own, w_other)


def token_scales(squares):
    return lax.rsqrt(squares[0] / D + EPSILON).T


def rope_kernel(raw, squares, cosine, sine_term, gain, packed):
    heads = gain.shape[1] // HD
    scales = token_scales(squares)
    for h in range(heads):
        core, at = h // (heads // 2), h % (heads // 2) * 3 * HD
        for n in range(2):
            value = raw[0, :, (3 * h + n) * HD : (3 * h + n + 1) * HD] * scales[:, n : n + 1]
            value = value * gain[n : n + 1, h * HD : (h + 1) * HD]
            turned = value * cosine[0] + pltpu.roll(value, HD // 2, 1) * sine_term[0]
            packed[core, 0, :, at + n * HD : at + (n + 1) * HD] = turned.astype(LOW)
        packed[core, 0, :, at + 2 * HD : at + 3 * HD] = raw[
            0, :, (3 * h + 2) * HD : (3 * h + 3) * HD
        ].astype(LOW)


def rope_specs(raw, gain):
    shards_of, tokens, columns = raw.shape
    return [
        pl.BlockSpec((1, tokens, columns), lambda k: (k, 0, 0)),
        pl.BlockSpec((1, 2, tokens), lambda k: (k, 0, 0)),
        pl.BlockSpec((1, tokens, HD), lambda k: (k, 0, 0)),
        pl.BlockSpec((1, tokens, HD), lambda k: (k, 0, 0)),
        pl.BlockSpec(gain.shape, lambda k: (0, 0)),
    ]


def rope_forward(raw, squares, cosine, sine_term, gain, deps=()):
    shards_of, tokens, columns = raw.shape
    return pl.pallas_call(
        with_deps(rope_kernel, 5, deps),
        grid=(shards_of,),
        in_specs=rope_specs(raw, gain) + dep_specs(deps),
        out_specs=pl.BlockSpec((2, 1, tokens, columns // 2), lambda k: (0, k, 0, 0)),
        out_shape=jax.ShapeDtypeStruct((2, shards_of, tokens, columns // 2), LOW),
        cost_estimate=scaled_cost(
            flops=8 * raw.size, bytes_accessed=6 * raw.size, transcendentals=0
        ),
        compiler_params=kernel_params(),
        name="rope",
    )(raw, squares, cosine, sine_term, gain, *deps)


def turned_back(grads, raw, cosine, sine_term, gain, scales, h, n):
    heads = gain.shape[1] // HD
    core, at = h // (heads // 2), (h % (heads // 2) * 3 + n) * HD
    value = grads[core, 0, :, at : at + HD].astype(FULL)
    value = value * cosine[0] - pltpu.roll(value, HD // 2, 1) * sine_term[0]
    normed = raw[0, :, (3 * h + n) * HD : (3 * h + n + 1) * HD] * scales[:, n : n + 1]
    return (value, normed, value * gain[n : n + 1, h * HD : (h + 1) * HD])


def rope_inner_kernel(raw, squares, cosine, sine_term, gain, grads, inner, gain_grad):
    heads = gain.shape[1] // HD
    scales = token_scales(squares)

    @pl.when(pl.program_id(0) == 0)
    def _():
        gain_grad[...] = jnp.zeros(gain_grad.shape, FULL)

    for n in range(2):
        total = None
        for h in range(heads):
            value, normed, scaled = turned_back(
                grads, raw, cosine, sine_term, gain, scales, h, n
            )
            term = normed * scaled
            total = term if total is None else total + term
            gain_grad[n : n + 1, h * HD : (h + 1) * HD] += jnp.sum(
                value * normed, axis=0, keepdims=True
            )
        inner[0, n : n + 1] = jnp.sum(total.T, axis=0, keepdims=True)


def rope_inner(raw, squares, cosine, sine_term, gain, grads, deps=()):
    shards_of, tokens, columns = raw.shape
    return pl.pallas_call(
        with_deps(rope_inner_kernel, 6, deps),
        grid=(shards_of,),
        in_specs=rope_specs(raw, gain)
        + [pl.BlockSpec((2, 1, tokens, columns // 2), lambda k: (0, k, 0, 0))]
        + dep_specs(deps),
        out_specs=[
            pl.BlockSpec((1, 2, tokens), lambda k: (k, 0, 0)),
            pl.BlockSpec(gain.shape, lambda k: (0, 0)),
        ],
        out_shape=[
            jax.ShapeDtypeStruct((shards_of, 2, tokens), FULL),
            jax.ShapeDtypeStruct(gain.shape, FULL),
        ],
        cost_estimate=scaled_cost(
            factor=4,
            flops=12 * raw.size, bytes_accessed=6 * raw.size, transcendentals=0
        ),
        compiler_params=kernel_params(),
        name="rope_inner",
    )(raw, squares, cosine, sine_term, gain, grads, *deps)


def rope_back_kernel(raw, squares, cosine, sine_term, gain, grads, inner, result):
    heads = gain.shape[1] // HD
    scales = token_scales(squares)
    means = (inner[0] / D).T
    for h in range(heads):
        for n in range(2):
            _, normed, scaled = turned_back(grads, raw, cosine, sine_term, gain, scales, h, n)
            value = scales[:, n : n + 1] * (scaled - normed * means[:, n : n + 1])
            result[0, :, (3 * h + n) * HD : (3 * h + n + 1) * HD] = value.astype(LOW)
        core, at = h // (heads // 2), (h % (heads // 2) * 3 + 2) * HD
        result[0, :, (3 * h + 2) * HD : (3 * h + 3) * HD] = grads[core, 0, :, at : at + HD]


def rope_backward(raw, squares, cosine, sine_term, gain, grads, inner, deps=()):
    shards_of, tokens, columns = raw.shape
    return pl.pallas_call(
        with_deps(rope_back_kernel, 7, deps),
        grid=(shards_of,),
        in_specs=rope_specs(raw, gain)
        + [
            pl.BlockSpec((2, 1, tokens, columns // 2), lambda k: (0, k, 0, 0)),
            pl.BlockSpec((1, 2, tokens), lambda k: (k, 0, 0)),
        ]
        + dep_specs(deps),
        out_specs=pl.BlockSpec((1, tokens, columns), lambda k: (k, 0, 0)),
        out_shape=jax.ShapeDtypeStruct((shards_of, tokens, columns), LOW),
        cost_estimate=scaled_cost(
            factor=4,
            flops=12 * raw.size, bytes_accessed=8 * raw.size, transcendentals=0
        ),
        compiler_params=kernel_params(),
        name="rope_back",
    )(raw, squares, cosine, sine_term, gain, grads, inner, *deps)


def qkv_back_kernel(grad, w_own, w_other, term):
    heads, half, columns = w_own.shape
    for part, weight in enumerate((w_own, w_other)):
        total = None
        for j in range(heads):
            value = dot_back(grad[:, j * columns : (j + 1) * columns], weight[j])
            total = value if total is None else total + value
        term[:, part * half : (part + 1) * half] = total.astype(LOW)


def qkv_backward(grad, w_own, w_other, deps=()):
    tokens, columns = grad.shape
    heads, half, _ = w_own.shape
    rows = min(tokens, 256)
    weight = pl.BlockSpec(w_own.shape, lambda i: (0, 0, 0))
    return pl.pallas_call(
        with_deps(qkv_back_kernel, 3, deps),
        grid=(tokens // rows,),
        in_specs=[pl.BlockSpec((rows, columns), lambda i: (i, 0)), weight, weight]
        + dep_specs(deps),
        out_specs=pl.BlockSpec((rows, 2 * half), lambda i: (i, 0)),
        out_shape=jax.ShapeDtypeStruct((tokens, 2 * half), LOW),
        cost_estimate=scaled_cost(
            factor=4,
            flops=4 * grad.size * half,
            bytes_accessed=4 * w_own.size + 2 * grad.size + 4 * tokens * half,
            transcendentals=0,
        ),
        compiler_params=kernel_params(),
        name="qkv_back",
    )(grad, w_own, w_other, *deps)


def swap(values, axis, step):
    count = lax.axis_size(axis)
    return lax.ppermute(values, axis, [(i, i ^ step) for i in range(count)])


def is_relative():
    return lax.axis_size("dp") == 4


def place_of(entry):
    if is_relative():
        return lax.axis_index("dp") ^ entry
    return entry


def gather_begin(values):
    if not is_relative():
        return ()
    return (swap(values, "dp", 1), swap(values, "dp", 2))


def gather_end(values, begun):
    if not is_relative():
        whole = lax.all_gather(values, "dp", axis=0)
        return [whole[k] for k in range(whole.shape[0])]
    first, second = begun
    half = first.shape[0] // 2
    third = jnp.concatenate([swap(second[:half], "dp", 1), swap(first[half:], "dp", 2)], axis=0)
    return [values, first, second, third]


def scatter_begin(parts):
    if not is_relative():
        return ()
    half = parts[0].shape[0] // 2
    _, first, second, third = parts
    return (
        swap(third[:half], "dp", 1),
        swap(third[half:], "dp", 2),
        swap(first[:half], "dp", 1),
        swap(second[half:], "dp", 2),
    )


def scatter_middle(parts, begun):
    if not is_relative():
        return ()
    half = parts[0].shape[0] // 2
    _, first, second, _ = parts
    low_third, high_third = begun[:2]
    return (
        swap((first[half:].astype(FULL) + high_third.astype(FULL)).astype(LOW), "dp", 1),
        swap((second[:half].astype(FULL) + low_third.astype(FULL)).astype(LOW), "dp", 2),
    )


def scatter_end(parts, begun, middle):
    if not is_relative():
        return lax.psum_scatter(jnp.stack(parts), "dp", scatter_dimension=0).astype(FULL)
    half = parts[0].shape[0] // 2
    own = parts[0].astype(FULL)
    first_low, second_high = begun[2:]
    first_high, second_low = middle
    return jnp.concatenate(
        [
            own[:half] + first_low.astype(FULL) + second_low.astype(FULL),
            own[half:] + first_high.astype(FULL) + second_high.astype(FULL),
        ],
        axis=0,
    )


def scatter_dp(parts):
    begun = scatter_begin(parts)
    return scatter_end(parts, begun, scatter_middle(parts, begun))


def trade_dp(parts):
    if not is_relative():
        traded = lax.all_to_all(jnp.stack(parts), "dp", 0, 0, tiled=True)
        return [traded[k] for k in range(traded.shape[0])]
    return [parts[0]] + [swap(parts[k], "dp", k) for k in range(1, 4)]


def exchange_dp(blocks):
    if not is_relative():
        return lax.all_to_all(blocks, "dp", 0, 0, tiled=True)
    me = lax.axis_index("dp")
    got = []
    for k in range(4):
        sent = lax.dynamic_index_in_dim(blocks, me ^ k, 0, keepdims=False)
        got.append(swap(sent, "dp", k) if k else sent)
    odd, far = me % 2 == 1, me >= 2
    first, second = jnp.where(odd, got[1], got[0]), jnp.where(odd, got[0], got[1])
    third, fourth = jnp.where(odd, got[3], got[2]), jnp.where(odd, got[2], got[3])
    return jnp.stack(
        [
            jnp.where(far, third, first),
            jnp.where(far, fourth, second),
            jnp.where(far, first, third),
            jnp.where(far, second, fourth),
        ]
    )


def exchange_row(blocks):
    other = 1 - lax.axis_index("row")
    sent = lax.dynamic_index_in_dim(blocks, other, 0, keepdims=True)
    return lax.dynamic_update_slice_in_dim(blocks, swap(sent, "row", 1), other, 0)


def sum_dp(values):
    if not is_relative():
        return lax.psum(values, "dp")
    one = swap(values, "dp", 1)
    values = values + jnp.stack([one[1], one[0], one[3], one[2]])
    two = swap(values, "dp", 2)
    return values + jnp.stack([two[2], two[3], two[0], two[1]])


def sum_all(values):
    for axis in ("row", "dp", "col"):
        step = 1
        while step < lax.axis_size(axis):
            values = values + swap(values, axis, step)
            step *= 2
    return values


def other_row(values):
    return swap(values, "row", 1)


def attend_kernel(starts, query, key, value, doc_key, doc_query, mixed, log_total):
    sequence = pl.program_id(0)
    parts, _, part, _ = query.shape
    length = parts * part
    nblock = starts.shape[1]
    block = length // nblock
    keys_in = key[...].reshape(length, HD)
    queries = query[...].reshape(length, HD)
    values_turned = value[...].reshape(length, HD).T
    scaling = HD ** (-0.5)
    for b in range(nblock):
        lo = b * block
        hi = lo + block
        scores = (
            lax.dot_general(
                keys_in[:hi],
                queries[lo:hi],
                (((1,), (1,)), ((), ())),
                preferred_element_type=FULL,
            )
            * scaling
        )
        place = lax.broadcasted_iota(jnp.int32, (hi, 1), 0)
        group = jnp.where(place >= starts[sequence, b] * block, doc_key[0, :hi, :], -1)
        scores = jnp.where(group == doc_query[0, :, lo:hi], scores, NEGATIVE)
        highest = jnp.max(scores, axis=0, keepdims=True)
        exponent = jnp.exp(scores - highest)
        total = jnp.sum(exponent, axis=0, keepdims=True)
        probability = (exponent * (1.0 / total)).astype(LOW)
        turned = jnp.dot(values_turned[:, :hi], probability, preferred_element_type=FULL)
        at = lo // part
        mixed[at, 0, lo - at * part : hi - at * part, :] = turned.T.astype(LOW)
        log_total[0, 0, :, lo:hi] = highest + jnp.log(total)


def attend_back_kernel(
    starts, query, key, value, grad_mixed, doc_key, doc_query, log_total, grads, grad_key, grad_value
):
    sequence = pl.program_id(0)
    head = pl.program_id(1)
    parts, _, part, _ = query.shape
    length = parts * part
    nblock = starts.shape[1]
    block = length // nblock
    keys_in = key[...].reshape(length, HD)
    queries = query[...].reshape(length, HD)
    values = value[...].reshape(length, HD)
    upstream = grad_mixed[...].reshape(length, HD)
    keys_turned = keys_in.T
    scaling = HD ** (-0.5)
    query_at = pl.ds(pl.multiple_of(3 * head * HD, HD), HD)
    for b in range(nblock - 1, -1, -1):
        lo = b * block
        hi = lo + block
        scores = (
            lax.dot_general(
                keys_in[:hi],
                queries[lo:hi],
                (((1,), (1,)), ((), ())),
                preferred_element_type=FULL,
            )
            * scaling
        )
        place = lax.broadcasted_iota(jnp.int32, (hi, 1), 0)
        group = jnp.where(place >= starts[sequence, b] * block, doc_key[0, :hi, :], -1)
        scores = jnp.where(group == doc_query[0, :, lo:hi], scores, NEGATIVE)
        probability = jnp.exp(scores - log_total[0, 0, :, lo:hi])
        term_value = jnp.dot(
            probability.astype(LOW), upstream[lo:hi], preferred_element_type=FULL
        )
        grad_prob = lax.dot_general(
            values[:hi], upstream[lo:hi], (((1,), (1,)), ((), ())), preferred_element_type=FULL
        )
        weighted = probability * grad_prob
        center = jnp.sum(weighted, axis=0, keepdims=True)
        grad_scores = (weighted - probability * center).astype(LOW)
        term_key = jnp.dot(grad_scores, queries[lo:hi], preferred_element_type=FULL)
        if b == nblock - 1:
            grad_value[...] = term_value
            grad_key[...] = term_key
        else:
            grad_value[:hi] += term_value
            grad_key[:hi] += term_key
        turned = jnp.dot(keys_turned[:, :hi], grad_scores, preferred_element_type=FULL) * scaling
        at = lo // part
        grads[at, 0, lo - at * part : hi - at * part, query_at] = turned.T.astype(LOW)
    key_at = pl.ds(pl.multiple_of((3 * head + 1) * HD, HD), HD)
    value_at = pl.ds(pl.multiple_of((3 * head + 2) * HD, HD), HD)
    grads[:, 0, :, key_at] = (grad_key[...] * scaling).astype(LOW).reshape(parts, part, HD)
    grads[:, 0, :, value_at] = grad_value[...].astype(LOW).reshape(parts, part, HD)


def attention_cost(packed, heads, products, factor):
    parts, nseq, part, _ = packed.shape
    pairs = nseq * heads * (parts * part) ** 2 * 5 // 8
    return scaled_cost(
        factor=factor, flops=2 * pairs * HD * products, bytes_accessed=2 * packed.size * 2, transcendentals=pairs
    )


def piece_spec(packed, stride, offset):
    parts, _, part, _ = packed.shape
    return pl.BlockSpec((parts, 1, part, HD), lambda s, h, *_: (0, s, 0, stride * h + offset))


def attend_forward(packed, starts, documents):
    parts, nseq, part, width = packed.shape
    heads = width // (3 * HD)
    length = parts * part
    return pl.pallas_call(
        attend_kernel,
        grid_spec=pltpu.PrefetchScalarGridSpec(
            num_scalar_prefetch=1,
            grid=(nseq, heads),
            in_specs=[
                piece_spec(packed, 3, 0),
                piece_spec(packed, 3, 1),
                piece_spec(packed, 3, 2),
                pl.BlockSpec((1, length, 1), lambda s, h, *_: (s, 0, 0)),
                pl.BlockSpec((1, 1, length), lambda s, h, *_: (s, 0, 0)),
            ],
            out_specs=[
                piece_spec(packed, 1, 0),
                pl.BlockSpec((1, 1, 1, length), lambda s, h, *_: (s, h, 0, 0)),
            ],
        ),
        out_shape=[
            jax.ShapeDtypeStruct((parts, nseq, part, heads * HD), LOW),
            jax.ShapeDtypeStruct((nseq, heads, 1, length), FULL),
        ],
        cost_estimate=attention_cost(packed, heads, 2, 2),
        compiler_params=pltpu.CompilerParams(vmem_limit_bytes=48 * 1024 * 1024),
        name="attend",
    )(starts, packed, packed, packed, documents[:, :, None], documents[:, None, :])


def attend_backward(packed, starts, documents, log_total, grad_mixed, deps=()):
    parts, nseq, part, width = packed.shape
    heads = width // (3 * HD)
    length = parts * part
    return pl.pallas_call(
        with_deps(attend_back_kernel, 8, deps),
        grid_spec=pltpu.PrefetchScalarGridSpec(
            num_scalar_prefetch=1,
            grid=(nseq, heads),
            in_specs=[
                piece_spec(packed, 3, 0),
                piece_spec(packed, 3, 1),
                piece_spec(packed, 3, 2),
                piece_spec(packed, 1, 0),
                pl.BlockSpec((1, length, 1), lambda s, h, *_: (s, 0, 0)),
                pl.BlockSpec((1, 1, length), lambda s, h, *_: (s, 0, 0)),
                pl.BlockSpec((1, 1, 1, length), lambda s, h, *_: (s, h, 0, 0)),
            ]
            + dep_specs(deps),
            out_specs=pl.BlockSpec((parts, 1, part, width), lambda s, h, *_: (0, s, 0, 0)),
            scratch_shapes=[pltpu.VMEM((length, HD), FULL), pltpu.VMEM((length, HD), FULL)],
        ),
        out_shape=jax.ShapeDtypeStruct(packed.shape, LOW),
        cost_estimate=attention_cost(packed, heads, 5, 5),
        compiler_params=pltpu.CompilerParams(vmem_limit_bytes=48 * 1024 * 1024),
        name="attend_back",
    )(
        starts,
        packed,
        packed,
        packed,
        grad_mixed,
        documents[:, :, None],
        documents[:, None, :],
        log_total,
        *deps,
    )


def angles(places):
    halfway = HD // 2
    frequency = ROPE_BASE ** (-jnp.arange(halfway, dtype=FULL) / halfway)
    turned = places.astype(FULL)[..., None] * jnp.concatenate([frequency, frequency])
    sign = jnp.where(jnp.arange(HD) < halfway, -1.0, 1.0)
    return (jnp.cos(turned), jnp.sin(turned) * sign)


def norm_back(upstream, normed, scaling, gain):
    scaled = upstream * gain
    inner = jnp.mean(normed * scaled, axis=1, keepdims=True)
    return (scaling * (scaled - normed * inner), jnp.sum(upstream * normed, axis=0))


def placed(shape, piece, starts):
    return lax.dynamic_update_slice(jnp.zeros(shape, FULL), piece, starts).reshape(-1)


def sequence_span(length, tokens):
    return max(1, length // tokens)


def regroup(values, span):
    if span == 1:
        return values
    n_dp, n_col = lax.axis_size("dp"), lax.axis_size("col")
    moves = []
    for i in range(n_dp):
        for j in range(n_col):
            to_i = i - i % span + j % span
            to_j = j - j % span + i % span
            moves.append((i * n_col + j, to_i * n_col + to_j))
    return lax.ppermute(values, ("dp", "col"), moves)


def heads_line_up():
    return H // lax.axis_size("col") == lax.axis_size("dp")


def fetch_qkv(low, deps):
    nb, inner, three, heads, _ = low.shape
    n_dp = lax.axis_size("dp")
    if not heads_line_up():
        whole = lax.all_gather(low, "dp", axis=1, tiled=True)
        whole = lax.all_gather(whole, "col", axis=3, tiled=True)
        mine = H // n_dp
        whole = lax.dynamic_slice_in_dim(whole, lax.axis_index("dp") * mine, mine, 3)
        return whole.transpose(3, 0, 1, 2, 4).reshape(mine, nb * HD, three * HD)
    sent = low.transpose(3, 0, 1, 2, 4).reshape(heads, nb * inner, three * HD)
    got = exchange_dp(after(sent, *deps)).reshape(n_dp, nb, inner, three * HD).transpose(1, 0, 2, 3)
    got = got.reshape(nb * HD, three * HD)
    return lax.all_gather(got, "col", axis=0)


def fetch_out(low):
    heads, inner, cols = low.shape
    if not heads_line_up():
        whole = lax.all_gather(low, "dp", axis=1, tiled=True)
        return lax.all_gather(whole, "col", axis=0, tiled=True).reshape(D, cols)
    got = exchange_dp(low).reshape(HD, cols)
    return lax.all_gather(got, "col", axis=0).reshape(heads * HD, cols)


def send_gate_up(weight):
    nb, inner, two, cols = weight.shape
    n_dp = lax.axis_size("dp")
    mine = cols // n_dp
    sent = weight.astype(LOW).reshape(nb, inner, two, n_dp, mine).transpose(3, 2, 0, 1, 4)
    return sent.reshape(n_dp, two * nb * inner, mine)


def fetch_gate_up(sent, shape):
    nb, inner, two, cols = shape
    n_dp = lax.axis_size("dp")
    mine = cols // n_dp
    got = exchange_dp(sent)
    got = got.reshape(n_dp, two, nb, inner, mine).transpose(1, 2, 0, 3, 4)
    got = got.reshape(two, nb * HD, mine)
    return (lax.all_gather(got, "col", axis=0), got)


def send_down(weight):
    blocks, inner, cols = weight.shape
    n_dp = lax.axis_size("dp")
    return weight.astype(LOW).reshape(n_dp, blocks // n_dp * inner, cols)


def fetch_down(sent, shape):
    blocks, inner, cols = shape
    n_dp, n_col = lax.axis_size("dp"), lax.axis_size("col")
    mine = blocks // n_dp
    got = exchange_dp(sent)
    got = got.reshape(n_dp, mine, inner, cols).transpose(1, 0, 2, 3).reshape(mine * HD, cols)
    return (lax.all_gather(got, "col", axis=0).reshape(n_col * mine * HD, cols), got)


def reduce_col(values):
    return lax.psum_scatter(values, "col", scatter_dimension=0)


def grad_for_other(left, rows, right, columns, steps, by_rows, deps=(), factor=2):
    places = (1, 0) if by_rows else (0, 1)
    return grad_block(left, places[0], rows, right, places[1], columns, steps, (), deps, factor, True)


def grad_for_own(left, rows, right, columns, steps, received, deps=(), factor=2):
    received = [other_row(piece) for piece in received]
    return grad_block(left, 0, rows, right, 0, columns, steps, received, deps, factor)


def in_turn(order, call, results, deps=()):
    for k in order:
        results[k] = call(k, deps)
        last = results[k]
        deps = (last[0] if isinstance(last, (list, tuple)) else last,)
    return deps


def settle_qkv(half, shape):
    nb, inner, three, heads, _ = shape
    n_dp = lax.axis_size("dp")
    mine = H // n_dp
    if not heads_line_up():
        half = half.reshape(mine, nb, HD, three, HD).transpose(1, 2, 3, 0, 4)
        whole = lax.dynamic_update_slice_in_dim(
            jnp.zeros((nb, HD, three, H, HD), LOW), half, lax.axis_index("dp") * mine, 3
        )
        whole = lax.psum_scatter(whole, "dp", scatter_dimension=1, tiled=True)
        return lax.psum_scatter(whole, "col", scatter_dimension=3, tiled=True).astype(FULL)
    summed = half
    sent = summed.reshape(nb, n_dp, inner, three * HD).transpose(1, 0, 2, 3)
    got = exchange_dp(sent.reshape(n_dp, nb * inner, three * HD))
    return got.reshape(n_dp, nb, inner, three, HD).transpose(1, 2, 3, 0, 4).astype(FULL)


def settle_out(half, shape):
    heads, inner, cols = shape
    if not heads_line_up():
        whole = half.reshape(H, HD, cols)
        whole = lax.psum_scatter(whole, "dp", scatter_dimension=1, tiled=True)
        return lax.psum_scatter(whole, "col", scatter_dimension=0, tiled=True).astype(FULL)
    return exchange_dp(half.reshape(lax.axis_size("dp"), inner, cols)).astype(FULL)


def send_gate_up_grad(summed, shape):
    nb, inner, two, cols = shape
    n_dp = lax.axis_size("dp")
    mine = cols // n_dp
    sent = summed.reshape(two, nb, n_dp, inner, mine).transpose(2, 0, 1, 3, 4)
    return sent.reshape(n_dp, two * nb * inner, mine)


def gate_up_grad(got, shape):
    nb, inner, two, cols = shape
    n_dp = lax.axis_size("dp")
    got = got.reshape(n_dp, two, nb, inner, cols // n_dp).transpose(2, 3, 1, 0, 4)
    return got.reshape(shape).astype(FULL)


def send_down_grad(summed, shape):
    blocks, inner, cols = shape
    n_dp = lax.axis_size("dp")
    mine = blocks // n_dp
    sent = summed.reshape(mine, n_dp, inner, cols).transpose(1, 0, 2, 3)
    return sent.reshape(n_dp, mine * inner, cols)


DECAY = 1.0 - STEP ** (-0.8)


def square_sums(matrices, also=None):
    partials = []
    for grad, _, _, _, row_shape, col_shape, row_at, col_at, _ in matrices:
        squares = grad * grad
        partials.append(
            placed(row_shape, jnp.sum(squares, axis=tuple(range(2, grad.ndim))), row_at)
        )
        partials.append(placed(col_shape, jnp.sum(squares, axis=(0, 1)), col_at))
    if also is not None:
        partials.append(also.reshape(-1))
    return jnp.concatenate(partials)


def scaled_updates(matrices, sums):
    updates, rows, cols, sizes = [], [], [], []
    at = 0
    for grad, _, old_row, old_col, row_shape, col_shape, row_at, col_at, _ in matrices:
        row_count, col_count = old_row.shape[0], old_col.shape[0]
        row_means = sums[at : at + row_count] / col_count + TINY_SQUARE
        at += row_count
        col_means = sums[at : at + col_count] / row_count + TINY_SQUARE
        at += col_count
        new_row = DECAY * old_row + (1.0 - DECAY) * row_means
        new_col = DECAY * old_col + (1.0 - DECAY) * col_means
        row_here = lax.dynamic_slice(new_row.reshape(row_shape), row_at, grad.shape[:2])
        col_here = lax.dynamic_slice(new_col.reshape(col_shape), col_at, grad.shape[2:])
        row_here = row_here.reshape(grad.shape[:2] + (1,) * (grad.ndim - 2))
        update = grad * lax.rsqrt(row_here * col_here[None, None] / jnp.mean(new_row))
        updates.append(update)
        rows.append(new_row)
        cols.append(new_col)
        sizes.append(jnp.sum(update * update))
    return (updates, rows, cols, jnp.stack(sizes))


def renew(matrices, updates, rows, cols, sizes):
    renewed = []
    for n, matrix in enumerate(matrices):
        mean_size = sizes[n] / (rows[n].shape[0] * cols[n].shape[0])
        clip = jnp.maximum(1.0, jnp.sqrt(mean_size) / CLIP_LEVEL)
        renewed.append(matrix[1] - matrix[-1] * updates[n] / clip)
    return renewed


def shards(
    inputs,
    cotangent,
    w_qkv,
    w_out,
    w_gate_up,
    w_down,
    gains,
    gain_state,
    row_state,
    col_state,
    positions,
    block_map,
):
    row_pos = lax.axis_index("row")
    col_pos = lax.axis_index("col")
    data_pos = lax.axis_index("dp")
    n_dp, n_col = lax.axis_size("dp"), lax.axis_size("col")
    length = positions.shape[1]
    chip_tokens = inputs.shape[0]
    tokens = chip_tokens // 2
    width = inputs.shape[1]
    span = sequence_span(length, chip_tokens)
    heads_here = H // n_dp
    local = heads_here * HD

    def enter(values):
        values = regroup(values, span)
        kept = lax.dynamic_slice_in_dim(values, row_pos * tokens, tokens, 0)
        sent = lax.dynamic_slice_in_dim(values, (1 - row_pos) * tokens, tokens, 0)
        return jnp.concatenate([kept, swap(sent, "row", 1)], axis=1)

    def leave(values):
        got = swap(values[:, width:], "row", 1)
        result = jnp.zeros((chip_tokens, width), values.dtype)
        result = lax.dynamic_update_slice_in_dim(result, values[:, :width], row_pos * tokens, 0)
        result = lax.dynamic_update_slice_in_dim(result, got, (1 - row_pos) * tokens, 0)
        return regroup(result, span)

    def own_first(vector):
        parts = vector.reshape(2, width)
        return jnp.concatenate(
            [
                lax.dynamic_index_in_dim(parts, row_pos, 0, keepdims=False),
                lax.dynamic_index_in_dim(parts, 1 - row_pos, 0, keepdims=False),
            ]
        )

    x_own = enter(inputs)
    qkv_own = fetch_qkv(w_qkv.astype(LOW), (x_own,))
    out_rows = fetch_out(w_out.astype(LOW))
    gu_sent = send_gate_up(w_gate_up)
    down_sent = send_down(w_down)
    begun = gather_begin(x_own)
    begun = tuple(after(share, gu_sent, down_sent) for share in begun)
    every_place = after(jnp.concatenate([positions, block_map], axis=1), *begun)
    if is_relative() and span == 1:
        twin = other_row(every_place)
        first = row_pos == 0
        every_place = jnp.concatenate(
            [jnp.where(first, every_place, twin), jnp.where(first, twin, every_place)]
        )
        every_place = lax.dynamic_slice_in_dim(every_place, col_pos, 1, 0)
        here = jnp.concatenate(trade_dp([every_place] * n_dp))
        sequences = n_dp
    else:
        every_place = lax.all_gather(every_place, ("dp", "row"), axis=0, tiled=True)
        sequences = n_dp // span
        numbers = []
        for k in range(sequences):
            first = place_of(k) if span == 1 else k * span + col_pos % span
            numbers.append(first * (n_col // span) + col_pos // span)
        here = jnp.concatenate(
            [lax.dynamic_slice_in_dim(every_place, number, 1, 0) for number in numbers]
        )
    places = here[:, :length]
    starts = here[:, length:]
    documents = jnp.cumsum((places == 0).astype(jnp.int32), axis=1)
    x_parts = gather_end(x_own, begun)
    qkv_own = after(qkv_own, *begun)
    qkv_other = other_row(qkv_own)
    x_all = jnp.stack(x_parts)
    gu_own, gu_got = fetch_gate_up(after(gu_sent, x_all), w_gate_up.shape)
    down_own, down_got = fetch_down(after(down_sent, x_all), w_down.shape)
    grad_result = enter(cotangent).astype(FULL)

    token_places = lax.dynamic_index_in_dim(
        places.reshape(n_dp, 2, tokens), row_pos, 1, keepdims=False
    )
    cosine, sine_term = angles(token_places)

    if heads_line_up():
        gain_here = lax.dynamic_index_in_dim(
            gains[:2].reshape(2, n_col, n_dp, HD), data_pos, 2, keepdims=False
        ).reshape(2, local)
    else:
        gain_here = lax.dynamic_slice_in_dim(gains[:2], data_pos * local, local, 1)

    raw, squares = qkv_forward(x_all, qkv_own, qkv_other)
    squares = sum_dp(squares)
    turn = (raw, squares, cosine, sine_term, gain_here)
    out_begun = ()
    if heads_line_up():
        out_begun = gather_begin(after(out_rows, gu_got, down_got))
    packed = rope_forward(*turn, (gu_got, down_got))

    def by_sequence(values):
        if span == 1:
            return values
        last = values.shape[-1]
        values = values.reshape(2, sequences, span, tokens, last).transpose(1, 2, 0, 3, 4)
        return values.reshape(1, sequences, length, last)

    def by_shard(values):
        if span == 1:
            return values
        last = values.shape[-1]
        values = values.reshape(sequences, span, 2, tokens, last).transpose(2, 0, 1, 3, 4)
        return values.reshape(2, n_dp, tokens, last)

    packed = by_sequence(exchange_row(packed))
    out_own = out_rows
    mixed, log_total = attend_forward(packed, starts, documents)
    if heads_line_up():
        out_begun = tuple(after(share, log_total) for share in out_begun)
        out_own = jnp.concatenate(gather_end(out_rows, out_begun), axis=0)
    out_other = other_row(out_own)
    mixed = exchange_row(by_shard(mixed))
    mixed = trade_dp([mixed[:, k] for k in range(n_dp)])
    attended = jnp.concatenate([piece[core] for piece in mixed for core in range(2)], axis=1)

    attn = down_forward(attended, out_own, out_other, FULL, (gu_own,))
    gain_attn = own_first(gains[2])[None, :]
    gain_mlp = own_first(gains[3])[None, :]
    attn_scale = lax.rsqrt(jnp.mean(attn * attn, axis=1, keepdims=True) + EPSILON)
    attn_hat = attn * attn_scale
    hidden_in = x_own.astype(FULL) + attn_hat * gain_attn
    h_own = hidden_in.astype(LOW)
    begun = gather_begin(h_own)
    gu_own = after(gu_own, h_own)
    gu_other = other_row(gu_own)
    by_arrival = list(range(n_dp))
    by_distance = [3, 1, 2, 0] if is_relative() else by_arrival
    gated = [None] * n_dp
    last, rest = (), by_arrival
    if is_relative():
        gated[0] = gate_forward(h_own, gu_own, gu_other)
        last, rest = (gated[0][0],), by_arrival[1:]
        begun = tuple(after(share, *last) for share in begun)
    h_parts = gather_end(h_own, begun)

    def gate_part(k, deps):
        deps = deps + ((h_parts[3], down_own) if k == 2 else ())
        return gate_forward(h_parts[k], gu_own, gu_other, deps)

    in_turn(rest, gate_part, gated, last)
    hiddens = [entry[0] for entry in gated]
    down_own = after(down_own, hiddens[2])
    down_other = other_row(down_own)
    terms = [None] * n_dp
    in_turn(
        by_distance,
        lambda k, deps: down_forward(hiddens[k], down_own, down_other, LOW, deps),
        terms,
    )
    mlp = scatter_dp(terms)
    mlp_scale = lax.rsqrt(jnp.mean(mlp * mlp, axis=1, keepdims=True) + EPSILON)
    mlp_hat = mlp * mlp_scale
    result = leave(hidden_in + mlp_hat * gain_mlp)

    grad_mlp, gain_mlp_grad = norm_back(grad_result, mlp_hat, mlp_scale, gain_mlp)
    m_own = grad_mlp.astype(LOW)
    weights = (gu_own, gu_other, down_own, down_other)
    backs = [None] * n_dp
    begun = gather_begin(m_own)
    if is_relative():
        m_parts = [m_own]
        last = in_turn(
            [0], lambda k, deps: mlp_backward(m_own, *gated[k][1:], *weights, deps), backs
        )
        begun = tuple(after(share, *last) for share in begun)
        rest = [1, 3, 2]
    else:
        last, rest = (), by_arrival
    m_parts = gather_end(m_own, begun)
    last = in_turn(
        rest,
        lambda k, deps: mlp_backward(m_parts[k], *gated[k][1:], *weights, deps),
        backs,
        last,
    )
    units = hiddens[0].shape[1]
    down_block = (hiddens, units, [m_parts], width, 1)
    gu_block = (
        h_parts,
        width,
        [[entry[0] for entry in backs], [entry[1] for entry in backs]],
        gu_own.shape[3],
        n_col,
    )
    terms = [entry[2] for entry in backs]
    begun = scatter_begin(terms)
    gu_rest = grad_for_other(*gu_block, True, last + begun[:3])
    down_rest = grad_for_other(*down_block, False, (gu_rest[0],) + begun[3:])
    middle = scatter_middle(terms, begun)
    gu_half = grad_for_own(*gu_block, gu_rest, (down_rest[0],) + middle)
    gu_sum = reduce_col(gu_half)
    terms[0] = after(terms[0], gu_half)
    grad_hidden_in = grad_result + scatter_end(terms, begun, middle)

    grad_attn, gain_attn_grad = norm_back(grad_hidden_in, attn_hat, attn_scale, gain_attn)
    grad_attn_low = grad_attn.astype(LOW)
    sent = attended_backward(grad_attn_low, out_own, out_other, n_dp, (gu_half,))
    out_block = ([attended], D, [[grad_attn_low]], width, 1)
    out_rest = grad_for_other(*out_block, False, (sent[0],), 4)
    grad_mixed = by_sequence(exchange_row(jnp.stack(trade_dp(sent), axis=1)))
    grads = attend_backward(packed, starts, documents, log_total, grad_mixed, (out_rest[0],))
    out_half = grad_for_own(*out_block, out_rest, (grads,), 4)
    grads = exchange_row(by_shard(grads))
    inner, gain_pair = rope_inner(*turn, grads)
    gu_got = exchange_dp(send_gate_up_grad(gu_sum, w_gate_up.shape))
    out_begun = ()
    if heads_line_up():
        out_parts = out_half.reshape(n_dp, local, width)
        out_parts = [out_parts[k] for k in range(n_dp)]
        out_begun = scatter_begin(out_parts)
    qkv_low = rope_backward(*turn, grads, sum_dp(inner))
    down_half = grad_for_own(*down_block, down_rest, (gu_sum, qkv_low) + out_begun)
    down_sum = reduce_col(down_half.reshape(n_col, -1, width))
    qkv_block = (
        [x_all.reshape(n_dp * tokens, D)],
        width,
        [[qkv_low.reshape(n_dp * tokens, 3 * local)]],
        3 * HD,
        heads_here,
    )
    out_middle = ()
    if heads_line_up():
        out_middle = scatter_middle(out_parts, out_begun)
    qkv_rest = grad_for_other(*qkv_block, True, (down_half,), 4)
    if heads_line_up():
        out_half = scatter_end(out_parts, out_begun, out_middle).astype(LOW)
        out_half = reduce_col(after(out_half.reshape(n_col, HD, width), gu_sum))
    down_got = exchange_dp(send_down_grad(down_sum, w_down.shape))
    grad_gu = gate_up_grad(gu_got, w_gate_up.shape)
    grad_down = down_got.reshape(w_down.shape).astype(FULL)
    grad_out = settle_out(out_half, w_out.shape)
    terms = [None] * n_dp

    def back_term(k, deps):
        deps = deps + ((grad_gu,) if k == by_distance[-1] else ())
        return qkv_backward(qkv_low[k], qkv_own, qkv_other, deps)

    last = in_turn(by_distance[:1], back_term, terms, (qkv_rest[0],))
    qkv_half = grad_for_own(*qkv_block, qkv_rest, last + out_middle, 4)
    in_turn(by_distance[1:], back_term, terms, (qkv_half,))
    begun = scatter_begin(terms)
    middle = scatter_middle(terms, begun)
    if heads_line_up():
        qkv_sum = reduce_col(after(qkv_half[:, 0], down_sum))
    else:
        qkv_sum = qkv_half
    grad_qkv = settle_qkv(qkv_sum, w_qkv.shape)
    terms[0] = after(terms[0], qkv_sum)
    grad_inputs = leave(grad_hidden_in + scatter_end(terms, begun, middle))

    if heads_line_up():
        gain_pair = placed(
            (2, n_col, n_dp, HD), gain_pair.reshape(2, n_col, 1, HD), (0, 0, data_pos, 0)
        )
    else:
        gain_pair = placed((2, D), gain_pair, (0, data_pos * local))
    gain_partial = jnp.concatenate(
        [
            gain_pair.reshape(2, D),
            own_first(gain_attn_grad)[None, :],
            own_first(gain_mlp_grad)[None, :],
        ]
    )

    nb_rows, inner_rows, _, heads_col, _ = grad_qkv.shape
    ff_blocks = grad_down.shape[0]
    ff_cols = grad_gu.shape[3]
    row_at = (row_pos * nb_rows, data_pos * inner_rows)
    early = [
        (
            grad_down,
            w_down,
            row_state[3 * D :],
            col_state[4 * D + 2 * FF :],
            (FF // HD, HD),
            (D,),
            (col_pos * ff_blocks, data_pos * inner_rows),
            (row_pos * width,),
            3.0 * FF ** (-0.5),
        ),
        (
            grad_gu,
            w_gate_up,
            row_state[2 * D : 3 * D],
            col_state[4 * D : 4 * D + 2 * FF],
            (D // HD, HD),
            (2, FF),
            row_at,
            (0, col_pos * ff_cols),
            3.0 * D ** (-0.5),
        ),
        (
            grad_out,
            w_out,
            row_state[D : 2 * D],
            col_state[3 * D : 4 * D],
            (H, HD),
            (D,),
            (col_pos * heads_col, data_pos * inner_rows),
            (row_pos * width,),
            3.0 * D ** (-0.5),
        ),
    ]
    early_updates, early_rows, early_cols, early_sizes = scaled_updates(
        early, sum_all(after(square_sums(early), qkv_half))
    )
    row_down, row_gu, row_out = early_rows
    col_down, col_gu, col_out = early_cols
    late = [
        (
            grad_qkv,
            w_qkv,
            row_state[:D],
            col_state[: 3 * D],
            (D // HD, HD),
            (3, H, HD),
            row_at,
            (0, col_pos * heads_col, 0),
            3.0 * D ** (-0.5),
        )
    ]
    sums = sum_all(square_sums(late, gain_partial))
    gain_grad = sums[-gain_partial.size :].reshape(gain_partial.shape)
    late_updates, late_rows, late_cols, late_sizes = scaled_updates(late, sums)
    new_down, new_gu, new_out, new_qkv = renew(
        early + late,
        early_updates + late_updates,
        early_rows + late_rows,
        early_cols + late_cols,
        sum_all(jnp.concatenate([early_sizes, late_sizes])),
    )
    (row_qkv,), (col_qkv,) = late_rows, late_cols
    gain_new_state = DECAY * gain_state + (1.0 - DECAY) * (gain_grad * gain_grad + TINY_SQUARE)
    gain_update = gain_grad * lax.rsqrt(gain_new_state)
    gain_update = gain_update / jnp.maximum(
        1.0, jnp.sqrt(jnp.mean(gain_update * gain_update, axis=1, keepdims=True)) / CLIP_LEVEL
    )
    new_gains = gains - GAIN_RATE * gain_update
    return (
        result,
        grad_inputs,
        grad_qkv,
        grad_out,
        grad_gu,
        grad_down,
        new_qkv,
        new_out,
        new_gu,
        new_down,
        new_qkv.astype(LOW),
        new_out.astype(LOW),
        new_gu.astype(LOW),
        new_down.astype(LOW),
        jnp.concatenate([row_qkv, row_out, row_gu, row_down]),
        jnp.concatenate([col_qkv, col_out, col_gu, col_down]),
        gain_grad,
        gain_new_state,
        new_gains,
    )


def solution(mesh):
    return jax.shard_map(
        shards,
        mesh=mesh,
        in_specs=(
            P(("dp", "col"), "row"),
            P(("dp", "col"), "row"),
            P("row", "dp", None, "col", None),
            P("col", "dp", "row"),
            P("row", "dp", None, "col"),
            P("col", "dp", "row"),
            P(),
            P(),
            P(),
            P(),
            P(("dp", "row"), None),
            P(("dp", "row"), None),
        ),
        out_specs=(
            P(("dp", "col"), "row"),
            P(("dp", "col"), "row"),
            P("row", "dp", None, "col", None),
            P("col", "dp", "row"),
            P("row", "dp", None, "col"),
            P("col", "dp", "row"),
            P("row", "dp", None, "col", None),
            P("col", "dp", "row"),
            P("row", "dp", None, "col"),
            P("col", "dp", "row"),
            P("row", "dp", None, "col", None),
            P("col", "dp", "row"),
            P("row", "dp", None, "col"),
            P("col", "dp", "row"),
            P(),
            P(),
            P(),
            P(),
            P(),
        ),
        check_vma=False,
    )
```

```python
import functools
import math

import jax
import jax.numpy as jnp
import numpy as np
from jax import lax
from jax.experimental import pallas as pl
from jax.experimental.pallas import tpu as pltpu
from jax.sharding import PartitionSpec as P

D = 2048
H = 16
HD = 128
FF = 8192
STEP = 3


EPSILON = 1e-06
TINY_SQUARE = 1e-30
ROPE_BASE = 500000.0
NEGATIVE = -1e30
CLIP_LEVEL = 0.5
GAIN_RATE = 0.3

LOW = jnp.bfloat16
FULL = jnp.float32


VMEM_LIMIT = 56 * 1024 * 1024


def dot(left, right):
    return jnp.dot(left, right, preferred_element_type=FULL)


def dot_back(left, right):
    return lax.dot_general(left, right, (((1,), (1,)), ((), ())), preferred_element_type=FULL)


def scaled_cost(flops, bytes_accessed, transcendentals, factor=2):
    return pl.CostEstimate(
        flops=factor * flops,
        bytes_accessed=factor * bytes_accessed,
        transcendentals=factor * transcendentals,
    )


def with_deps(kernel, count, deps):
    def body(*refs):
        return kernel(*refs[:count], *refs[count + len(deps) :])

    return body


def dep_specs(deps):
    return [pl.BlockSpec(memory_space=pl.ANY)] * len(deps)


def after(value, *others):
    if not others:
        return value

    def body(*refs):
        pass

    return pl.pallas_call(
        body,
        in_specs=dep_specs((value,) + others),
        out_specs=pl.BlockSpec(memory_space=pl.ANY),
        out_shape=jax.ShapeDtypeStruct(value.shape, value.dtype),
        input_output_aliases={0: 0},
        name="after",
    )(value, *others)


def kernel_params():
    return pltpu.CompilerParams(vmem_limit_bytes=VMEM_LIMIT)


def gate_kernel(h, gu_own, gu_other, hidden, by_gate, by_up):
    half = gu_own.shape[2]
    left = h[:, :half]
    right = h[:, half:]
    gate = dot(left, gu_own[0, 0]) + dot(right, gu_other[0, 0])
    up = dot(left, gu_own[0, 1]) + dot(right, gu_other[0, 1])
    sigmoid_gate = 1.0 / (1.0 + jnp.exp(-gate))
    silu = gate * sigmoid_gate
    hidden[...] = (silu * up).astype(LOW)
    by_gate[...] = (up * sigmoid_gate * (1.0 + gate * (1.0 - sigmoid_gate))).astype(LOW)
    by_up[...] = silu.astype(LOW)


def gate_forward(h, gu_own, gu_other, deps=()):
    tokens, width = h.shape
    n_col, _, half, mine = gu_own.shape
    weight = pl.BlockSpec((1, 2, half, mine), lambda j: (j, 0, 0, 0))
    piece = pl.BlockSpec((tokens, mine), lambda j: (0, j))
    shape = jax.ShapeDtypeStruct((tokens, n_col * mine), LOW)
    return pl.pallas_call(
        with_deps(gate_kernel, 3, deps),
        grid=(n_col,),
        in_specs=[pl.BlockSpec((tokens, width), lambda j: (0, 0)), weight, weight]
        + dep_specs(deps),
        out_specs=[piece, piece, piece],
        out_shape=[shape, shape, shape],
        cost_estimate=scaled_cost(
            flops=4 * tokens * width * n_col * mine,
            bytes_accessed=4 * gu_own.size + 2 * h.size + 6 * tokens * n_col * mine,
            transcendentals=tokens * n_col * mine,
        ),
        compiler_params=kernel_params(),
        name="gate_up",
    )(h, gu_own, gu_other, *deps)


def down_kernel(hidden, down_own, down_other, term):
    half = down_own.shape[1]
    term[:, :half] = dot(hidden[...], down_own[...]).astype(term.dtype)
    term[:, half:] = dot(hidden[...], down_other[...]).astype(term.dtype)


def down_forward(hidden, down_own, down_other, kind=LOW, deps=()):
    tokens, units = hidden.shape
    half = down_own.shape[1]
    rows = min(tokens, 256)
    weight = pl.BlockSpec((units, half), lambda i: (0, 0))
    return pl.pallas_call(
        with_deps(down_kernel, 3, deps),
        grid=(tokens // rows,),
        in_specs=[pl.BlockSpec((rows, units), lambda i: (i, 0)), weight, weight]
        + dep_specs(deps),
        out_specs=pl.BlockSpec((rows, 2 * half), lambda i: (i, 0)),
        out_shape=jax.ShapeDtypeStruct((tokens, 2 * half), kind),
        cost_estimate=scaled_cost(
            flops=4 * tokens * units * half,
            bytes_accessed=4 * down_own.size + 2 * hidden.size + 4 * tokens * half,
            transcendentals=0,
        ),
        compiler_params=kernel_params(),
        name="down",
    )(hidden, down_own, down_other, *deps)


def attended_back_kernel(grad, out_own, out_other, *results):
    half = out_own.shape[1]
    value = dot_back(grad[:, :half], out_own[...]) + dot_back(grad[:, half:], out_other[...])
    for k in range(len(results)):

        @pl.when(pl.program_id(0) == k)
        def _(k=k):
            results[k][0] = value.astype(LOW)


def attended_backward(grad, out_own, out_other, n_dp, deps):
    tokens, width = grad.shape
    rows, half = out_own.shape
    columns = rows // n_dp // 2
    weight = pl.BlockSpec((columns, half), lambda k, c: (2 * k + c, 0))

    def result_spec(i):
        return pl.BlockSpec(
            (1, tokens, columns), lambda k, c: (jnp.clip(2 * (k - i) + c, 0, 1), 0, 0)
        )

    return pl.pallas_call(
        with_deps(attended_back_kernel, 3, deps),
        grid=(n_dp, 2),
        in_specs=[pl.BlockSpec((tokens, width), lambda k, c: (0, 0)), weight, weight]
        + dep_specs(deps),
        out_specs=[result_spec(i) for i in range(n_dp)],
        out_shape=[jax.ShapeDtypeStruct((2, tokens, columns), LOW)] * n_dp,
        cost_estimate=scaled_cost(
            factor=3,
            flops=2 * grad.size * rows,
            bytes_accessed=4 * out_own.size + 2 * grad.size + 2 * tokens * rows,
            transcendentals=0,
        ),
        compiler_params=kernel_params(),
        name="attended_back",
    )(grad, out_own, out_other, *deps)


def mlp_back_kernel(
    m, by_gate, by_up, gu_own, gu_other, down_own, down_other, grad_gate, grad_up, term, total
):
    j = pl.program_id(0)
    half = gu_own.shape[2]
    grad_hidden = dot_back(m[:, :half], down_own[0]) + dot_back(m[:, half:], down_other[0])
    low_gate = (grad_hidden * by_gate[...].astype(FULL)).astype(LOW)
    low_up = (grad_hidden * by_up[...].astype(FULL)).astype(LOW)
    grad_gate[...] = low_gate
    grad_up[...] = low_up
    own = dot_back(low_gate, gu_own[0, 0]) + dot_back(low_up, gu_own[0, 1])
    other = dot_back(low_gate, gu_other[0, 0]) + dot_back(low_up, gu_other[0, 1])

    @pl.when(j == 0)
    def _():
        total[:, :half] = own
        total[:, half:] = other

    @pl.when(j > 0)
    def _():
        total[:, :half] += own
        total[:, half:] += other

    @pl.when(j == pl.num_programs(0) - 1)
    def _():
        term[...] = total[...].astype(LOW)


def mlp_backward(m, by_gate, by_up, gu_own, gu_other, down_own, down_other, deps=()):
    tokens, width = m.shape
    n_col, _, half, mine = gu_own.shape
    weight = pl.BlockSpec((1, 2, half, mine), lambda j: (j, 0, 0, 0))
    weight_down = pl.BlockSpec((1, mine, half), lambda j: (j, 0, 0))
    piece = pl.BlockSpec((tokens, mine), lambda j: (0, j))
    whole = pl.BlockSpec((tokens, width), lambda j: (0, 0))
    shape = jax.ShapeDtypeStruct((tokens, n_col * mine), LOW)
    return pl.pallas_call(
        with_deps(mlp_back_kernel, 7, deps),
        grid=(n_col,),
        in_specs=[whole, piece, piece, weight, weight, weight_down, weight_down]
        + dep_specs(deps),
        out_specs=[piece, piece, whole],
        out_shape=[shape, shape, jax.ShapeDtypeStruct((tokens, width), LOW)],
        scratch_shapes=[pltpu.VMEM((tokens, width), FULL)],
        cost_estimate=scaled_cost(
            flops=6 * tokens * width * n_col * mine,
            bytes_accessed=6 * gu_own.size + 4 * m.size + 8 * tokens * n_col * mine,
            transcendentals=0,
        ),
        compiler_params=kernel_params(),
        name="mlp_back",
    )(
        m,
        by_gate,
        by_up,
        gu_own,
        gu_other,
        down_own.reshape(n_col, mine, half),
        down_other.reshape(n_col, mine, half),
        *deps,
    )


def grad_kernel(count, groups, received, pieces, *refs):
    left = refs[:count]
    right = refs[count : count + count * groups]
    others = refs[count + count * groups : count + count * groups + received]
    results, turned = refs[-1 - pieces : -1], refs[-1]
    part = left[0].shape[0]
    step = pl.program_id(1)

    @pl.when(step == 0)
    def _():
        for k in range(count):
            turned[:, k * part : (k + 1) * part] = left[k][...].T

    for g in range(groups):
        total = None
        for k in range(count):
            term = dot(turned[:, k * part : (k + 1) * part], right[g * count + k][...])
            total = term if total is None else total + term
        if not received and pieces == 1:
            results[0][0, g] = total.astype(LOW)
        for n in range(max(received, pieces) if received or pieces > 1 else 0):

            @pl.when(step == n)
            def _(n=n):
                value = total + others[n][0, g].astype(FULL) if received else total
                results[n if pieces > 1 else 0][0, g] = value.astype(LOW)


def grad_block(
    left, left_at, rows, right, right_at, columns, steps, received, deps=(), factor=2, split=False
):
    count, groups = len(left), len(right)
    part = left[0].shape[0]
    tile = min(rows, 512)
    tiles = rows // tile
    left_spec = pl.BlockSpec((part, tile), lambda a, j: (0, left_at * tiles + a))
    right_spec = pl.BlockSpec((part, columns), lambda a, j: (0, right_at + j))
    share_spec = pl.BlockSpec((1, groups, tile, columns), lambda a, j: (0, 0, a, 0))
    result_spec = pl.BlockSpec((1, groups, tile, columns), lambda a, j: (j, 0, a, 0))
    operands = list(left) + [piece for group in right for piece in group] + list(received)
    specs = [left_spec] * count + [right_spec] * (count * groups) + [share_spec] * len(received)
    reads = len(operands)
    size = steps * groups * rows * columns
    pieces = steps if split else 1
    results = pl.pallas_call(
        with_deps(
            functools.partial(grad_kernel, count, groups, len(received), pieces), reads, deps
        ),
        grid=(tiles, steps),
        in_specs=specs + dep_specs(deps),
        out_specs=[share_spec if split else result_spec] * pieces,
        out_shape=[jax.ShapeDtypeStruct((steps // pieces, groups, rows, columns), LOW)] * pieces,
        scratch_shapes=[pltpu.VMEM((tile, count * part), LOW)],
        cost_estimate=scaled_cost(
            factor=factor,
            flops=2 * size * count * part,
            bytes_accessed=4 * size + 2 * count * part * (rows + steps * groups * columns * tiles),
            transcendentals=0,
        ),
        compiler_params=kernel_params(),
        name="weight_grad",
    )(*operands, *deps)
    return results if split else results[0]


def qkv_kernel(x, w_own, w_other, raw, squares, query_sum, key_sum):
    j = pl.program_id(1)
    half = w_own.shape[1]
    got = dot(x[0, :, :half], w_own[0]) + dot(x[0, :, half:], w_other[0])
    raw[0] = got
    query = got[:, :HD]
    key = got[:, HD : 2 * HD]

    @pl.when(j == 0)
    def _():
        query_sum[...] = query * query
        key_sum[...] = key * key

    @pl.when(j > 0)
    def _():
        query_sum[...] += query * query
        key_sum[...] += key * key

    @pl.when(j == pl.num_programs(1) - 1)
    def _():
        squares[0, 0:1] = jnp.sum(query_sum[...].T, axis=0, keepdims=True)
        squares[0, 1:2] = jnp.sum(key_sum[...].T, axis=0, keepdims=True)


def qkv_forward(x, w_own, w_other):
    shards_of, tokens, width = x.shape
    heads, half, columns = w_own.shape
    weight = pl.BlockSpec((1, half, columns), lambda k, j: (j, 0, 0))
    return pl.pallas_call(
        qkv_kernel,
        grid=(shards_of, heads),
        in_specs=[pl.BlockSpec((1, tokens, width), lambda k, j: (k, 0, 0)), weight, weight],
        out_specs=[
            pl.BlockSpec((1, tokens, columns), lambda k, j: (k, 0, j)),
            pl.BlockSpec((1, 2, tokens), lambda k, j: (k, 0, 0)),
        ],
        out_shape=[
            jax.ShapeDtypeStruct((shards_of, tokens, heads * columns), FULL),
            jax.ShapeDtypeStruct((shards_of, 2, tokens), FULL),
        ],
        scratch_shapes=[pltpu.VMEM((tokens, HD), FULL), pltpu.VMEM((tokens, HD), FULL)],
        cost_estimate=scaled_cost(
            flops=2 * x.size * heads * columns,
            bytes_accessed=2 * x.size + 4 * shards_of * w_own.size + 4 * shards_of * tokens * heads * columns,
            transcendentals=0,
        ),
        compiler_params=kernel_params(),
        name="qkv",
    )(x, w_own, w_other)


def token_scales(squares):
    return lax.rsqrt(squares[0] / D + EPSILON).T


def rope_kernel(raw, squares, cosine, sine_term, gain, packed):
    heads = gain.shape[1] // HD
    scales = token_scales(squares)
    for h in range(heads):
        core, at = h // (heads // 2), h % (heads // 2) * 3 * HD
        for n in range(2):
            value = raw[0, :, (3 * h + n) * HD : (3 * h + n + 1) * HD] * scales[:, n : n + 1]
            value = value * gain[n : n + 1, h * HD : (h + 1) * HD]
            turned = value * cosine[0] + pltpu.roll(value, HD // 2, 1) * sine_term[0]
            packed[core, 0, :, at + n * HD : at + (n + 1) * HD] = turned.astype(LOW)
        packed[core, 0, :, at + 2 * HD : at + 3 * HD] = raw[
            0, :, (3 * h + 2) * HD : (3 * h + 3) * HD
        ].astype(LOW)


def rope_specs(raw, gain):
    shards_of, tokens, columns = raw.shape
    return [
        pl.BlockSpec((1, tokens, columns), lambda k: (k, 0, 0)),
        pl.BlockSpec((1, 2, tokens), lambda k: (k, 0, 0)),
        pl.BlockSpec((1, tokens, HD), lambda k: (k, 0, 0)),
        pl.BlockSpec((1, tokens, HD), lambda k: (k, 0, 0)),
        pl.BlockSpec(gain.shape, lambda k: (0, 0)),
    ]


def rope_forward(raw, squares, cosine, sine_term, gain, deps=()):
    shards_of, tokens, columns = raw.shape
    return pl.pallas_call(
        with_deps(rope_kernel, 5, deps),
        grid=(shards_of,),
        in_specs=rope_specs(raw, gain) + dep_specs(deps),
        out_specs=pl.BlockSpec((2, 1, tokens, columns // 2), lambda k: (0, k, 0, 0)),
        out_shape=jax.ShapeDtypeStruct((2, shards_of, tokens, columns // 2), LOW),
        cost_estimate=scaled_cost(
            flops=8 * raw.size, bytes_accessed=6 * raw.size, transcendentals=0
        ),
        compiler_params=kernel_params(),
        name="rope",
    )(raw, squares, cosine, sine_term, gain, *deps)


def turned_back(grads, raw, cosine, sine_term, gain, scales, h, n):
    heads = gain.shape[1] // HD
    core, at = h // (heads // 2), (h % (heads // 2) * 3 + n) * HD
    value = grads[core, 0, :, at : at + HD].astype(FULL)
    value = value * cosine[0] - pltpu.roll(value, HD // 2, 1) * sine_term[0]
    normed = raw[0, :, (3 * h + n) * HD : (3 * h + n + 1) * HD] * scales[:, n : n + 1]
    return (value, normed, value * gain[n : n + 1, h * HD : (h + 1) * HD])


def rope_inner_kernel(raw, squares, cosine, sine_term, gain, grads, inner, gain_grad):
    heads = gain.shape[1] // HD
    scales = token_scales(squares)

    @pl.when(pl.program_id(0) == 0)
    def _():
        gain_grad[...] = jnp.zeros(gain_grad.shape, FULL)

    for n in range(2):
        total = None
        for h in range(heads):
            value, normed, scaled = turned_back(
                grads, raw, cosine, sine_term, gain, scales, h, n
            )
            term = normed * scaled
            total = term if total is None else total + term
            gain_grad[n : n + 1, h * HD : (h + 1) * HD] += jnp.sum(
                value * normed, axis=0, keepdims=True
            )
        inner[0, n : n + 1] = jnp.sum(total.T, axis=0, keepdims=True)


def rope_inner(raw, squares, cosine, sine_term, gain, grads, deps=()):
    shards_of, tokens, columns = raw.shape
    return pl.pallas_call(
        with_deps(rope_inner_kernel, 6, deps),
        grid=(shards_of,),
        in_specs=rope_specs(raw, gain)
        + [pl.BlockSpec((2, 1, tokens, columns // 2), lambda k: (0, k, 0, 0))]
        + dep_specs(deps),
        out_specs=[
            pl.BlockSpec((1, 2, tokens), lambda k: (k, 0, 0)),
            pl.BlockSpec(gain.shape, lambda k: (0, 0)),
        ],
        out_shape=[
            jax.ShapeDtypeStruct((shards_of, 2, tokens), FULL),
            jax.ShapeDtypeStruct(gain.shape, FULL),
        ],
        cost_estimate=scaled_cost(
            factor=4,
            flops=12 * raw.size, bytes_accessed=6 * raw.size, transcendentals=0
        ),
        compiler_params=kernel_params(),
        name="rope_inner",
    )(raw, squares, cosine, sine_term, gain, grads, *deps)


def rope_back_kernel(raw, squares, cosine, sine_term, gain, grads, inner, result):
    heads = gain.shape[1] // HD
    scales = token_scales(squares)
    means = (inner[0] / D).T
    for h in range(heads):
        for n in range(2):
            _, normed, scaled = turned_back(grads, raw, cosine, sine_term, gain, scales, h, n)
            value = scales[:, n : n + 1] * (scaled - normed * means[:, n : n + 1])
            result[0, :, (3 * h + n) * HD : (3 * h + n + 1) * HD] = value.astype(LOW)
        core, at = h // (heads // 2), (h % (heads // 2) * 3 + 2) * HD
        result[0, :, (3 * h + 2) * HD : (3 * h + 3) * HD] = grads[core, 0, :, at : at + HD]


def rope_backward(raw, squares, cosine, sine_term, gain, grads, inner, deps=()):
    shards_of, tokens, columns = raw.shape
    return pl.pallas_call(
        with_deps(rope_back_kernel, 7, deps),
        grid=(shards_of,),
        in_specs=rope_specs(raw, gain)
        + [
            pl.BlockSpec((2, 1, tokens, columns // 2), lambda k: (0, k, 0, 0)),
            pl.BlockSpec((1, 2, tokens), lambda k: (k, 0, 0)),
        ]
        + dep_specs(deps),
        out_specs=pl.BlockSpec((1, tokens, columns), lambda k: (k, 0, 0)),
        out_shape=jax.ShapeDtypeStruct((shards_of, tokens, columns), LOW),
        cost_estimate=scaled_cost(
            factor=4,
            flops=12 * raw.size, bytes_accessed=8 * raw.size, transcendentals=0
        ),
        compiler_params=kernel_params(),
        name="rope_back",
    )(raw, squares, cosine, sine_term, gain, grads, inner, *deps)


def qkv_back_kernel(grad, w_own, w_other, term):
    heads, half, columns = w_own.shape
    for part, weight in enumerate((w_own, w_other)):
        total = None
        for j in range(heads):
            value = dot_back(grad[:, j * columns : (j + 1) * columns], weight[j])
            total = value if total is None else total + value
        term[:, part * half : (part + 1) * half] = total.astype(LOW)


def qkv_backward(grad, w_own, w_other, deps=()):
    tokens, columns = grad.shape
    heads, half, _ = w_own.shape
    rows = min(tokens, 256)
    weight = pl.BlockSpec(w_own.shape, lambda i: (0, 0, 0))
    return pl.pallas_call(
        with_deps(qkv_back_kernel, 3, deps),
        grid=(tokens // rows,),
        in_specs=[pl.BlockSpec((rows, columns), lambda i: (i, 0)), weight, weight]
        + dep_specs(deps),
        out_specs=pl.BlockSpec((rows, 2 * half), lambda i: (i, 0)),
        out_shape=jax.ShapeDtypeStruct((tokens, 2 * half), LOW),
        cost_estimate=scaled_cost(
            factor=4,
            flops=4 * grad.size * half,
            bytes_accessed=4 * w_own.size + 2 * grad.size + 4 * tokens * half,
            transcendentals=0,
        ),
        compiler_params=kernel_params(),
        name="qkv_back",
    )(grad, w_own, w_other, *deps)


def swap(values, axis, step):
    count = lax.axis_size(axis)
    return lax.ppermute(values, axis, [(i, i ^ step) for i in range(count)])


def is_relative():
    return lax.axis_size("dp") == 4


def place_of(entry):
    if is_relative():
        return lax.axis_index("dp") ^ entry
    return entry


def gather_begin(values):
    if not is_relative():
        return ()
    return (swap(values, "dp", 1), swap(values, "dp", 2))


def gather_end(values, begun):
    if not is_relative():
        whole = lax.all_gather(values, "dp", axis=0)
        return [whole[k] for k in range(whole.shape[0])]
    first, second = begun
    half = first.shape[0] // 2
    third = jnp.concatenate([swap(second[:half], "dp", 1), swap(first[half:], "dp", 2)], axis=0)
    return [values, first, second, third]


def scatter_begin(parts):
    if not is_relative():
        return ()
    half = parts[0].shape[0] // 2
    _, first, second, third = parts
    return (
        swap(third[:half], "dp", 1),
        swap(third[half:], "dp", 2),
        swap(first[:half], "dp", 1),
        swap(second[half:], "dp", 2),
    )


def scatter_middle(parts, begun):
    if not is_relative():
        return ()
    half = parts[0].shape[0] // 2
    _, first, second, _ = parts
    low_third, high_third = begun[:2]
    return (
        swap((first[half:].astype(FULL) + high_third.astype(FULL)).astype(LOW), "dp", 1),
        swap((second[:half].astype(FULL) + low_third.astype(FULL)).astype(LOW), "dp", 2),
    )


def scatter_end(parts, begun, middle):
    if not is_relative():
        return lax.psum_scatter(jnp.stack(parts), "dp", scatter_dimension=0).astype(FULL)
    half = parts[0].shape[0] // 2
    own = parts[0].astype(FULL)
    first_low, second_high = begun[2:]
    first_high, second_low = middle
    return jnp.concatenate(
        [
            own[:half] + first_low.astype(FULL) + second_low.astype(FULL),
            own[half:] + first_high.astype(FULL) + second_high.astype(FULL),
        ],
        axis=0,
    )


def scatter_dp(parts):
    begun = scatter_begin(parts)
    return scatter_end(parts, begun, scatter_middle(parts, begun))


def trade_dp(parts):
    if not is_relative():
        traded = lax.all_to_all(jnp.stack(parts), "dp", 0, 0, tiled=True)
        return [traded[k] for k in range(traded.shape[0])]
    return [parts[0]] + [swap(parts[k], "dp", k) for k in range(1, 4)]


def exchange_dp(blocks):
    if not is_relative():
        return lax.all_to_all(blocks, "dp", 0, 0, tiled=True)
    me = lax.axis_index("dp")
    got = []
    for k in range(4):
        sent = lax.dynamic_index_in_dim(blocks, me ^ k, 0, keepdims=False)
        got.append(swap(sent, "dp", k) if k else sent)
    odd, far = me % 2 == 1, me >= 2
    first, second = jnp.where(odd, got[1], got[0]), jnp.where(odd, got[0], got[1])
    third, fourth = jnp.where(odd, got[3], got[2]), jnp.where(odd, got[2], got[3])
    return jnp.stack(
        [
            jnp.where(far, third, first),
            jnp.where(far, fourth, second),
            jnp.where(far, first, third),
            jnp.where(far, second, fourth),
        ]
    )


def exchange_row(blocks):
    other = 1 - lax.axis_index("row")
    sent = lax.dynamic_index_in_dim(blocks, other, 0, keepdims=True)
    return lax.dynamic_update_slice_in_dim(blocks, swap(sent, "row", 1), other, 0)


def sum_dp(values):
    if not is_relative():
        return lax.psum(values, "dp")
    one = swap(values, "dp", 1)
    values = values + jnp.stack([one[1], one[0], one[3], one[2]])
    two = swap(values, "dp", 2)
    return values + jnp.stack([two[2], two[3], two[0], two[1]])


def sum_all(values):
    for axis in ("row", "dp", "col"):
        step = 1
        while step < lax.axis_size(axis):
            values = values + swap(values, axis, step)
            step *= 2
    return values


def other_row(values):
    return swap(values, "row", 1)


def attend_kernel(starts, query, key, value, doc_key, doc_query, mixed, log_total):
    sequence = pl.program_id(0)
    parts, _, part, _ = query.shape
    length = parts * part
    nblock = starts.shape[1]
    block = length // nblock
    keys_in = key[...].reshape(length, HD)
    queries = query[...].reshape(length, HD)
    values_turned = value[...].reshape(length, HD).T
    scaling = HD ** (-0.5)
    for b in range(nblock):
        lo = b * block
        hi = lo + block
        scores = (
            lax.dot_general(
                keys_in[:hi],
                queries[lo:hi],
                (((1,), (1,)), ((), ())),
                preferred_element_type=FULL,
            )
            * scaling
        )
        place = lax.broadcasted_iota(jnp.int32, (hi, 1), 0)
        group = jnp.where(place >= starts[sequence, b] * block, doc_key[0, :hi, :], -1)
        scores = jnp.where(group == doc_query[0, :, lo:hi], scores, NEGATIVE)
        highest = jnp.max(scores, axis=0, keepdims=True)
        exponent = jnp.exp(scores - highest)
        total = jnp.sum(exponent, axis=0, keepdims=True)
        probability = (exponent * (1.0 / total)).astype(LOW)
        turned = jnp.dot(values_turned[:, :hi], probability, preferred_element_type=FULL)
        at = lo // part
        mixed[at, 0, lo - at * part : hi - at * part, :] = turned.T.astype(LOW)
        log_total[0, 0, :, lo:hi] = highest + jnp.log(total)


def attend_back_kernel(
    starts, query, key, value, grad_mixed, doc_key, doc_query, log_total, grads, grad_key, grad_value
):
    sequence = pl.program_id(0)
    head = pl.program_id(1)
    parts, _, part, _ = query.shape
    length = parts * part
    nblock = starts.shape[1]
    block = length // nblock
    keys_in = key[...].reshape(length, HD)
    queries = query[...].reshape(length, HD)
    values = value[...].reshape(length, HD)
    upstream = grad_mixed[...].reshape(length, HD)
    keys_turned = keys_in.T
    scaling = HD ** (-0.5)
    query_at = pl.ds(pl.multiple_of(3 * head * HD, HD), HD)
    for b in range(nblock - 1, -1, -1):
        lo = b * block
        hi = lo + block
        scores = (
            lax.dot_general(
                keys_in[:hi],
                queries[lo:hi],
                (((1,), (1,)), ((), ())),
                preferred_element_type=FULL,
            )
            * scaling
        )
        place = lax.broadcasted_iota(jnp.int32, (hi, 1), 0)
        group = jnp.where(place >= starts[sequence, b] * block, doc_key[0, :hi, :], -1)
        scores = jnp.where(group == doc_query[0, :, lo:hi], scores, NEGATIVE)
        probability = jnp.exp(scores - log_total[0, 0, :, lo:hi])
        term_value = jnp.dot(
            probability.astype(LOW), upstream[lo:hi], preferred_element_type=FULL
        )
        grad_prob = lax.dot_general(
            values[:hi], upstream[lo:hi], (((1,), (1,)), ((), ())), preferred_element_type=FULL
        )
        weighted = probability * grad_prob
        center = jnp.sum(weighted, axis=0, keepdims=True)
        grad_scores = (weighted - probability * center).astype(LOW)
        term_key = jnp.dot(grad_scores, queries[lo:hi], preferred_element_type=FULL)
        if b == nblock - 1:
            grad_value[...] = term_value
            grad_key[...] = term_key
        else:
            grad_value[:hi] += term_value
            grad_key[:hi] += term_key
        turned = jnp.dot(keys_turned[:, :hi], grad_scores, preferred_element_type=FULL) * scaling
        at = lo // part
        grads[at, 0, lo - at * part : hi - at * part, query_at] = turned.T.astype(LOW)
    key_at = pl.ds(pl.multiple_of((3 * head + 1) * HD, HD), HD)
    value_at = pl.ds(pl.multiple_of((3 * head + 2) * HD, HD), HD)
    grads[:, 0, :, key_at] = (grad_key[...] * scaling).astype(LOW).reshape(parts, part, HD)
    grads[:, 0, :, value_at] = grad_value[...].astype(LOW).reshape(parts, part, HD)


def attention_cost(packed, heads, products, factor):
    parts, nseq, part, _ = packed.shape
    pairs = nseq * heads * (parts * part) ** 2 * 5 // 8
    return scaled_cost(
        factor=factor, flops=2 * pairs * HD * products, bytes_accessed=2 * packed.size * 2, transcendentals=pairs
    )


def piece_spec(packed, stride, offset):
    parts, _, part, _ = packed.shape
    return pl.BlockSpec((parts, 1, part, HD), lambda s, h, *_: (0, s, 0, stride * h + offset))


def attend_forward(packed, starts, documents):
    parts, nseq, part, width = packed.shape
    heads = width // (3 * HD)
    length = parts * part
    return pl.pallas_call(
        attend_kernel,
        grid_spec=pltpu.PrefetchScalarGridSpec(
            num_scalar_prefetch=1,
            grid=(nseq, heads),
            in_specs=[
                piece_spec(packed, 3, 0),
                piece_spec(packed, 3, 1),
                piece_spec(packed, 3, 2),
                pl.BlockSpec((1, length, 1), lambda s, h, *_: (s, 0, 0)),
                pl.BlockSpec((1, 1, length), lambda s, h, *_: (s, 0, 0)),
            ],
            out_specs=[
                piece_spec(packed, 1, 0),
                pl.BlockSpec((1, 1, 1, length), lambda s, h, *_: (s, h, 0, 0)),
            ],
        ),
        out_shape=[
            jax.ShapeDtypeStruct((parts, nseq, part, heads * HD), LOW),
            jax.ShapeDtypeStruct((nseq, heads, 1, length), FULL),
        ],
        cost_estimate=attention_cost(packed, heads, 2, 2),
        compiler_params=pltpu.CompilerParams(vmem_limit_bytes=48 * 1024 * 1024),
        name="attend",
    )(starts, packed, packed, packed, documents[:, :, None], documents[:, None, :])


def attend_backward(packed, starts, documents, log_total, grad_mixed, deps=()):
    parts, nseq, part, width = packed.shape
    heads = width // (3 * HD)
    length = parts * part
    return pl.pallas_call(
        with_deps(attend_back_kernel, 8, deps),
        grid_spec=pltpu.PrefetchScalarGridSpec(
            num_scalar_prefetch=1,
            grid=(nseq, heads),
            in_specs=[
                piece_spec(packed, 3, 0),
                piece_spec(packed, 3, 1),
                piece_spec(packed, 3, 2),
                piece_spec(packed, 1, 0),
                pl.BlockSpec((1, length, 1), lambda s, h, *_: (s, 0, 0)),
                pl.BlockSpec((1, 1, length), lambda s, h, *_: (s, 0, 0)),
                pl.BlockSpec((1, 1, 1, length), lambda s, h, *_: (s, h, 0, 0)),
            ]
            + dep_specs(deps),
            out_specs=pl.BlockSpec((parts, 1, part, width), lambda s, h, *_: (0, s, 0, 0)),
            scratch_shapes=[pltpu.VMEM((length, HD), FULL), pltpu.VMEM((length, HD), FULL)],
        ),
        out_shape=jax.ShapeDtypeStruct(packed.shape, LOW),
        cost_estimate=attention_cost(packed, heads, 5, 5),
        compiler_params=pltpu.CompilerParams(vmem_limit_bytes=48 * 1024 * 1024),
        name="attend_back",
    )(
        starts,
        packed,
        packed,
        packed,
        grad_mixed,
        documents[:, :, None],
        documents[:, None, :],
        log_total,
        *deps,
    )


def angles(places):
    halfway = HD // 2
    frequency = ROPE_BASE ** (-jnp.arange(halfway, dtype=FULL) / halfway)
    turned = places.astype(FULL)[..., None] * jnp.concatenate([frequency, frequency])
    sign = jnp.where(jnp.arange(HD) < halfway, -1.0, 1.0)
    return (jnp.cos(turned), jnp.sin(turned) * sign)


def norm_back(upstream, normed, scaling, gain):
    scaled = upstream * gain
    inner = jnp.mean(normed * scaled, axis=1, keepdims=True)
    return (scaling * (scaled - normed * inner), jnp.sum(upstream * normed, axis=0))


def placed(shape, piece, starts):
    return lax.dynamic_update_slice(jnp.zeros(shape, FULL), piece, starts).reshape(-1)


def sequence_span(length, tokens):
    return max(1, length // tokens)


def regroup(values, span):
    if span == 1:
        return values
    n_dp, n_col = lax.axis_size("dp"), lax.axis_size("col")
    moves = []
    for i in range(n_dp):
        for j in range(n_col):
            to_i = i - i % span + j % span
            to_j = j - j % span + i % span
            moves.append((i * n_col + j, to_i * n_col + to_j))
    return lax.ppermute(values, ("dp", "col"), moves)


def heads_line_up():
    return H // lax.axis_size("col") == lax.axis_size("dp")


def fetch_qkv(low, deps):
    nb, inner, three, heads, _ = low.shape
    n_dp = lax.axis_size("dp")
    if not heads_line_up():
        whole = lax.all_gather(low, "dp", axis=1, tiled=True)
        whole = lax.all_gather(whole, "col", axis=3, tiled=True)
        mine = H // n_dp
        whole = lax.dynamic_slice_in_dim(whole, lax.axis_index("dp") * mine, mine, 3)
        return whole.transpose(3, 0, 1, 2, 4).reshape(mine, nb * HD, three * HD)
    sent = low.transpose(3, 0, 1, 2, 4).reshape(heads, nb * inner, three * HD)
    got = exchange_dp(after(sent, *deps)).reshape(n_dp, nb, inner, three * HD).transpose(1, 0, 2, 3)
    got = got.reshape(nb * HD, three * HD)
    return lax.all_gather(got, "col", axis=0)


def fetch_out(low):
    heads, inner, cols = low.shape
    if not heads_line_up():
        whole = lax.all_gather(low, "dp", axis=1, tiled=True)
        return lax.all_gather(whole, "col", axis=0, tiled=True).reshape(D, cols)
    got = exchange_dp(low).reshape(HD, cols)
    return lax.all_gather(got, "col", axis=0).reshape(heads * HD, cols)


def send_gate_up(weight):
    nb, inner, two, cols = weight.shape
    n_dp = lax.axis_size("dp")
    mine = cols // n_dp
    sent = weight.astype(LOW).reshape(nb, inner, two, n_dp, mine).transpose(3, 2, 0, 1, 4)
    return sent.reshape(n_dp, two * nb * inner, mine)


def fetch_gate_up(sent, shape):
    nb, inner, two, cols = shape
    n_dp = lax.axis_size("dp")
    mine = cols // n_dp
    got = exchange_dp(sent)
    got = got.reshape(n_dp, two, nb, inner, mine).transpose(1, 2, 0, 3, 4)
    got = got.reshape(two, nb * HD, mine)
    return (lax.all_gather(got, "col", axis=0), got)


def send_down(weight):
    blocks, inner, cols = weight.shape
    n_dp = lax.axis_size("dp")
    return weight.astype(LOW).reshape(n_dp, blocks // n_dp * inner, cols)


def fetch_down(sent, shape):
    blocks, inner, cols = shape
    n_dp, n_col = lax.axis_size("dp"), lax.axis_size("col")
    mine = blocks // n_dp
    got = exchange_dp(sent)
    got = got.reshape(n_dp, mine, inner, cols).transpose(1, 0, 2, 3).reshape(mine * HD, cols)
    return (lax.all_gather(got, "col", axis=0).reshape(n_col * mine * HD, cols), got)


def reduce_col(values):
    return lax.psum_scatter(values, "col", scatter_dimension=0)


def grad_for_other(left, rows, right, columns, steps, by_rows, deps=(), factor=2):
    places = (1, 0) if by_rows else (0, 1)
    return grad_block(left, places[0], rows, right, places[1], columns, steps, (), deps, factor, True)


def grad_for_own(left, rows, right, columns, steps, received, deps=(), factor=2):
    received = [other_row(piece) for piece in received]
    return grad_block(left, 0, rows, right, 0, columns, steps, received, deps, factor)


def in_turn(order, call, results, deps=()):
    for k in order:
        results[k] = call(k, deps)
        last = results[k]
        deps = (last[0] if isinstance(last, (list, tuple)) else last,)
    return deps


def settle_qkv(half, shape):
    nb, inner, three, heads, _ = shape
    n_dp = lax.axis_size("dp")
    mine = H // n_dp
    if not heads_line_up():
        half = half.reshape(mine, nb, HD, three, HD).transpose(1, 2, 3, 0, 4)
        whole = lax.dynamic_update_slice_in_dim(
            jnp.zeros((nb, HD, three, H, HD), LOW), half, lax.axis_index("dp") * mine, 3
        )
        whole = lax.psum_scatter(whole, "dp", scatter_dimension=1, tiled=True)
        return lax.psum_scatter(whole, "col", scatter_dimension=3, tiled=True).astype(FULL)
    summed = half
    sent = summed.reshape(nb, n_dp, inner, three * HD).transpose(1, 0, 2, 3)
    got = exchange_dp(sent.reshape(n_dp, nb * inner, three * HD))
    return got.reshape(n_dp, nb, inner, three, HD).transpose(1, 2, 3, 0, 4).astype(FULL)


def settle_out(half, shape):
    heads, inner, cols = shape
    if not heads_line_up():
        whole = half.reshape(H, HD, cols)
        whole = lax.psum_scatter(whole, "dp", scatter_dimension=1, tiled=True)
        return lax.psum_scatter(whole, "col", scatter_dimension=0, tiled=True).astype(FULL)
    return exchange_dp(half.reshape(lax.axis_size("dp"), inner, cols)).astype(FULL)


def send_gate_up_grad(summed, shape):
    nb, inner, two, cols = shape
    n_dp = lax.axis_size("dp")
    mine = cols // n_dp
    sent = summed.reshape(two, nb, n_dp, inner, mine).transpose(2, 0, 1, 3, 4)
    return sent.reshape(n_dp, two * nb * inner, mine)


def gate_up_grad(got, shape):
    nb, inner, two, cols = shape
    n_dp = lax.axis_size("dp")
    got = got.reshape(n_dp, two, nb, inner, cols // n_dp).transpose(2, 3, 1, 0, 4)
    return got.reshape(shape).astype(FULL)


def send_down_grad(summed, shape):
    blocks, inner, cols = shape
    n_dp = lax.axis_size("dp")
    mine = blocks // n_dp
    sent = summed.reshape(mine, n_dp, inner, cols).transpose(1, 0, 2, 3)
    return sent.reshape(n_dp, mine * inner, cols)


DECAY = 1.0 - STEP ** (-0.8)


def square_sums(matrices):
    rows, cols = [], []
    for grad, _, row_shape, col_shape, row_at, col_at, _ in matrices:
        squares = grad * grad
        rows.append(placed(row_shape, jnp.sum(squares, axis=tuple(range(2, grad.ndim))), row_at))
        cols.append(placed(col_shape, jnp.sum(squares, axis=(0, 1)), col_at))
    return (jnp.concatenate(rows), jnp.concatenate(cols))


def spans(shapes):
    at, result = 0, []
    for shape in shapes:
        result.append((at, at + math.prod(shape)))
        at = result[-1][1]
    return result


def new_states(matrices, row_sums, col_sums, old_row, old_col):
    row_spans = spans([matrix[2] for matrix in matrices])
    col_spans = spans([matrix[3] for matrix in matrices])
    row_parts = np.concatenate(
        [np.full(b - a, 1.0 / (d - c), np.float32) for (a, b), (c, d) in zip(row_spans, col_spans)]
    )
    col_parts = np.concatenate(
        [np.full(d - c, 1.0 / (b - a), np.float32) for (a, b), (c, d) in zip(row_spans, col_spans)]
    )
    new_row = DECAY * old_row + (1.0 - DECAY) * (row_sums * row_parts + TINY_SQUARE)
    new_col = DECAY * old_col + (1.0 - DECAY) * (col_sums * col_parts + TINY_SQUARE)
    return (new_row, new_col)


def scaled_updates(matrices, new_row, new_col):
    row_spans = spans([matrix[2] for matrix in matrices])
    col_spans = spans([matrix[3] for matrix in matrices])
    updates, sizes = [], []
    for n, (grad, _, row_shape, col_shape, row_at, col_at, _) in enumerate(matrices):
        row_all = new_row[slice(*row_spans[n])]
        col_all = new_col[slice(*col_spans[n])]
        row_here = lax.dynamic_slice(row_all.reshape(row_shape), row_at, grad.shape[:2])
        col_here = lax.dynamic_slice(col_all.reshape(col_shape), col_at, grad.shape[2:])
        row_here = row_here.reshape(grad.shape[:2] + (1,) * (grad.ndim - 2))
        update = grad * lax.rsqrt(row_here * col_here[None, None] / jnp.mean(row_all))
        updates.append(update)
        sizes.append(jnp.sum(update * update))
    lane = lax.broadcasted_iota(jnp.int32, (8, 128), 1)
    packed = jnp.zeros((8, 128), FULL)
    for n, size in enumerate(sizes):
        packed = jnp.where(lane == n, size, packed)
    return (updates, packed)


def renew(matrices, updates, sizes):
    renewed = []
    for n, matrix in enumerate(matrices):
        count = math.prod(matrix[2]) * math.prod(matrix[3])
        clip = jnp.maximum(1.0, jnp.sqrt(sizes[0, n] / count) / CLIP_LEVEL)
        renewed.append(matrix[1] - matrix[-1] * updates[n] / clip)
    return renewed


def shards(
    inputs,
    cotangent,
    w_qkv,
    w_out,
    w_gate_up,
    w_down,
    gains,
    gain_state,
    row_state,
    col_state,
    positions,
    block_map,
):
    row_pos = lax.axis_index("row")
    col_pos = lax.axis_index("col")
    data_pos = lax.axis_index("dp")
    n_dp, n_col = lax.axis_size("dp"), lax.axis_size("col")
    length = positions.shape[1]
    chip_tokens = inputs.shape[0]
    tokens = chip_tokens // 2
    width = inputs.shape[1]
    span = sequence_span(length, chip_tokens)
    heads_here = H // n_dp
    local = heads_here * HD

    def enter(values):
        values = regroup(values, span)
        kept = lax.dynamic_slice_in_dim(values, row_pos * tokens, tokens, 0)
        sent = lax.dynamic_slice_in_dim(values, (1 - row_pos) * tokens, tokens, 0)
        return jnp.concatenate([kept, swap(sent, "row", 1)], axis=1)

    def leave(values):
        got = swap(values[:, width:], "row", 1)
        result = jnp.zeros((chip_tokens, width), values.dtype)
        result = lax.dynamic_update_slice_in_dim(result, values[:, :width], row_pos * tokens, 0)
        result = lax.dynamic_update_slice_in_dim(result, got, (1 - row_pos) * tokens, 0)
        return regroup(result, span)

    def own_first(vector):
        parts = vector.reshape(2, width)
        return jnp.concatenate(
            [
                lax.dynamic_index_in_dim(parts, row_pos, 0, keepdims=False),
                lax.dynamic_index_in_dim(parts, 1 - row_pos, 0, keepdims=False),
            ]
        )

    x_own = enter(inputs)
    qkv_own = fetch_qkv(w_qkv.astype(LOW), (x_own,))
    out_rows = fetch_out(w_out.astype(LOW))
    gu_sent = send_gate_up(w_gate_up)
    down_sent = send_down(w_down)
    begun = gather_begin(x_own)
    begun = tuple(after(share, gu_sent, down_sent) for share in begun)
    every_place = after(jnp.concatenate([positions, block_map], axis=1), *begun)
    if is_relative() and span == 1:
        twin = other_row(every_place)
        first = row_pos == 0
        every_place = jnp.concatenate(
            [jnp.where(first, every_place, twin), jnp.where(first, twin, every_place)]
        )
        every_place = lax.dynamic_slice_in_dim(every_place, col_pos, 1, 0)
        here = jnp.concatenate(trade_dp([every_place] * n_dp))
        sequences = n_dp
    else:
        every_place = lax.all_gather(every_place, ("dp", "row"), axis=0, tiled=True)
        sequences = n_dp // span
        numbers = []
        for k in range(sequences):
            first = place_of(k) if span == 1 else k * span + col_pos % span
            numbers.append(first * (n_col // span) + col_pos // span)
        here = jnp.concatenate(
            [lax.dynamic_slice_in_dim(every_place, number, 1, 0) for number in numbers]
        )
    places = here[:, :length]
    starts = here[:, length:]
    documents = jnp.cumsum((places == 0).astype(jnp.int32), axis=1)
    x_parts = gather_end(x_own, begun)
    qkv_own = after(qkv_own, *begun)
    qkv_other = other_row(qkv_own)
    x_all = jnp.stack(x_parts)
    gu_own, gu_got = fetch_gate_up(after(gu_sent, x_all), w_gate_up.shape)
    down_own, down_got = fetch_down(after(down_sent, x_all), w_down.shape)
    grad_result = enter(cotangent).astype(FULL)

    token_places = lax.dynamic_index_in_dim(
        places.reshape(n_dp, 2, tokens), row_pos, 1, keepdims=False
    )
    cosine, sine_term = angles(token_places)

    if heads_line_up():
        gain_here = lax.dynamic_index_in_dim(
            gains[:2].reshape(2, n_col, n_dp, HD), data_pos, 2, keepdims=False
        ).reshape(2, local)
    else:
        gain_here = lax.dynamic_slice_in_dim(gains[:2], data_pos * local, local, 1)

    raw, squares = qkv_forward(x_all, qkv_own, qkv_other)
    squares = sum_dp(squares)
    turn = (raw, squares, cosine, sine_term, gain_here)
    out_begun = ()
    if heads_line_up():
        out_begun = gather_begin(after(out_rows, gu_got, down_got))
    packed = rope_forward(*turn, (gu_got, down_got))

    def by_sequence(values):
        if span == 1:
            return values
        last = values.shape[-1]
        values = values.reshape(2, sequences, span, tokens, last).transpose(1, 2, 0, 3, 4)
        return values.reshape(1, sequences, length, last)

    def by_shard(values):
        if span == 1:
            return values
        last = values.shape[-1]
        values = values.reshape(sequences, span, 2, tokens, last).transpose(2, 0, 1, 3, 4)
        return values.reshape(2, n_dp, tokens, last)

    packed = by_sequence(exchange_row(packed))
    out_own = out_rows
    mixed, log_total = attend_forward(packed, starts, documents)
    if heads_line_up():
        out_begun = tuple(after(share, log_total) for share in out_begun)
        out_own = jnp.concatenate(gather_end(out_rows, out_begun), axis=0)
    out_other = other_row(out_own)
    mixed = exchange_row(by_shard(mixed))
    mixed = trade_dp([mixed[:, k] for k in range(n_dp)])
    attended = jnp.concatenate([piece[core] for piece in mixed for core in range(2)], axis=1)

    attn = down_forward(attended, out_own, out_other, FULL, (gu_own,))
    gain_attn = own_first(gains[2])[None, :]
    gain_mlp = own_first(gains[3])[None, :]
    attn_scale = lax.rsqrt(jnp.mean(attn * attn, axis=1, keepdims=True) + EPSILON)
    attn_hat = attn * attn_scale
    hidden_in = x_own.astype(FULL) + attn_hat * gain_attn
    h_own = hidden_in.astype(LOW)
    begun = gather_begin(h_own)
    gu_own = after(gu_own, h_own)
    gu_other = other_row(gu_own)
    by_arrival = list(range(n_dp))
    by_distance = [3, 1, 2, 0] if is_relative() else by_arrival
    gated = [None] * n_dp
    last, rest = (), by_arrival
    if is_relative():
        gated[0] = gate_forward(h_own, gu_own, gu_other)
        last, rest = (gated[0][0],), by_arrival[1:]
        begun = tuple(after(share, *last) for share in begun)
    h_parts = gather_end(h_own, begun)

    def gate_part(k, deps):
        deps = deps + ((h_parts[3], down_own) if k == 2 else ())
        return gate_forward(h_parts[k], gu_own, gu_other, deps)

    in_turn(rest, gate_part, gated, last)
    hiddens = [entry[0] for entry in gated]
    down_own = after(down_own, hiddens[2])
    down_other = other_row(down_own)
    terms = [None] * n_dp
    in_turn(
        by_distance,
        lambda k, deps: down_forward(hiddens[k], down_own, down_other, LOW, deps),
        terms,
    )
    mlp = scatter_dp(terms)
    mlp_scale = lax.rsqrt(jnp.mean(mlp * mlp, axis=1, keepdims=True) + EPSILON)
    mlp_hat = mlp * mlp_scale
    result = leave(hidden_in + mlp_hat * gain_mlp)

    grad_mlp, gain_mlp_grad = norm_back(grad_result, mlp_hat, mlp_scale, gain_mlp)
    m_own = grad_mlp.astype(LOW)
    weights = (gu_own, gu_other, down_own, down_other)
    backs = [None] * n_dp
    begun = gather_begin(m_own)
    if is_relative():
        m_parts = [m_own]
        last = in_turn(
            [0], lambda k, deps: mlp_backward(m_own, *gated[k][1:], *weights, deps), backs
        )
        begun = tuple(after(share, *last) for share in begun)
        rest = [1, 3, 2]
    else:
        last, rest = (), by_arrival
    m_parts = gather_end(m_own, begun)
    last = in_turn(
        rest,
        lambda k, deps: mlp_backward(m_parts[k], *gated[k][1:], *weights, deps),
        backs,
        last,
    )
    units = hiddens[0].shape[1]
    down_block = (hiddens, units, [m_parts], width, 1)
    gu_block = (
        h_parts,
        width,
        [[entry[0] for entry in backs], [entry[1] for entry in backs]],
        gu_own.shape[3],
        n_col,
    )
    terms = [entry[2] for entry in backs]
    begun = scatter_begin(terms)
    gu_rest = grad_for_other(*gu_block, True, last + begun[:3])
    down_rest = grad_for_other(*down_block, False, (gu_rest[0],) + begun[3:])
    middle = scatter_middle(terms, begun)
    gu_half = grad_for_own(*gu_block, gu_rest, (down_rest[0],) + middle)
    gu_sum = reduce_col(gu_half)
    terms[0] = after(terms[0], gu_half)
    grad_hidden_in = grad_result + scatter_end(terms, begun, middle)

    grad_attn, gain_attn_grad = norm_back(grad_hidden_in, attn_hat, attn_scale, gain_attn)
    grad_attn_low = grad_attn.astype(LOW)
    sent = attended_backward(grad_attn_low, out_own, out_other, n_dp, (gu_half,))
    out_block = ([attended], D, [[grad_attn_low]], width, 1)
    out_rest = grad_for_other(*out_block, False, (sent[0],), 4)
    grad_mixed = by_sequence(exchange_row(jnp.stack(trade_dp(sent), axis=1)))
    grads = attend_backward(packed, starts, documents, log_total, grad_mixed, (out_rest[0],))
    out_half = grad_for_own(*out_block, out_rest, (grads,), 4)
    grads = exchange_row(by_shard(grads))
    inner, gain_pair = rope_inner(*turn, grads)
    gu_got = exchange_dp(send_gate_up_grad(gu_sum, w_gate_up.shape))
    out_begun = ()
    if heads_line_up():
        out_parts = out_half.reshape(n_dp, local, width)
        out_parts = [out_parts[k] for k in range(n_dp)]
        out_begun = scatter_begin(out_parts)
    qkv_low = rope_backward(*turn, grads, sum_dp(inner))
    down_half = grad_for_own(*down_block, down_rest, (gu_sum, qkv_low) + out_begun)
    down_sum = reduce_col(down_half.reshape(n_col, -1, width))
    qkv_block = (
        [x_all.reshape(n_dp * tokens, D)],
        width,
        [[qkv_low.reshape(n_dp * tokens, 3 * local)]],
        3 * HD,
        heads_here,
    )
    out_middle = ()
    if heads_line_up():
        out_middle = scatter_middle(out_parts, out_begun)
    qkv_rest = grad_for_other(*qkv_block, True, (down_half,), 4)
    if heads_line_up():
        out_half = scatter_end(out_parts, out_begun, out_middle).astype(LOW)
        out_half = reduce_col(after(out_half.reshape(n_col, HD, width), gu_sum))
    down_got = exchange_dp(send_down_grad(down_sum, w_down.shape))
    grad_gu = gate_up_grad(gu_got, w_gate_up.shape)
    grad_down = down_got.reshape(w_down.shape).astype(FULL)
    grad_out = settle_out(out_half, w_out.shape)
    terms = [None] * n_dp
    back_order = [3, 1, 0, 2] if is_relative() else by_arrival

    def back_term(k, deps):
        deps = deps + ((grad_gu,) if k == back_order[-1] else ())
        return qkv_backward(qkv_low[k], qkv_own, qkv_other, deps)

    last = in_turn(back_order[:1], back_term, terms, (qkv_rest[0],))
    qkv_half = grad_for_own(*qkv_block, qkv_rest, last + out_middle, 4)
    in_turn(back_order[1:], back_term, terms, (qkv_half,))
    begun = scatter_begin(terms)
    middle = scatter_middle(terms, begun)
    if heads_line_up():
        qkv_sum = reduce_col(after(qkv_half[:, 0], down_sum))
    else:
        qkv_sum = qkv_half
    grad_qkv = settle_qkv(qkv_sum, w_qkv.shape)
    grad_inputs = leave(grad_hidden_in + scatter_end(terms, begun, middle))

    if heads_line_up():
        gain_pair = placed(
            (2, n_col, n_dp, HD), gain_pair.reshape(2, n_col, 1, HD), (0, 0, data_pos, 0)
        )
    else:
        gain_pair = placed((2, D), gain_pair, (0, data_pos * local))
    gain_partial = jnp.concatenate(
        [
            gain_pair.reshape(2, D),
            own_first(gain_attn_grad)[None, :],
            own_first(gain_mlp_grad)[None, :],
        ]
    )

    nb_rows, inner_rows, _, heads_col, _ = grad_qkv.shape
    ff_blocks = grad_down.shape[0]
    ff_cols = grad_gu.shape[3]
    row_at = (row_pos * nb_rows, data_pos * inner_rows)
    out_at = (col_pos * heads_col, data_pos * inner_rows)
    down_at = (col_pos * ff_blocks, data_pos * inner_rows)
    own_half = (row_pos * width,)
    rate, down_rate = 3.0 * D ** (-0.5), 3.0 * FF ** (-0.5)
    matrices = [
        (grad_qkv, w_qkv, (D // HD, HD), (3, H, HD), row_at, (0, col_pos * heads_col, 0), rate),
        (grad_out, w_out, (H, HD), (D,), out_at, own_half, rate),
        (grad_gu, w_gate_up, (D // HD, HD), (2, FF), row_at, (0, col_pos * ff_cols), rate),
        (grad_down, w_down, (FF // HD, HD), (D,), down_at, own_half, down_rate),
    ]
    row_part, col_part = square_sums(matrices)
    sums = sum_all(jnp.concatenate([row_part, col_part, gain_partial.reshape(-1)]))
    row_end, col_end = row_part.size, row_part.size + col_part.size
    new_row, new_col = new_states(
        matrices, sums[:row_end], sums[row_end:col_end], row_state, col_state
    )
    gain_grad = sums[col_end:].reshape(gain_partial.shape)
    updates, sizes = scaled_updates(matrices, new_row, new_col)
    new_qkv, new_out, new_gu, new_down = renew(matrices, updates, sum_all(sizes))
    gain_new_state = DECAY * gain_state + (1.0 - DECAY) * (gain_grad * gain_grad + TINY_SQUARE)
    gain_update = gain_grad * lax.rsqrt(gain_new_state)
    gain_update = gain_update / jnp.maximum(
        1.0, jnp.sqrt(jnp.mean(gain_update * gain_update, axis=1, keepdims=True)) / CLIP_LEVEL
    )
    new_gains = gains - GAIN_RATE * gain_update
    return (
        result,
        grad_inputs,
        grad_qkv,
        grad_out,
        grad_gu,
        grad_down,
        new_qkv,
        new_out,
        new_gu,
        new_down,
        new_qkv.astype(LOW),
        new_out.astype(LOW),
        new_gu.astype(LOW),
        new_down.astype(LOW),
        new_row,
        new_col,
        gain_grad,
        gain_new_state,
        new_gains,
    )


def solution(mesh):
    return jax.shard_map(
        shards,
        mesh=mesh,
        in_specs=(
            P(("dp", "col"), "row"),
            P(("dp", "col"), "row"),
            P("row", "dp", None, "col", None),
            P("col", "dp", "row"),
            P("row", "dp", None, "col"),
            P("col", "dp", "row"),
            P(),
            P(),
            P(),
            P(),
            P(("dp", "row"), None),
            P(("dp", "row"), None),
        ),
        out_specs=(
            P(("dp", "col"), "row"),
            P(("dp", "col"), "row"),
            P("row", "dp", None, "col", None),
            P("col", "dp", "row"),
            P("row", "dp", None, "col"),
            P("col", "dp", "row"),
            P("row", "dp", None, "col", None),
            P("col", "dp", "row"),
            P("row", "dp", None, "col"),
            P("col", "dp", "row"),
            P("row", "dp", None, "col", None),
            P("col", "dp", "row"),
            P("row", "dp", None, "col"),
            P("col", "dp", "row"),
            P(),
            P(),
            P(),
            P(),
            P(),
        ),
        check_vma=False,
    )
```

```python
import functools
import math

import jax
import jax.numpy as jnp
import numpy as np
from jax import lax
from jax.experimental import pallas as pl
from jax.experimental.pallas import tpu as pltpu
from jax.sharding import PartitionSpec as P

D = 2048
H = 16
HD = 128
FF = 8192
STEP = 3


EPSILON = 1e-06
TINY_SQUARE = 1e-30
ROPE_BASE = 500000.0
NEGATIVE = -1e30
CLIP_LEVEL = 0.5
GAIN_RATE = 0.3

LOW = jnp.bfloat16
FULL = jnp.float32


VMEM_LIMIT = 56 * 1024 * 1024


def dot(left, right):
    return jnp.dot(left, right, preferred_element_type=FULL)


def dot_back(left, right):
    return lax.dot_general(left, right, (((1,), (1,)), ((), ())), preferred_element_type=FULL)


def scaled_cost(flops, bytes_accessed, transcendentals, factor=2):
    return pl.CostEstimate(
        flops=factor * flops,
        bytes_accessed=factor * bytes_accessed,
        transcendentals=factor * transcendentals,
    )


def with_deps(kernel, count, deps):
    def body(*refs):
        return kernel(*refs[:count], *refs[count + len(deps) :])

    return body


def dep_specs(deps):
    return [pl.BlockSpec(memory_space=pl.ANY)] * len(deps)


def after(value, *others):
    if not others:
        return value

    def body(*refs):
        pass

    return pl.pallas_call(
        body,
        in_specs=dep_specs((value,) + others),
        out_specs=pl.BlockSpec(memory_space=pl.ANY),
        out_shape=jax.ShapeDtypeStruct(value.shape, value.dtype),
        input_output_aliases={0: 0},
        name="after",
    )(value, *others)


def kernel_params():
    return pltpu.CompilerParams(vmem_limit_bytes=VMEM_LIMIT)


def gate_kernel(h, gu_own, gu_other, hidden, by_gate, by_up):
    half = gu_own.shape[2]
    left = h[:, :half]
    right = h[:, half:]
    gate = dot(left, gu_own[0, 0]) + dot(right, gu_other[0, 0])
    up = dot(left, gu_own[0, 1]) + dot(right, gu_other[0, 1])
    sigmoid_gate = 1.0 / (1.0 + jnp.exp(-gate))
    silu = gate * sigmoid_gate
    hidden[...] = (silu * up).astype(LOW)
    by_gate[...] = (up * sigmoid_gate * (1.0 + gate * (1.0 - sigmoid_gate))).astype(LOW)
    by_up[...] = silu.astype(LOW)


def gate_forward(h, gu_own, gu_other, deps=()):
    tokens, width = h.shape
    n_col, _, half, mine = gu_own.shape
    weight = pl.BlockSpec((1, 2, half, mine), lambda j: (j, 0, 0, 0))
    piece = pl.BlockSpec((tokens, mine), lambda j: (0, j))
    shape = jax.ShapeDtypeStruct((tokens, n_col * mine), LOW)
    return pl.pallas_call(
        with_deps(gate_kernel, 3, deps),
        grid=(n_col,),
        in_specs=[pl.BlockSpec((tokens, width), lambda j: (0, 0)), weight, weight]
        + dep_specs(deps),
        out_specs=[piece, piece, piece],
        out_shape=[shape, shape, shape],
        cost_estimate=scaled_cost(
            flops=4 * tokens * width * n_col * mine,
            bytes_accessed=4 * gu_own.size + 2 * h.size + 6 * tokens * n_col * mine,
            transcendentals=tokens * n_col * mine,
        ),
        compiler_params=kernel_params(),
        name="gate_up",
    )(h, gu_own, gu_other, *deps)


def down_kernel(hidden, down_own, down_other, term):
    half = down_own.shape[1]
    term[:, :half] = dot(hidden[...], down_own[...]).astype(term.dtype)
    term[:, half:] = dot(hidden[...], down_other[...]).astype(term.dtype)


def down_forward(hidden, down_own, down_other, kind=LOW, deps=()):
    tokens, units = hidden.shape
    half = down_own.shape[1]
    rows = min(tokens, 256)
    weight = pl.BlockSpec((units, half), lambda i: (0, 0))
    return pl.pallas_call(
        with_deps(down_kernel, 3, deps),
        grid=(tokens // rows,),
        in_specs=[pl.BlockSpec((rows, units), lambda i: (i, 0)), weight, weight]
        + dep_specs(deps),
        out_specs=pl.BlockSpec((rows, 2 * half), lambda i: (i, 0)),
        out_shape=jax.ShapeDtypeStruct((tokens, 2 * half), kind),
        cost_estimate=scaled_cost(
            flops=4 * tokens * units * half,
            bytes_accessed=4 * down_own.size + 2 * hidden.size + 4 * tokens * half,
            transcendentals=0,
        ),
        compiler_params=kernel_params(),
        name="down",
    )(hidden, down_own, down_other, *deps)


def attended_back_kernel(grad, out_own, out_other, *results):
    half = out_own.shape[1]
    value = dot_back(grad[:, :half], out_own[...]) + dot_back(grad[:, half:], out_other[...])
    for k in range(len(results)):

        @pl.when(pl.program_id(0) == k)
        def _(k=k):
            results[k][0] = value.astype(LOW)


def attended_backward(grad, out_own, out_other, n_dp, deps):
    tokens, width = grad.shape
    rows, half = out_own.shape
    columns = rows // n_dp // 2
    weight = pl.BlockSpec((columns, half), lambda k, c: (2 * k + c, 0))

    def result_spec(i):
        return pl.BlockSpec(
            (1, tokens, columns), lambda k, c: (jnp.clip(2 * (k - i) + c, 0, 1), 0, 0)
        )

    return pl.pallas_call(
        with_deps(attended_back_kernel, 3, deps),
        grid=(n_dp, 2),
        in_specs=[pl.BlockSpec((tokens, width), lambda k, c: (0, 0)), weight, weight]
        + dep_specs(deps),
        out_specs=[result_spec(i) for i in range(n_dp)],
        out_shape=[jax.ShapeDtypeStruct((2, tokens, columns), LOW)] * n_dp,
        cost_estimate=scaled_cost(
            factor=3,
            flops=2 * grad.size * rows,
            bytes_accessed=4 * out_own.size + 2 * grad.size + 2 * tokens * rows,
            transcendentals=0,
        ),
        compiler_params=kernel_params(),
        name="attended_back",
    )(grad, out_own, out_other, *deps)


def mlp_back_kernel(
    m, by_gate, by_up, gu_own, gu_other, down_own, down_other, grad_gate, grad_up, term, total
):
    j = pl.program_id(0)
    half = gu_own.shape[2]
    grad_hidden = dot_back(m[:, :half], down_own[0]) + dot_back(m[:, half:], down_other[0])
    low_gate = (grad_hidden * by_gate[...].astype(FULL)).astype(LOW)
    low_up = (grad_hidden * by_up[...].astype(FULL)).astype(LOW)
    grad_gate[...] = low_gate
    grad_up[...] = low_up
    own = dot_back(low_gate, gu_own[0, 0]) + dot_back(low_up, gu_own[0, 1])
    other = dot_back(low_gate, gu_other[0, 0]) + dot_back(low_up, gu_other[0, 1])

    @pl.when(j == 0)
    def _():
        total[:, :half] = own
        total[:, half:] = other

    @pl.when(j > 0)
    def _():
        total[:, :half] += own
        total[:, half:] += other

    @pl.when(j == pl.num_programs(0) - 1)
    def _():
        term[...] = total[...].astype(LOW)


def mlp_backward(m, by_gate, by_up, gu_own, gu_other, down_own, down_other, deps=()):
    tokens, width = m.shape
    n_col, _, half, mine = gu_own.shape
    weight = pl.BlockSpec((1, 2, half, mine), lambda j: (j, 0, 0, 0))
    weight_down = pl.BlockSpec((1, mine, half), lambda j: (j, 0, 0))
    piece = pl.BlockSpec((tokens, mine), lambda j: (0, j))
    whole = pl.BlockSpec((tokens, width), lambda j: (0, 0))
    shape = jax.ShapeDtypeStruct((tokens, n_col * mine), LOW)
    return pl.pallas_call(
        with_deps(mlp_back_kernel, 7, deps),
        grid=(n_col,),
        in_specs=[whole, piece, piece, weight, weight, weight_down, weight_down]
        + dep_specs(deps),
        out_specs=[piece, piece, whole],
        out_shape=[shape, shape, jax.ShapeDtypeStruct((tokens, width), LOW)],
        scratch_shapes=[pltpu.VMEM((tokens, width), FULL)],
        cost_estimate=scaled_cost(
            flops=6 * tokens * width * n_col * mine,
            bytes_accessed=6 * gu_own.size + 4 * m.size + 8 * tokens * n_col * mine,
            transcendentals=0,
        ),
        compiler_params=kernel_params(),
        name="mlp_back",
    )(
        m,
        by_gate,
        by_up,
        gu_own,
        gu_other,
        down_own.reshape(n_col, mine, half),
        down_other.reshape(n_col, mine, half),
        *deps,
    )


def grad_kernel(count, groups, received, pieces, *refs):
    left = refs[:count]
    right = refs[count : count + count * groups]
    others = refs[count + count * groups : count + count * groups + received]
    results, turned = refs[-1 - pieces : -1], refs[-1]
    part = left[0].shape[0]
    step = pl.program_id(1)

    @pl.when(step == 0)
    def _():
        for k in range(count):
            turned[:, k * part : (k + 1) * part] = left[k][...].T

    for g in range(groups):
        total = None
        for k in range(count):
            term = dot(turned[:, k * part : (k + 1) * part], right[g * count + k][...])
            total = term if total is None else total + term
        if not received and pieces == 1:
            results[0][0, g] = total.astype(LOW)
        for n in range(max(received, pieces) if received or pieces > 1 else 0):

            @pl.when(step == n)
            def _(n=n):
                value = total + others[n][0, g].astype(FULL) if received else total
                results[n if pieces > 1 else 0][0, g] = value.astype(LOW)


def grad_block(
    left, left_at, rows, right, right_at, columns, steps, received, deps=(), factor=2, split=False
):
    count, groups = len(left), len(right)
    part = left[0].shape[0]
    tile = min(rows, 512)
    tiles = rows // tile
    left_spec = pl.BlockSpec((part, tile), lambda a, j: (0, left_at * tiles + a))
    right_spec = pl.BlockSpec((part, columns), lambda a, j: (0, right_at + j))
    share_spec = pl.BlockSpec((1, groups, tile, columns), lambda a, j: (0, 0, a, 0))
    result_spec = pl.BlockSpec((1, groups, tile, columns), lambda a, j: (j, 0, a, 0))
    operands = list(left) + [piece for group in right for piece in group] + list(received)
    specs = [left_spec] * count + [right_spec] * (count * groups) + [share_spec] * len(received)
    reads = len(operands)
    size = steps * groups * rows * columns
    pieces = steps if split else 1
    results = pl.pallas_call(
        with_deps(
            functools.partial(grad_kernel, count, groups, len(received), pieces), reads, deps
        ),
        grid=(tiles, steps),
        in_specs=specs + dep_specs(deps),
        out_specs=[share_spec if split else result_spec] * pieces,
        out_shape=[jax.ShapeDtypeStruct((steps // pieces, groups, rows, columns), LOW)] * pieces,
        scratch_shapes=[pltpu.VMEM((tile, count * part), LOW)],
        cost_estimate=scaled_cost(
            factor=factor,
            flops=2 * size * count * part,
            bytes_accessed=4 * size + 2 * count * part * (rows + steps * groups * columns * tiles),
            transcendentals=0,
        ),
        compiler_params=kernel_params(),
        name="weight_grad",
    )(*operands, *deps)
    return results if split else results[0]


def qkv_kernel(x, w_own, w_other, raw, squares, query_sum, key_sum):
    j = pl.program_id(1)
    half = w_own.shape[1]
    got = dot(x[0, :, :half], w_own[0]) + dot(x[0, :, half:], w_other[0])
    raw[0] = got
    query = got[:, :HD]
    key = got[:, HD : 2 * HD]

    @pl.when(j == 0)
    def _():
        query_sum[...] = query * query
        key_sum[...] = key * key

    @pl.when(j > 0)
    def _():
        query_sum[...] += query * query
        key_sum[...] += key * key

    @pl.when(j == pl.num_programs(1) - 1)
    def _():
        squares[0, 0:1] = jnp.sum(query_sum[...].T, axis=0, keepdims=True)
        squares[0, 1:2] = jnp.sum(key_sum[...].T, axis=0, keepdims=True)


def qkv_forward(x, w_own, w_other):
    shards_of, tokens, width = x.shape
    heads, half, columns = w_own.shape
    weight = pl.BlockSpec((1, half, columns), lambda k, j: (j, 0, 0))
    return pl.pallas_call(
        qkv_kernel,
        grid=(shards_of, heads),
        in_specs=[pl.BlockSpec((1, tokens, width), lambda k, j: (k, 0, 0)), weight, weight],
        out_specs=[
            pl.BlockSpec((1, tokens, columns), lambda k, j: (k, 0, j)),
            pl.BlockSpec((1, 2, tokens), lambda k, j: (k, 0, 0)),
        ],
        out_shape=[
            jax.ShapeDtypeStruct((shards_of, tokens, heads * columns), FULL),
            jax.ShapeDtypeStruct((shards_of, 2, tokens), FULL),
        ],
        scratch_shapes=[pltpu.VMEM((tokens, HD), FULL), pltpu.VMEM((tokens, HD), FULL)],
        cost_estimate=scaled_cost(
            flops=2 * x.size * heads * columns,
            bytes_accessed=2 * x.size + 4 * shards_of * w_own.size + 4 * shards_of * tokens * heads * columns,
            transcendentals=0,
        ),
        compiler_params=kernel_params(),
        name="qkv",
    )(x, w_own, w_other)


def token_scales(squares):
    return lax.rsqrt(squares[0] / D + EPSILON).T


def rope_kernel(raw, squares, cosine, sine_term, gain, packed):
    heads = gain.shape[1] // HD
    scales = token_scales(squares)
    for h in range(heads):
        core, at = h // (heads // 2), h % (heads // 2) * 3 * HD
        for n in range(2):
            value = raw[0, :, (3 * h + n) * HD : (3 * h + n + 1) * HD] * scales[:, n : n + 1]
            value = value * gain[n : n + 1, h * HD : (h + 1) * HD]
            turned = value * cosine[0] + pltpu.roll(value, HD // 2, 1) * sine_term[0]
            packed[core, 0, :, at + n * HD : at + (n + 1) * HD] = turned.astype(LOW)
        packed[core, 0, :, at + 2 * HD : at + 3 * HD] = raw[
            0, :, (3 * h + 2) * HD : (3 * h + 3) * HD
        ].astype(LOW)


def rope_specs(raw, gain):
    shards_of, tokens, columns = raw.shape
    return [
        pl.BlockSpec((1, tokens, columns), lambda k: (k, 0, 0)),
        pl.BlockSpec((1, 2, tokens), lambda k: (k, 0, 0)),
        pl.BlockSpec((1, tokens, HD), lambda k: (k, 0, 0)),
        pl.BlockSpec((1, tokens, HD), lambda k: (k, 0, 0)),
        pl.BlockSpec(gain.shape, lambda k: (0, 0)),
    ]


def rope_forward(raw, squares, cosine, sine_term, gain, deps=()):
    shards_of, tokens, columns = raw.shape
    return pl.pallas_call(
        with_deps(rope_kernel, 5, deps),
        grid=(shards_of,),
        in_specs=rope_specs(raw, gain) + dep_specs(deps),
        out_specs=pl.BlockSpec((2, 1, tokens, columns // 2), lambda k: (0, k, 0, 0)),
        out_shape=jax.ShapeDtypeStruct((2, shards_of, tokens, columns // 2), LOW),
        cost_estimate=scaled_cost(
            flops=8 * raw.size, bytes_accessed=6 * raw.size, transcendentals=0
        ),
        compiler_params=kernel_params(),
        name="rope",
    )(raw, squares, cosine, sine_term, gain, *deps)


def turned_back(grads, raw, cosine, sine_term, gain, scales, h, n):
    heads = gain.shape[1] // HD
    core, at = h // (heads // 2), (h % (heads // 2) * 3 + n) * HD
    value = grads[core, 0, :, at : at + HD].astype(FULL)
    value = value * cosine[0] - pltpu.roll(value, HD // 2, 1) * sine_term[0]
    normed = raw[0, :, (3 * h + n) * HD : (3 * h + n + 1) * HD] * scales[:, n : n + 1]
    return (value, normed, value * gain[n : n + 1, h * HD : (h + 1) * HD])


def rope_inner_kernel(raw, squares, cosine, sine_term, gain, grads, inner, gain_grad):
    heads = gain.shape[1] // HD
    scales = token_scales(squares)

    @pl.when(pl.program_id(0) == 0)
    def _():
        gain_grad[...] = jnp.zeros(gain_grad.shape, FULL)

    for n in range(2):
        total = None
        for h in range(heads):
            value, normed, scaled = turned_back(
                grads, raw, cosine, sine_term, gain, scales, h, n
            )
            term = normed * scaled
            total = term if total is None else total + term
            gain_grad[n : n + 1, h * HD : (h + 1) * HD] += jnp.sum(
                value * normed, axis=0, keepdims=True
            )
        inner[0, n : n + 1] = jnp.sum(total.T, axis=0, keepdims=True)


def rope_inner(raw, squares, cosine, sine_term, gain, grads, deps=()):
    shards_of, tokens, columns = raw.shape
    return pl.pallas_call(
        with_deps(rope_inner_kernel, 6, deps),
        grid=(shards_of,),
        in_specs=rope_specs(raw, gain)
        + [pl.BlockSpec((2, 1, tokens, columns // 2), lambda k: (0, k, 0, 0))]
        + dep_specs(deps),
        out_specs=[
            pl.BlockSpec((1, 2, tokens), lambda k: (k, 0, 0)),
            pl.BlockSpec(gain.shape, lambda k: (0, 0)),
        ],
        out_shape=[
            jax.ShapeDtypeStruct((shards_of, 2, tokens), FULL),
            jax.ShapeDtypeStruct(gain.shape, FULL),
        ],
        cost_estimate=scaled_cost(
            factor=4,
            flops=12 * raw.size, bytes_accessed=6 * raw.size, transcendentals=0
        ),
        compiler_params=kernel_params(),
        name="rope_inner",
    )(raw, squares, cosine, sine_term, gain, grads, *deps)


def rope_back_kernel(raw, squares, cosine, sine_term, gain, grads, inner, result):
    heads = gain.shape[1] // HD
    scales = token_scales(squares)
    means = (inner[0] / D).T
    for h in range(heads):
        for n in range(2):
            _, normed, scaled = turned_back(grads, raw, cosine, sine_term, gain, scales, h, n)
            value = scales[:, n : n + 1] * (scaled - normed * means[:, n : n + 1])
            result[0, :, (3 * h + n) * HD : (3 * h + n + 1) * HD] = value.astype(LOW)
        core, at = h // (heads // 2), (h % (heads // 2) * 3 + 2) * HD
        result[0, :, (3 * h + 2) * HD : (3 * h + 3) * HD] = grads[core, 0, :, at : at + HD]


def rope_backward(raw, squares, cosine, sine_term, gain, grads, inner, deps=()):
    shards_of, tokens, columns = raw.shape
    return pl.pallas_call(
        with_deps(rope_back_kernel, 7, deps),
        grid=(shards_of,),
        in_specs=rope_specs(raw, gain)
        + [
            pl.BlockSpec((2, 1, tokens, columns // 2), lambda k: (0, k, 0, 0)),
            pl.BlockSpec((1, 2, tokens), lambda k: (k, 0, 0)),
        ]
        + dep_specs(deps),
        out_specs=pl.BlockSpec((1, tokens, columns), lambda k: (k, 0, 0)),
        out_shape=jax.ShapeDtypeStruct((shards_of, tokens, columns), LOW),
        cost_estimate=scaled_cost(
            factor=4,
            flops=12 * raw.size, bytes_accessed=8 * raw.size, transcendentals=0
        ),
        compiler_params=kernel_params(),
        name="rope_back",
    )(raw, squares, cosine, sine_term, gain, grads, inner, *deps)


def qkv_back_kernel(grad, w_own, w_other, term):
    heads, half, columns = w_own.shape
    for part, weight in enumerate((w_own, w_other)):
        total = None
        for j in range(heads):
            value = dot_back(grad[:, j * columns : (j + 1) * columns], weight[j])
            total = value if total is None else total + value
        term[:, part * half : (part + 1) * half] = total.astype(LOW)


def qkv_backward(grad, w_own, w_other, deps=()):
    tokens, columns = grad.shape
    heads, half, _ = w_own.shape
    rows = min(tokens, 256)
    weight = pl.BlockSpec(w_own.shape, lambda i: (0, 0, 0))
    return pl.pallas_call(
        with_deps(qkv_back_kernel, 3, deps),
        grid=(tokens // rows,),
        in_specs=[pl.BlockSpec((rows, columns), lambda i: (i, 0)), weight, weight]
        + dep_specs(deps),
        out_specs=pl.BlockSpec((rows, 2 * half), lambda i: (i, 0)),
        out_shape=jax.ShapeDtypeStruct((tokens, 2 * half), LOW),
        cost_estimate=scaled_cost(
            factor=4,
            flops=4 * grad.size * half,
            bytes_accessed=4 * w_own.size + 2 * grad.size + 4 * tokens * half,
            transcendentals=0,
        ),
        compiler_params=kernel_params(),
        name="qkv_back",
    )(grad, w_own, w_other, *deps)


def swap(values, axis, step):
    count = lax.axis_size(axis)
    return lax.ppermute(values, axis, [(i, i ^ step) for i in range(count)])


def is_relative():
    return lax.axis_size("dp") == 4


def place_of(entry):
    if is_relative():
        return lax.axis_index("dp") ^ entry
    return entry


def gather_begin(values):
    if not is_relative():
        return ()
    return (swap(values, "dp", 1), swap(values, "dp", 2))


def gather_end(values, begun):
    if not is_relative():
        whole = lax.all_gather(values, "dp", axis=0)
        return [whole[k] for k in range(whole.shape[0])]
    first, second = begun
    half = first.shape[0] // 2
    third = jnp.concatenate([swap(second[:half], "dp", 1), swap(first[half:], "dp", 2)], axis=0)
    return [values, first, second, third]


def scatter_begin(parts):
    if not is_relative():
        return ()
    half = parts[0].shape[0] // 2
    _, first, second, third = parts
    return (
        swap(third[:half], "dp", 1),
        swap(third[half:], "dp", 2),
        swap(first[:half], "dp", 1),
        swap(second[half:], "dp", 2),
    )


def scatter_middle(parts, begun):
    if not is_relative():
        return ()
    half = parts[0].shape[0] // 2
    _, first, second, _ = parts
    low_third, high_third = begun[:2]
    return (
        swap((first[half:].astype(FULL) + high_third.astype(FULL)).astype(LOW), "dp", 1),
        swap((second[:half].astype(FULL) + low_third.astype(FULL)).astype(LOW), "dp", 2),
    )


def scatter_end(parts, begun, middle):
    if not is_relative():
        return lax.psum_scatter(jnp.stack(parts), "dp", scatter_dimension=0).astype(FULL)
    half = parts[0].shape[0] // 2
    own = parts[0].astype(FULL)
    first_low, second_high = begun[2:]
    first_high, second_low = middle
    return jnp.concatenate(
        [
            own[:half] + first_low.astype(FULL) + second_low.astype(FULL),
            own[half:] + first_high.astype(FULL) + second_high.astype(FULL),
        ],
        axis=0,
    )


def scatter_dp(parts):
    begun = scatter_begin(parts)
    return scatter_end(parts, begun, scatter_middle(parts, begun))


def trade_dp(parts):
    if not is_relative():
        traded = lax.all_to_all(jnp.stack(parts), "dp", 0, 0, tiled=True)
        return [traded[k] for k in range(traded.shape[0])]
    return [parts[0]] + [swap(parts[k], "dp", k) for k in range(1, 4)]


def exchange_dp(blocks):
    if not is_relative():
        return lax.all_to_all(blocks, "dp", 0, 0, tiled=True)
    me = lax.axis_index("dp")
    got = []
    for k in range(4):
        sent = lax.dynamic_index_in_dim(blocks, me ^ k, 0, keepdims=False)
        got.append(swap(sent, "dp", k) if k else sent)
    odd, far = me % 2 == 1, me >= 2
    first, second = jnp.where(odd, got[1], got[0]), jnp.where(odd, got[0], got[1])
    third, fourth = jnp.where(odd, got[3], got[2]), jnp.where(odd, got[2], got[3])
    return jnp.stack(
        [
            jnp.where(far, third, first),
            jnp.where(far, fourth, second),
            jnp.where(far, first, third),
            jnp.where(far, second, fourth),
        ]
    )


def exchange_row(blocks):
    other = 1 - lax.axis_index("row")
    sent = lax.dynamic_index_in_dim(blocks, other, 0, keepdims=True)
    return lax.dynamic_update_slice_in_dim(blocks, swap(sent, "row", 1), other, 0)


def sum_dp(values):
    if not is_relative():
        return lax.psum(values, "dp")
    one = swap(values, "dp", 1)
    values = values + jnp.stack([one[1], one[0], one[3], one[2]])
    two = swap(values, "dp", 2)
    return values + jnp.stack([two[2], two[3], two[0], two[1]])


def sum_all(values):
    for axis in ("row", "dp", "col"):
        step = 1
        while step < lax.axis_size(axis):
            values = values + swap(values, axis, step)
            step *= 2
    return values


def other_row(values):
    return swap(values, "row", 1)


def attend_kernel(starts, query, key, value, doc_key, doc_query, mixed, log_total):
    sequence = pl.program_id(0)
    parts, _, part, _ = query.shape
    length = parts * part
    nblock = starts.shape[1]
    block = length // nblock
    keys_in = key[...].reshape(length, HD)
    queries = query[...].reshape(length, HD)
    values_turned = value[...].reshape(length, HD).T
    scaling = HD ** (-0.5)
    for b in range(nblock):
        lo = b * block
        hi = lo + block
        scores = (
            lax.dot_general(
                keys_in[:hi],
                queries[lo:hi],
                (((1,), (1,)), ((), ())),
                preferred_element_type=FULL,
            )
            * scaling
        )
        place = lax.broadcasted_iota(jnp.int32, (hi, 1), 0)
        group = jnp.where(place >= starts[sequence, b] * block, doc_key[0, :hi, :], -1)
        scores = jnp.where(group == doc_query[0, :, lo:hi], scores, NEGATIVE)
        highest = jnp.max(scores, axis=0, keepdims=True)
        exponent = jnp.exp(scores - highest)
        total = jnp.sum(exponent, axis=0, keepdims=True)
        probability = (exponent * (1.0 / total)).astype(LOW)
        turned = jnp.dot(values_turned[:, :hi], probability, preferred_element_type=FULL)
        at = lo // part
        mixed[at, 0, lo - at * part : hi - at * part, :] = turned.T.astype(LOW)
        log_total[0, 0, :, lo:hi] = highest + jnp.log(total)


def attend_back_kernel(
    starts, query, key, value, grad_mixed, doc_key, doc_query, log_total, grads, grad_key, grad_value
):
    sequence = pl.program_id(0)
    head = pl.program_id(1)
    parts, _, part, _ = query.shape
    length = parts * part
    nblock = starts.shape[1]
    block = length // nblock
    keys_in = key[...].reshape(length, HD)
    queries = query[...].reshape(length, HD)
    values = value[...].reshape(length, HD)
    upstream = grad_mixed[...].reshape(length, HD)
    keys_turned = keys_in.T
    scaling = HD ** (-0.5)
    query_at = pl.ds(pl.multiple_of(3 * head * HD, HD), HD)
    for b in range(nblock - 1, -1, -1):
        lo = b * block
        hi = lo + block
        scores = (
            lax.dot_general(
                keys_in[:hi],
                queries[lo:hi],
                (((1,), (1,)), ((), ())),
                preferred_element_type=FULL,
            )
            * scaling
        )
        place = lax.broadcasted_iota(jnp.int32, (hi, 1), 0)
        group = jnp.where(place >= starts[sequence, b] * block, doc_key[0, :hi, :], -1)
        scores = jnp.where(group == doc_query[0, :, lo:hi], scores, NEGATIVE)
        probability = jnp.exp(scores - log_total[0, 0, :, lo:hi])
        term_value = jnp.dot(
            probability.astype(LOW), upstream[lo:hi], preferred_element_type=FULL
        )
        grad_prob = lax.dot_general(
            values[:hi], upstream[lo:hi], (((1,), (1,)), ((), ())), preferred_element_type=FULL
        )
        weighted = probability * grad_prob
        center = jnp.sum(weighted, axis=0, keepdims=True)
        grad_scores = (weighted - probability * center).astype(LOW)
        term_key = jnp.dot(grad_scores, queries[lo:hi], preferred_element_type=FULL)
        if b == nblock - 1:
            grad_value[...] = term_value
            grad_key[...] = term_key
        else:
            grad_value[:hi] += term_value
            grad_key[:hi] += term_key
        turned = jnp.dot(keys_turned[:, :hi], grad_scores, preferred_element_type=FULL) * scaling
        at = lo // part
        grads[at, 0, lo - at * part : hi - at * part, query_at] = turned.T.astype(LOW)
    key_at = pl.ds(pl.multiple_of((3 * head + 1) * HD, HD), HD)
    value_at = pl.ds(pl.multiple_of((3 * head + 2) * HD, HD), HD)
    grads[:, 0, :, key_at] = (grad_key[...] * scaling).astype(LOW).reshape(parts, part, HD)
    grads[:, 0, :, value_at] = grad_value[...].astype(LOW).reshape(parts, part, HD)


def attention_cost(packed, heads, products, factor):
    parts, nseq, part, _ = packed.shape
    pairs = nseq * heads * (parts * part) ** 2 * 5 // 8
    return scaled_cost(
        factor=factor, flops=2 * pairs * HD * products, bytes_accessed=2 * packed.size * 2, transcendentals=pairs
    )


def piece_spec(packed, stride, offset):
    parts, _, part, _ = packed.shape
    return pl.BlockSpec((parts, 1, part, HD), lambda s, h, *_: (0, s, 0, stride * h + offset))


def attend_forward(packed, starts, documents):
    parts, nseq, part, width = packed.shape
    heads = width // (3 * HD)
    length = parts * part
    return pl.pallas_call(
        attend_kernel,
        grid_spec=pltpu.PrefetchScalarGridSpec(
            num_scalar_prefetch=1,
            grid=(nseq, heads),
            in_specs=[
                piece_spec(packed, 3, 0),
                piece_spec(packed, 3, 1),
                piece_spec(packed, 3, 2),
                pl.BlockSpec((1, length, 1), lambda s, h, *_: (s, 0, 0)),
                pl.BlockSpec((1, 1, length), lambda s, h, *_: (s, 0, 0)),
            ],
            out_specs=[
                piece_spec(packed, 1, 0),
                pl.BlockSpec((1, 1, 1, length), lambda s, h, *_: (s, h, 0, 0)),
            ],
        ),
        out_shape=[
            jax.ShapeDtypeStruct((parts, nseq, part, heads * HD), LOW),
            jax.ShapeDtypeStruct((nseq, heads, 1, length), FULL),
        ],
        cost_estimate=attention_cost(packed, heads, 2, 2),
        compiler_params=pltpu.CompilerParams(vmem_limit_bytes=48 * 1024 * 1024),
        name="attend",
    )(starts, packed, packed, packed, documents[:, :, None], documents[:, None, :])


def attend_backward(packed, starts, documents, log_total, grad_mixed, deps=()):
    parts, nseq, part, width = packed.shape
    heads = width // (3 * HD)
    length = parts * part
    return pl.pallas_call(
        with_deps(attend_back_kernel, 8, deps),
        grid_spec=pltpu.PrefetchScalarGridSpec(
            num_scalar_prefetch=1,
            grid=(nseq, heads),
            in_specs=[
                piece_spec(packed, 3, 0),
                piece_spec(packed, 3, 1),
                piece_spec(packed, 3, 2),
                piece_spec(packed, 1, 0),
                pl.BlockSpec((1, length, 1), lambda s, h, *_: (s, 0, 0)),
                pl.BlockSpec((1, 1, length), lambda s, h, *_: (s, 0, 0)),
                pl.BlockSpec((1, 1, 1, length), lambda s, h, *_: (s, h, 0, 0)),
            ]
            + dep_specs(deps),
            out_specs=pl.BlockSpec((parts, 1, part, width), lambda s, h, *_: (0, s, 0, 0)),
            scratch_shapes=[pltpu.VMEM((length, HD), FULL), pltpu.VMEM((length, HD), FULL)],
        ),
        out_shape=jax.ShapeDtypeStruct(packed.shape, LOW),
        cost_estimate=attention_cost(packed, heads, 5, 5),
        compiler_params=pltpu.CompilerParams(vmem_limit_bytes=48 * 1024 * 1024),
        name="attend_back",
    )(
        starts,
        packed,
        packed,
        packed,
        grad_mixed,
        documents[:, :, None],
        documents[:, None, :],
        log_total,
        *deps,
    )


def angles(places):
    halfway = HD // 2
    frequency = ROPE_BASE ** (-jnp.arange(halfway, dtype=FULL) / halfway)
    turned = places.astype(FULL)[..., None] * jnp.concatenate([frequency, frequency])
    sign = jnp.where(jnp.arange(HD) < halfway, -1.0, 1.0)
    return (jnp.cos(turned), jnp.sin(turned) * sign)


def norm_back(upstream, normed, scaling, gain):
    scaled = upstream * gain
    inner = jnp.mean(normed * scaled, axis=1, keepdims=True)
    return (scaling * (scaled - normed * inner), jnp.sum(upstream * normed, axis=0))


def placed(shape, piece, starts):
    return lax.dynamic_update_slice(jnp.zeros(shape, FULL), piece, starts).reshape(-1)


def sequence_span(length, tokens):
    return max(1, length // tokens)


def regroup(values, span):
    if span == 1:
        return values
    n_dp, n_col = lax.axis_size("dp"), lax.axis_size("col")
    moves = []
    for i in range(n_dp):
        for j in range(n_col):
            to_i = i - i % span + j % span
            to_j = j - j % span + i % span
            moves.append((i * n_col + j, to_i * n_col + to_j))
    return lax.ppermute(values, ("dp", "col"), moves)


def heads_line_up():
    return H // lax.axis_size("col") == lax.axis_size("dp")


def fetch_qkv(low, deps):
    nb, inner, three, heads, _ = low.shape
    n_dp = lax.axis_size("dp")
    if not heads_line_up():
        whole = lax.all_gather(low, "dp", axis=1, tiled=True)
        whole = lax.all_gather(whole, "col", axis=3, tiled=True)
        mine = H // n_dp
        whole = lax.dynamic_slice_in_dim(whole, lax.axis_index("dp") * mine, mine, 3)
        return whole.transpose(3, 0, 1, 2, 4).reshape(mine, nb * HD, three * HD)
    sent = low.transpose(3, 0, 1, 2, 4).reshape(heads, nb * inner, three * HD)
    got = exchange_dp(after(sent, *deps)).reshape(n_dp, nb, inner, three * HD).transpose(1, 0, 2, 3)
    got = got.reshape(nb * HD, three * HD)
    return lax.all_gather(got, "col", axis=0)


def fetch_out(low):
    heads, inner, cols = low.shape
    if not heads_line_up():
        whole = lax.all_gather(low, "dp", axis=1, tiled=True)
        return lax.all_gather(whole, "col", axis=0, tiled=True).reshape(D, cols)
    got = exchange_dp(low).reshape(HD, cols)
    return lax.all_gather(got, "col", axis=0).reshape(heads * HD, cols)


def send_gate_up(weight):
    nb, inner, two, cols = weight.shape
    n_dp = lax.axis_size("dp")
    mine = cols // n_dp
    sent = weight.astype(LOW).reshape(nb, inner, two, n_dp, mine).transpose(3, 2, 0, 1, 4)
    return sent.reshape(n_dp, two * nb * inner, mine)


def fetch_gate_up(sent, shape):
    nb, inner, two, cols = shape
    n_dp = lax.axis_size("dp")
    mine = cols // n_dp
    got = exchange_dp(sent)
    got = got.reshape(n_dp, two, nb, inner, mine).transpose(1, 2, 0, 3, 4)
    got = got.reshape(two, nb * HD, mine)
    return (lax.all_gather(got, "col", axis=0), got)


def send_down(weight):
    blocks, inner, cols = weight.shape
    n_dp = lax.axis_size("dp")
    return weight.astype(LOW).reshape(n_dp, blocks // n_dp * inner, cols)


def fetch_down(sent, shape):
    blocks, inner, cols = shape
    n_dp, n_col = lax.axis_size("dp"), lax.axis_size("col")
    mine = blocks // n_dp
    got = exchange_dp(sent)
    got = got.reshape(n_dp, mine, inner, cols).transpose(1, 0, 2, 3).reshape(mine * HD, cols)
    return (lax.all_gather(got, "col", axis=0).reshape(n_col * mine * HD, cols), got)


def reduce_col(values):
    return lax.psum_scatter(values, "col", scatter_dimension=0)


def reduce_col_by_permutes(values):
    if lax.axis_size("col") != 4:
        return reduce_col(values)
    me = lax.axis_index("col")
    total = lax.dynamic_index_in_dim(values, me, 0, keepdims=False).astype(FULL)
    for k in range(1, 4):
        sent = lax.dynamic_index_in_dim(values, me ^ k, 0, keepdims=False)
        total = total + swap(sent, "col", k).astype(FULL)
    return total.astype(LOW)


def grad_for_other(left, rows, right, columns, steps, by_rows, deps=(), factor=2):
    places = (1, 0) if by_rows else (0, 1)
    return grad_block(left, places[0], rows, right, places[1], columns, steps, (), deps, factor, True)


def grad_for_own(left, rows, right, columns, steps, received, deps=(), factor=2):
    received = [other_row(piece) for piece in received]
    return grad_block(left, 0, rows, right, 0, columns, steps, received, deps, factor)


def in_turn(order, call, results, deps=()):
    for k in order:
        results[k] = call(k, deps)
        last = results[k]
        deps = (last[0] if isinstance(last, (list, tuple)) else last,)
    return deps


def settle_qkv(half, shape):
    nb, inner, three, heads, _ = shape
    n_dp = lax.axis_size("dp")
    mine = H // n_dp
    if not heads_line_up():
        half = half.reshape(mine, nb, HD, three, HD).transpose(1, 2, 3, 0, 4)
        whole = lax.dynamic_update_slice_in_dim(
            jnp.zeros((nb, HD, three, H, HD), LOW), half, lax.axis_index("dp") * mine, 3
        )
        whole = lax.psum_scatter(whole, "dp", scatter_dimension=1, tiled=True)
        return lax.psum_scatter(whole, "col", scatter_dimension=3, tiled=True).astype(FULL)
    summed = half
    sent = summed.reshape(nb, n_dp, inner, three * HD).transpose(1, 0, 2, 3)
    got = exchange_dp(sent.reshape(n_dp, nb * inner, three * HD))
    return got.reshape(n_dp, nb, inner, three, HD).transpose(1, 2, 3, 0, 4).astype(FULL)


def settle_out(half, shape):
    heads, inner, cols = shape
    if not heads_line_up():
        whole = half.reshape(H, HD, cols)
        whole = lax.psum_scatter(whole, "dp", scatter_dimension=1, tiled=True)
        return lax.psum_scatter(whole, "col", scatter_dimension=0, tiled=True).astype(FULL)
    return exchange_dp(half.reshape(lax.axis_size("dp"), inner, cols)).astype(FULL)


def send_gate_up_grad(summed, shape):
    nb, inner, two, cols = shape
    n_dp = lax.axis_size("dp")
    mine = cols // n_dp
    sent = summed.reshape(two, nb, n_dp, inner, mine).transpose(2, 0, 1, 3, 4)
    return sent.reshape(n_dp, two * nb * inner, mine)


def gate_up_grad(got, shape):
    nb, inner, two, cols = shape
    n_dp = lax.axis_size("dp")
    got = got.reshape(n_dp, two, nb, inner, cols // n_dp).transpose(2, 3, 1, 0, 4)
    return got.reshape(shape).astype(FULL)


def send_down_grad(summed, shape):
    blocks, inner, cols = shape
    n_dp = lax.axis_size("dp")
    mine = blocks // n_dp
    sent = summed.reshape(mine, n_dp, inner, cols).transpose(1, 0, 2, 3)
    return sent.reshape(n_dp, mine * inner, cols)


DECAY = 1.0 - STEP ** (-0.8)


def square_sums(matrices):
    rows, cols = [], []
    for grad, _, row_shape, col_shape, row_at, col_at, _ in matrices:
        squares = grad * grad
        rows.append(placed(row_shape, jnp.sum(squares, axis=tuple(range(2, grad.ndim))), row_at))
        cols.append(placed(col_shape, jnp.sum(squares, axis=(0, 1)), col_at))
    return (jnp.concatenate(rows), jnp.concatenate(cols))


def spans(shapes):
    at, result = 0, []
    for shape in shapes:
        result.append((at, at + math.prod(shape)))
        at = result[-1][1]
    return result


def new_states(matrices, row_sums, col_sums, old_row, old_col):
    row_spans = spans([matrix[2] for matrix in matrices])
    col_spans = spans([matrix[3] for matrix in matrices])
    row_parts = np.concatenate(
        [np.full(b - a, 1.0 / (d - c), np.float32) for (a, b), (c, d) in zip(row_spans, col_spans)]
    )
    col_parts = np.concatenate(
        [np.full(d - c, 1.0 / (b - a), np.float32) for (a, b), (c, d) in zip(row_spans, col_spans)]
    )
    new_row = DECAY * old_row + (1.0 - DECAY) * (row_sums * row_parts + TINY_SQUARE)
    new_col = DECAY * old_col + (1.0 - DECAY) * (col_sums * col_parts + TINY_SQUARE)
    return (new_row, new_col)


def scaled_updates(matrices, new_row, new_col):
    row_spans = spans([matrix[2] for matrix in matrices])
    col_spans = spans([matrix[3] for matrix in matrices])
    updates, sizes = [], []
    for n, (grad, _, row_shape, col_shape, row_at, col_at, _) in enumerate(matrices):
        row_all = new_row[slice(*row_spans[n])]
        col_all = new_col[slice(*col_spans[n])]
        row_here = lax.dynamic_slice(row_all.reshape(row_shape), row_at, grad.shape[:2])
        col_here = lax.dynamic_slice(col_all.reshape(col_shape), col_at, grad.shape[2:])
        row_here = row_here.reshape(grad.shape[:2] + (1,) * (grad.ndim - 2))
        update = grad * lax.rsqrt(row_here * col_here[None, None] / jnp.mean(row_all))
        updates.append(update)
        sizes.append(jnp.sum(update * update))
    lane = lax.broadcasted_iota(jnp.int32, (8, 128), 1)
    packed = jnp.zeros((8, 128), FULL)
    for n, size in enumerate(sizes):
        packed = jnp.where(lane == n, size, packed)
    return (updates, packed)


def renew(matrices, updates, sizes):
    renewed = []
    for n, matrix in enumerate(matrices):
        count = math.prod(matrix[2]) * math.prod(matrix[3])
        clip = jnp.maximum(1.0, jnp.sqrt(sizes[0, n] / count) / CLIP_LEVEL)
        renewed.append(matrix[1] - matrix[-1] * updates[n] / clip)
    return renewed


def shards(
    inputs,
    cotangent,
    w_qkv,
    w_out,
    w_gate_up,
    w_down,
    gains,
    gain_state,
    row_state,
    col_state,
    positions,
    block_map,
):
    row_pos = lax.axis_index("row")
    col_pos = lax.axis_index("col")
    data_pos = lax.axis_index("dp")
    n_dp, n_col = lax.axis_size("dp"), lax.axis_size("col")
    length = positions.shape[1]
    chip_tokens = inputs.shape[0]
    tokens = chip_tokens // 2
    width = inputs.shape[1]
    span = sequence_span(length, chip_tokens)
    heads_here = H // n_dp
    local = heads_here * HD

    def enter(values):
        values = regroup(values, span)
        kept = lax.dynamic_slice_in_dim(values, row_pos * tokens, tokens, 0)
        sent = lax.dynamic_slice_in_dim(values, (1 - row_pos) * tokens, tokens, 0)
        return jnp.concatenate([kept, swap(sent, "row", 1)], axis=1)

    def leave(values):
        got = swap(values[:, width:], "row", 1)
        result = jnp.zeros((chip_tokens, width), values.dtype)
        result = lax.dynamic_update_slice_in_dim(result, values[:, :width], row_pos * tokens, 0)
        result = lax.dynamic_update_slice_in_dim(result, got, (1 - row_pos) * tokens, 0)
        return regroup(result, span)

    def own_first(vector):
        parts = vector.reshape(2, width)
        return jnp.concatenate(
            [
                lax.dynamic_index_in_dim(parts, row_pos, 0, keepdims=False),
                lax.dynamic_index_in_dim(parts, 1 - row_pos, 0, keepdims=False),
            ]
        )

    x_own = enter(inputs)
    qkv_own = fetch_qkv(w_qkv.astype(LOW), (x_own,))
    out_rows = fetch_out(w_out.astype(LOW))
    gu_sent = send_gate_up(w_gate_up)
    down_sent = send_down(w_down)
    begun = gather_begin(x_own)
    begun = tuple(after(share, gu_sent, down_sent) for share in begun)
    every_place = after(jnp.concatenate([positions, block_map], axis=1), *begun)
    if is_relative() and span == 1:
        twin = other_row(every_place)
        first = row_pos == 0
        every_place = jnp.concatenate(
            [jnp.where(first, every_place, twin), jnp.where(first, twin, every_place)]
        )
        every_place = lax.dynamic_slice_in_dim(every_place, col_pos, 1, 0)
        here = jnp.concatenate(trade_dp([every_place] * n_dp))
        sequences = n_dp
    else:
        every_place = lax.all_gather(every_place, ("dp", "row"), axis=0, tiled=True)
        sequences = n_dp // span
        numbers = []
        for k in range(sequences):
            first = place_of(k) if span == 1 else k * span + col_pos % span
            numbers.append(first * (n_col // span) + col_pos // span)
        here = jnp.concatenate(
            [lax.dynamic_slice_in_dim(every_place, number, 1, 0) for number in numbers]
        )
    places = here[:, :length]
    starts = here[:, length:]
    documents = jnp.cumsum((places == 0).astype(jnp.int32), axis=1)
    x_parts = gather_end(x_own, begun)
    qkv_own = after(qkv_own, *begun)
    qkv_other = other_row(qkv_own)
    x_all = jnp.stack(x_parts)
    gu_own, gu_got = fetch_gate_up(after(gu_sent, x_all), w_gate_up.shape)
    down_own, down_got = fetch_down(after(down_sent, x_all), w_down.shape)
    grad_result = enter(cotangent).astype(FULL)

    token_places = lax.dynamic_index_in_dim(
        places.reshape(n_dp, 2, tokens), row_pos, 1, keepdims=False
    )
    cosine, sine_term = angles(token_places)

    if heads_line_up():
        gain_here = lax.dynamic_index_in_dim(
            gains[:2].reshape(2, n_col, n_dp, HD), data_pos, 2, keepdims=False
        ).reshape(2, local)
    else:
        gain_here = lax.dynamic_slice_in_dim(gains[:2], data_pos * local, local, 1)

    raw, squares = qkv_forward(x_all, qkv_own, qkv_other)
    squares = sum_dp(squares)
    turn = (raw, squares, cosine, sine_term, gain_here)
    out_begun = ()
    if heads_line_up():
        out_begun = gather_begin(after(out_rows, gu_got, down_got))
    packed = rope_forward(*turn, (gu_got, down_got))

    def by_sequence(values):
        if span == 1:
            return values
        last = values.shape[-1]
        values = values.reshape(2, sequences, span, tokens, last).transpose(1, 2, 0, 3, 4)
        return values.reshape(1, sequences, length, last)

    def by_shard(values):
        if span == 1:
            return values
        last = values.shape[-1]
        values = values.reshape(sequences, span, 2, tokens, last).transpose(2, 0, 1, 3, 4)
        return values.reshape(2, n_dp, tokens, last)

    packed = by_sequence(exchange_row(packed))
    out_own = out_rows
    mixed, log_total = attend_forward(packed, starts, documents)
    if heads_line_up():
        out_begun = tuple(after(share, log_total) for share in out_begun)
        out_own = jnp.concatenate(gather_end(out_rows, out_begun), axis=0)
    out_other = other_row(out_own)
    mixed = exchange_row(by_shard(mixed))
    mixed = trade_dp([mixed[:, k] for k in range(n_dp)])
    attended = jnp.concatenate([piece[core] for piece in mixed for core in range(2)], axis=1)

    attn = down_forward(attended, out_own, out_other, FULL, (gu_own,))
    gain_attn = own_first(gains[2])[None, :]
    gain_mlp = own_first(gains[3])[None, :]
    attn_scale = lax.rsqrt(jnp.mean(attn * attn, axis=1, keepdims=True) + EPSILON)
    attn_hat = attn * attn_scale
    hidden_in = x_own.astype(FULL) + attn_hat * gain_attn
    h_own = hidden_in.astype(LOW)
    begun = gather_begin(h_own)
    gu_own = after(gu_own, h_own)
    gu_other = other_row(gu_own)
    by_arrival = list(range(n_dp))
    by_distance = [3, 1, 2, 0] if is_relative() else by_arrival
    gated = [None] * n_dp
    last, rest = (), by_arrival
    if is_relative():
        gated[0] = gate_forward(h_own, gu_own, gu_other)
        last, rest = (gated[0][0],), by_arrival[1:]
        begun = tuple(after(share, *last) for share in begun)
    h_parts = gather_end(h_own, begun)

    def gate_part(k, deps):
        deps = deps + ((h_parts[3], down_own) if k == 2 else ())
        return gate_forward(h_parts[k], gu_own, gu_other, deps)

    in_turn(rest, gate_part, gated, last)
    hiddens = [entry[0] for entry in gated]
    down_own = after(down_own, hiddens[2])
    down_other = other_row(down_own)
    terms = [None] * n_dp
    in_turn(
        by_distance,
        lambda k, deps: down_forward(hiddens[k], down_own, down_other, LOW, deps),
        terms,
    )
    mlp = scatter_dp(terms)
    mlp_scale = lax.rsqrt(jnp.mean(mlp * mlp, axis=1, keepdims=True) + EPSILON)
    mlp_hat = mlp * mlp_scale
    result = leave(hidden_in + mlp_hat * gain_mlp)

    grad_mlp, gain_mlp_grad = norm_back(grad_result, mlp_hat, mlp_scale, gain_mlp)
    m_own = grad_mlp.astype(LOW)
    weights = (gu_own, gu_other, down_own, down_other)
    backs = [None] * n_dp
    begun = gather_begin(m_own)
    if is_relative():
        m_parts = [m_own]
        last = in_turn(
            [0], lambda k, deps: mlp_backward(m_own, *gated[k][1:], *weights, deps), backs
        )
        begun = tuple(after(share, *last) for share in begun)
        rest = [1, 3, 2]
    else:
        last, rest = (), by_arrival
    m_parts = gather_end(m_own, begun)
    last = in_turn(
        rest,
        lambda k, deps: mlp_backward(m_parts[k], *gated[k][1:], *weights, deps),
        backs,
        last,
    )
    units = hiddens[0].shape[1]
    down_block = (hiddens, units, [m_parts], width, 1)
    gu_block = (
        h_parts,
        width,
        [[entry[0] for entry in backs], [entry[1] for entry in backs]],
        gu_own.shape[3],
        n_col,
    )
    terms = [entry[2] for entry in backs]
    begun = scatter_begin(terms)
    gu_rest = grad_for_other(*gu_block, True, last + begun[:3])
    down_rest = grad_for_other(*down_block, False, (gu_rest[0],) + begun[3:])
    middle = scatter_middle(terms, begun)
    gu_half = grad_for_own(*gu_block, gu_rest, (down_rest[0],) + middle)
    gu_sum = reduce_col(gu_half)
    terms[0] = after(terms[0], gu_half)
    grad_hidden_in = grad_result + scatter_end(terms, begun, middle)

    grad_attn, gain_attn_grad = norm_back(grad_hidden_in, attn_hat, attn_scale, gain_attn)
    grad_attn_low = grad_attn.astype(LOW)
    sent = attended_backward(grad_attn_low, out_own, out_other, n_dp, (gu_half,))
    out_block = ([attended], D, [[grad_attn_low]], width, 1)
    out_rest = grad_for_other(*out_block, False, (sent[0],), 4)
    grad_mixed = by_sequence(exchange_row(jnp.stack(trade_dp(sent), axis=1)))
    grads = attend_backward(packed, starts, documents, log_total, grad_mixed, (out_rest[0],))
    out_half = grad_for_own(*out_block, out_rest, (grads,), 4)
    grads = exchange_row(by_shard(grads))
    inner, gain_pair = rope_inner(*turn, grads)
    gu_got = exchange_dp(send_gate_up_grad(gu_sum, w_gate_up.shape))
    out_begun = ()
    if heads_line_up():
        out_parts = out_half.reshape(n_dp, local, width)
        out_parts = [out_parts[k] for k in range(n_dp)]
        out_begun = scatter_begin(out_parts)
    qkv_low = rope_backward(*turn, grads, sum_dp(inner))
    down_half = grad_for_own(*down_block, down_rest, (gu_sum, qkv_low) + out_begun)
    down_sum = reduce_col(down_half.reshape(n_col, -1, width))
    qkv_block = (
        [x_all.reshape(n_dp * tokens, D)],
        width,
        [[qkv_low.reshape(n_dp * tokens, 3 * local)]],
        3 * HD,
        heads_here,
    )
    out_middle = ()
    if heads_line_up():
        out_middle = scatter_middle(out_parts, out_begun)
    qkv_rest = grad_for_other(*qkv_block, True, (down_half,), 4)
    if heads_line_up():
        out_half = scatter_end(out_parts, out_begun, out_middle).astype(LOW)
        out_half = reduce_col_by_permutes(after(out_half.reshape(n_col, HD, width), qkv_rest[0]))
    down_got = exchange_dp(send_down_grad(down_sum, w_down.shape))
    grad_gu = gate_up_grad(gu_got, w_gate_up.shape)
    grad_down = down_got.reshape(w_down.shape).astype(FULL)
    grad_out = settle_out(out_half, w_out.shape)
    terms = [None] * n_dp
    back_order = [3, 1, 0, 2] if is_relative() else by_arrival

    def back_term(k, deps):
        deps = deps + ((grad_gu,) if k == back_order[-1] else ())
        return qkv_backward(qkv_low[k], qkv_own, qkv_other, deps)

    last = in_turn(back_order[:1], back_term, terms, (qkv_rest[0],))
    qkv_half = grad_for_own(*qkv_block, qkv_rest, last + out_middle, 4)
    in_turn(back_order[1:], back_term, terms, (qkv_half,))
    begun = scatter_begin(terms)
    middle = scatter_middle(terms, begun)
    if heads_line_up():
        qkv_sum = reduce_col(after(qkv_half[:, 0], down_sum))
    else:
        qkv_sum = qkv_half
    grad_qkv = settle_qkv(qkv_sum, w_qkv.shape)
    grad_inputs = leave(grad_hidden_in + scatter_end(terms, begun, middle))

    if heads_line_up():
        gain_pair = placed(
            (2, n_col, n_dp, HD), gain_pair.reshape(2, n_col, 1, HD), (0, 0, data_pos, 0)
        )
    else:
        gain_pair = placed((2, D), gain_pair, (0, data_pos * local))
    gain_partial = jnp.concatenate(
        [
            gain_pair.reshape(2, D),
            own_first(gain_attn_grad)[None, :],
            own_first(gain_mlp_grad)[None, :],
        ]
    )

    nb_rows, inner_rows, _, heads_col, _ = grad_qkv.shape
    ff_blocks = grad_down.shape[0]
    ff_cols = grad_gu.shape[3]
    row_at = (row_pos * nb_rows, data_pos * inner_rows)
    out_at = (col_pos * heads_col, data_pos * inner_rows)
    down_at = (col_pos * ff_blocks, data_pos * inner_rows)
    own_half = (row_pos * width,)
    rate, down_rate = 3.0 * D ** (-0.5), 3.0 * FF ** (-0.5)
    matrices = [
        (grad_qkv, w_qkv, (D // HD, HD), (3, H, HD), row_at, (0, col_pos * heads_col, 0), rate),
        (grad_out, w_out, (H, HD), (D,), out_at, own_half, rate),
        (grad_gu, w_gate_up, (D // HD, HD), (2, FF), row_at, (0, col_pos * ff_cols), rate),
        (grad_down, w_down, (FF // HD, HD), (D,), down_at, own_half, down_rate),
    ]
    row_part, col_part = square_sums(matrices)
    sums = sum_all(jnp.concatenate([row_part, col_part, gain_partial.reshape(-1)]))
    row_end, col_end = row_part.size, row_part.size + col_part.size
    new_row, new_col = new_states(
        matrices, sums[:row_end], sums[row_end:col_end], row_state, col_state
    )
    gain_grad = sums[col_end:].reshape(gain_partial.shape)
    updates, sizes = scaled_updates(matrices, new_row, new_col)
    new_qkv, new_out, new_gu, new_down = renew(matrices, updates, sum_all(sizes))
    gain_new_state = DECAY * gain_state + (1.0 - DECAY) * (gain_grad * gain_grad + TINY_SQUARE)
    gain_update = gain_grad * lax.rsqrt(gain_new_state)
    gain_update = gain_update / jnp.maximum(
        1.0, jnp.sqrt(jnp.mean(gain_update * gain_update, axis=1, keepdims=True)) / CLIP_LEVEL
    )
    new_gains = gains - GAIN_RATE * gain_update
    return (
        result,
        grad_inputs,
        grad_qkv,
        grad_out,
        grad_gu,
        grad_down,
        new_qkv,
        new_out,
        new_gu,
        new_down,
        new_qkv.astype(LOW),
        new_out.astype(LOW),
        new_gu.astype(LOW),
        new_down.astype(LOW),
        new_row,
        new_col,
        gain_grad,
        gain_new_state,
        new_gains,
    )


def solution(mesh):
    return jax.shard_map(
        shards,
        mesh=mesh,
        in_specs=(
            P(("dp", "col"), "row"),
            P(("dp", "col"), "row"),
            P("row", "dp", None, "col", None),
            P("col", "dp", "row"),
            P("row", "dp", None, "col"),
            P("col", "dp", "row"),
            P(),
            P(),
            P(),
            P(),
            P(("dp", "row"), None),
            P(("dp", "row"), None),
        ),
        out_specs=(
            P(("dp", "col"), "row"),
            P(("dp", "col"), "row"),
            P("row", "dp", None, "col", None),
            P("col", "dp", "row"),
            P("row", "dp", None, "col"),
            P("col", "dp", "row"),
            P("row", "dp", None, "col", None),
            P("col", "dp", "row"),
            P("row", "dp", None, "col"),
            P("col", "dp", "row"),
            P("row", "dp", None, "col", None),
            P("col", "dp", "row"),
            P("row", "dp", None, "col"),
            P("col", "dp", "row"),
            P(),
            P(),
            P(),
            P(),
            P(),
        ),
        check_vma=False,
    )
```
